256 devices in a mesh: section: 2 (over core), expert: 16 (over x_lo, z), dp: 8 (over x_hi, y).
Axes of the slice: x: 4 (x_hi: 2, x_lo: 2; x = x_hi * 2 + x_lo), y: 4, z: 8, core: 2. Of those that a mesh axis runs over, the one named last changes fastest.
Arguments:
- section_input: bfloat16 [2, 16384, 4096], P('section', ('expert', 'dp')), may hold values from -6 to 6
- routing: int32 [2, 16384, 8], P('section', ('expert', 'dp')), may hold values from 0 to 127, as said below
- out_grad: bfloat16 [2, 16384, 4096], P('section', ('expert', 'dp')), may hold values from -6 to 6
- norm_gain: float32 [2, 4096], P('section'), may hold values from 0.1 to 1.9
- router: bfloat16 [2, 4096, 128], P('section'), may hold values from -0.09375 to 0.09375
- w_in: bfloat16 [2, 16, 4096, 1536], P('section', 'expert', 'dp'), may hold values from -0.09375 to 0.09375
- w_out: bfloat16 [2, 16, 768, 4096], P('section', 'expert', None, 'dp'), may hold values from -0.21875 to 0.21875
Outputs:
- handoff: bfloat16 [2, 16384, 4096], P('section', ('expert', 'dp'))
- handback: bfloat16 [2, 16384, 4096], P('section', ('expert', 'dp'))
- grad_in: bfloat16 [2, 16, 4096, 1536], P('section', 'expert', 'dp')
- grad_out: bfloat16 [2, 16, 768, 4096], P('section', 'expert', None, 'dp')
- grad_router: bfloat16 [2, 4096, 128], P('section')
- grad_gain: float32 [2, 4096], P('section')
The draws below stay inside these ranges and needn't reach their ends.
Inputs may be any that keep to these rules, and one draw needn't show every extreme that they name: `routing`: each row names 8 different experts. In each aligned block of 128 rows (the rows of one device) no expert is named more than 10 times.
All inputs are finite; a program needn't handle non-finite values.
Results may differ from the reference program's by a relative error of at most 0.027.
Values may be sent and summed in bfloat16 or wider, within the bound.
No kernel may reach another device: no remote copies, remote signals or barrier semaphores. Data moves between devices by JAX's collectives and lax.ppermute only.
A program may use at most 128 MiB of HBM per device.

```python
import jax
import jax.numpy as jnp
from jax import lax

D = 4096
H = 768
EXPERTS = 128
TOPK = 8
TOK_DEV = 128
SECTIONS = 2
WIN = 16
TOKENS = 16384
MOST = 10
N_DP = 8


def draw_section_input(key, part):
    key = jax.random.fold_in(key, 5)
    key_base, key_rows, key_cols = jax.random.split(key, 3)
    col_scale = jnp.exp(jax.random.uniform(key_cols, (SECTIONS, 1, D), jnp.float32, jnp.log(0.3), jnp.log(3.0)))
    base = jax.random.truncated_normal(key_base, -4.0, 4.0, (SECTIONS, TOKENS, D), jnp.float32)
    row_scale = jnp.exp(jax.random.uniform(key_rows, (SECTIONS, TOKENS, 1), jnp.float32, jnp.log(0.05), jnp.log(0.5)))
    return (base * row_scale * col_scale).astype(jnp.bfloat16)


def draw_routing(key, part):
    key = jax.random.fold_in(key, 11)
    block_count = TOKENS // TOK_DEV
    extra = EXPERTS * 5 // 8
    cycle_length = EXPERTS - 1 + extra

    def one_section(section_key):
        hot_key, block_key = jax.random.split(section_key)
        hot_expert = jax.random.randint(hot_key, (), 0, WIN).astype(jnp.int32)

        def one_block(this_key):
            perm_key, order_key, roll_key = jax.random.split(this_key, 3)
            others = jax.random.permutation(perm_key, EXPERTS - 1).astype(jnp.int32)
            others = others + (others >= hot_expert).astype(jnp.int32)
            cycle = jnp.concatenate([others, others[:extra]])
            row_idx = jnp.arange(TOK_DEV, dtype=jnp.int32)[:, None]
            col_idx = jnp.arange(TOPK, dtype=jnp.int32)[None, :]
            place_hot = row_idx * (TOPK - 1) + col_idx - 1
            place_rest = MOST * (TOPK - 1) + (row_idx - MOST) * TOPK + col_idx
            place = jnp.where(row_idx < MOST, place_hot, place_rest)
            picked = cycle[jnp.mod(place, cycle_length)]
            chosen = jnp.where((row_idx < MOST) & (col_idx == 0), hot_expert, picked)
            row_order = jax.random.permutation(order_key, TOK_DEV)
            chosen = chosen[row_order]
            shifts = jax.random.randint(roll_key, (TOK_DEV, 1), 0, TOPK).astype(jnp.int32)
            rolled = jnp.mod(col_idx + shifts, TOPK)
            return jnp.take_along_axis(chosen, rolled, axis=1)
        block_keys = jax.random.split(block_key, block_count)
        return jax.vmap(one_block)(block_keys).reshape(TOKENS, TOPK)
    section_keys = jax.random.split(key, SECTIONS)
    return jax.vmap(one_section)(section_keys).astype(jnp.int32)


def level_of(stream_key, extent, pieces, low, high):
    factor_of = 1.0
    for axis_at, shards_of in pieces:
        draws = jax.random.uniform(jax.random.fold_in(jax.random.fold_in(stream_key, 6), axis_at), (shards_of,), jnp.float32, low / len(pieces), high / len(pieces))
        factor_of = factor_of * jnp.repeat(jnp.exp(draws), extent[axis_at] // shards_of).reshape((-1,) + (1,) * (len(extent) - 1 - axis_at))
    return factor_of


def normal_values(rng, extent, spread, reach, shards=(), kind=jnp.bfloat16):
    factor_of = level_of(rng, extent, shards, -0.22, 0.18) if shards else 1.0
    drawn = jax.random.normal(rng, extent, jnp.float32) * spread * factor_of
    return jnp.minimum(jnp.maximum(drawn, -reach), reach).astype(kind)


def setup_inputs(seed: int = 0) -> dict:
    arg_keys = jax.random.split(jax.random.key(seed), 8)
    return {
        "section_input": draw_section_input(jax.random.fold_in(arg_keys[7], 71), 0),
        "routing": draw_routing(jax.random.fold_in(arg_keys[7], 71), 0),
        "out_grad": normal_values(arg_keys[2], (SECTIONS, TOKENS, D), 1.0, 6.0, ((0, 2), (1, 128))),
        "norm_gain": jnp.clip(1.0 + 0.18 * jax.random.normal(arg_keys[3], (SECTIONS, D), jnp.float32), 0.1, 1.9),
        "router": normal_values(arg_keys[4], (SECTIONS, D, EXPERTS), D ** -0.5, 0.09375, ((0, 2),)),
        "w_in": normal_values(arg_keys[5], (SECTIONS, WIN, D, 2 * H), D ** -0.5, 0.09375, ((0, 2), (1, 16), (2, 8))),
        "w_out": normal_values(arg_keys[6], (SECTIONS, WIN, H, D), H ** -0.5, 0.21875, ((0, 2), (1, 16), (3, 8))),
    }


def silu_parts(values):
    sigmoid = jax.nn.sigmoid(values)
    return (values * sigmoid, sigmoid * (1.0 + values * (1.0 - sigmoid)))

def block_sum(left, right):
    row_count = left.shape[0]
    part_width = left.shape[1] // N_DP
    left_blocks = left.reshape(row_count, N_DP, part_width).astype(jnp.float32)
    right_blocks = right.reshape(N_DP, part_width, right.shape[1]).astype(jnp.float32)
    partial_terms = jnp.einsum('rjd,jdh->jrh', left_blocks, right_blocks, precision=lax.Precision.HIGHEST)
    rounded = lax.optimization_barrier(partial_terms.astype(jnp.bfloat16))
    return lax.optimization_barrier(jnp.sum(rounded.astype(jnp.float32), axis=0))

def section_layer(block_input, route_ids, grad_top, gain_vector, router_table, weight_first, weight_second):
    x_wide = block_input.astype(jnp.float32)
    inv_rms = lax.rsqrt(lax.optimization_barrier(jnp.mean(x_wide * x_wide, axis=1, keepdims=True)) + 1e-06)
    normed = (x_wide * inv_rms * gain_vector[None, :]).astype(jnp.bfloat16)
    logits = jnp.dot(normed, router_table, preferred_element_type=jnp.float32)
    chosen = jnp.take_along_axis(logits, route_ids, axis=1)
    exp_terms = jnp.exp(chosen)
    gate_weights = exp_terms / lax.optimization_barrier(jnp.sum(exp_terms, axis=1, keepdims=True))
    block_count = TOKENS // TOK_DEV
    pair_count = TOK_DEV * TOPK
    block_ids = route_ids.reshape(block_count, pair_count)
    window = jnp.arange(WIN, dtype=jnp.int32)
    matches = (block_ids[:, :, None] == window[None, None, :]).astype(jnp.int32)
    slot_rank = jnp.cumsum(matches, axis=1) - 1
    slot_ids = jnp.arange(MOST, dtype=jnp.int32)
    slot_hits = matches[..., None] * (slot_rank[..., None] == slot_ids).astype(jnp.int32)
    pair_local = jnp.arange(pair_count, dtype=jnp.int32)
    pair_of = lax.optimization_barrier(jnp.sum(slot_hits * pair_local[None, :, None, None], axis=1))
    valid = lax.optimization_barrier(jnp.sum(slot_hits, axis=1))
    pair_global = pair_of + (jnp.arange(block_count, dtype=jnp.int32) * pair_count)[:, None, None]
    token_of = pair_global // TOPK
    slot_gate = gate_weights.reshape(-1)[pair_global] * valid.astype(jnp.float32)
    row_total = block_count * MOST
    token_rows = token_of.transpose(1, 0, 2).reshape(WIN, row_total)
    gate_rows = slot_gate.transpose(1, 0, 2).reshape(WIN, row_total)
    valid_rows = valid.transpose(1, 0, 2).reshape(WIN, row_total)
    pair_rows = pair_global.transpose(1, 0, 2).reshape(WIN, row_total)

    def expert_work(items):
        tokens_here, gates_here, valid_here, first_here, second_here = items
        expert_rows = normed[tokens_here] * valid_here[:, None].astype(jnp.bfloat16)
        pre_act = block_sum(expert_rows, first_here)
        activated, act_slope = silu_parts(pre_act[:, :H])
        up_part = pre_act[:, H:]
        hidden = (activated * up_part).astype(jnp.bfloat16)
        expert_out = jnp.dot(hidden, second_here, preferred_element_type=jnp.float32).astype(jnp.bfloat16)
        grad_rows = grad_top[tokens_here].astype(jnp.float32)
        route_grad = (gates_here[:, None] * grad_rows).astype(jnp.bfloat16)
        gate_grad = lax.optimization_barrier(jnp.sum(grad_rows * expert_out.astype(jnp.float32), axis=1)) * valid_here.astype(jnp.float32)
        hidden_grad = block_sum(route_grad, second_here.T)
        pre_grad = jnp.concatenate([hidden_grad * up_part * act_slope, hidden_grad * activated], axis=1).astype(jnp.bfloat16)
        first_grad = lax.dot_general(expert_rows, pre_grad, (((0,), (0,)), ((), ())), preferred_element_type=jnp.float32)
        second_grad = lax.dot_general(hidden, route_grad, (((0,), (0,)), ((), ())), preferred_element_type=jnp.float32)
        expert_back = lax.dot_general(pre_grad, first_here, (((1,), (1,)), ((), ())), preferred_element_type=jnp.float32).astype(jnp.bfloat16)
        return (expert_out, gate_grad, expert_back, first_grad.astype(jnp.bfloat16), second_grad.astype(jnp.bfloat16))
    outs_all, gate_all, back_all, first_grads, second_grads = lax.map(expert_work, (token_rows, gate_rows, valid_rows, weight_first, weight_second))
    flat_tokens = token_rows.reshape(-1)
    mixed = jnp.zeros((TOKENS, D), jnp.float32).at[flat_tokens].add(gate_rows.reshape(-1)[:, None] * outs_all.reshape(-1, D).astype(jnp.float32))
    layer_out = (x_wide + mixed).astype(jnp.bfloat16)
    gate_grad = jnp.zeros((TOKENS * TOPK,), jnp.float32).at[pair_rows.reshape(-1)].add(gate_all.reshape(-1)).reshape(TOKENS, TOPK)
    inner_sum = lax.optimization_barrier(jnp.sum(gate_weights * gate_grad, axis=1, keepdims=True))
    chosen_grad = gate_weights * (gate_grad - inner_sum)
    columns = jnp.arange(EXPERTS, dtype=jnp.int32)
    logit_grad = lax.optimization_barrier(jnp.sum(chosen_grad[:, :, None] * (route_ids[:, :, None] == columns).astype(jnp.float32), axis=1))
    normed_back = jnp.zeros((TOKENS, D), jnp.float32).at[flat_tokens].add(back_all.reshape(-1, D).astype(jnp.float32))
    normed_grad = normed_back + jnp.dot(logit_grad, router_table.astype(jnp.float32).T, precision=lax.Precision.HIGHEST)
    router_grad = jnp.dot(normed.astype(jnp.float32).T, logit_grad, precision=lax.Precision.HIGHEST).astype(jnp.bfloat16)
    gain_grad = lax.optimization_barrier(jnp.sum(normed_grad * x_wide * inv_rms, axis=0))
    weighted = gain_vector[None, :] * normed_grad
    in_grad = (grad_top.astype(jnp.float32) + inv_rms * weighted - x_wide * inv_rms * inv_rms * inv_rms * lax.optimization_barrier(jnp.mean(x_wide * weighted, axis=1, keepdims=True))).astype(jnp.bfloat16)
    return (layer_out, in_grad, first_grads, second_grads, router_grad, gain_grad)

def reference(section_input, routing, out_grad, norm_gain, router, w_in, w_out):
    results = [section_layer(section_input[index], routing[index], out_grad[index], norm_gain[index], router[index], w_in[index], w_out[index]) for index in range(SECTIONS)]
    layer_outs = jnp.stack([item[0] for item in results])
    in_grads = jnp.stack([item[1] for item in results])
    grad_in = jnp.stack([item[2] for item in results])
    grad_out = jnp.stack([item[3] for item in results])
    grad_router = jnp.stack([item[4] for item in results])
    grad_gain = jnp.stack([item[5] for item in results])
    handoff = jnp.roll(layer_outs, 1, axis=0)
    handback = jnp.roll(in_grads, -1, axis=0)
    return (handoff, handback, grad_in, grad_out, grad_router, grad_gain)
```

```python
import jax
import jax.numpy as jnp
from jax import lax
from jax.sharding import PartitionSpec as P

MOST = 10
LANES = 128
BF = jnp.bfloat16
F32 = jnp.float32
ALL = ("dp", "expert")


def exchange(blocks, axes):
    return lax.all_to_all(blocks, axes, split_axis=0, concat_axis=0, tiled=True)


def mm(left, right, contract):
    return lax.dot_general(left, right, (contract, ((), ())), preferred_element_type=F32)


def two_terms(values):
    high = values.astype(BF)
    return high, (values - high.astype(F32)).astype(BF)


def mm_wide_left(left, right, contract):
    high, low = two_terms(left)
    return mm(high, right, contract) + mm(low, right, contract)


def shards(section_input, routing, out_grad, norm_gain, router, w_in, w_out):
    experts = lax.axis_size("expert")
    replicas = lax.axis_size("dp")
    x = section_input[0]
    route_ids = routing[0]
    grad_top = out_grad[0]
    gain = norm_gain[0][None, :]
    table = router[0]
    first = w_in[0, 0]
    second = w_out[0, 0]
    tokens, width = x.shape
    part = width // replicas
    hidden_width = second.shape[0]
    slots = MOST
    rows = experts * slots
    router_width = table.shape[1]

    xw = x.astype(F32)
    inv_rms = lax.rsqrt(jnp.mean(xw * xw, axis=1, keepdims=True) + 1e-06)
    normed = (xw * inv_rms * gain).astype(BF)
    logits = jnp.dot(normed, table, preferred_element_type=F32)
    columns = jnp.arange(router_width, dtype=jnp.int32)
    named = jnp.any(route_ids[:, :, None] == columns, axis=1)
    powers = jnp.where(named, jnp.exp(logits), 0.0)
    gates = powers / jnp.sum(powers, axis=1, keepdims=True)
    window = named[:, :experts]
    earlier = jnp.tri(tokens, tokens, -1, dtype=BF)
    rank = jnp.dot(earlier, window.astype(BF), preferred_element_type=F32)
    slot_ids = jnp.arange(slots, dtype=F32)
    hits = (window[:, :, None] & (rank[:, :, None] == slot_ids)).reshape(tokens, rows)
    place = hits.astype(BF)
    combine = jnp.where(hits, jnp.repeat(gates[:, :experts], slots, axis=1), 0.0)
    slot_gate = jnp.sum(combine, axis=0)[:, None]

    def outbound(picked):
        return picked.astype(BF).reshape(experts, slots, replicas, part).transpose(2, 0, 1, 3)

    picked_normed = mm(place, normed, ((0,), (0,)))
    picked_grad = mm(place, grad_top, ((0,), (0,))) * slot_gate
    message = jnp.concatenate([outbound(picked_normed), outbound(picked_grad)], axis=2)
    message = message.reshape(replicas * experts, 2 * slots * part // LANES, LANES)
    arrived = exchange(message, ALL).reshape(replicas * experts, 2 * slots, part)
    expert_rows = arrived[:, :slots].reshape(-1, part)
    grad_rows = arrived[:, slots:].reshape(-1, part)

    partial = jnp.concatenate(
        [mm(expert_rows, first, ((1,), (0,))).astype(BF), mm(grad_rows, second, ((1,), (1,))).astype(BF)],
        axis=1,
    ).reshape(replicas, rows, 3 * hidden_width)
    total = jnp.sum(exchange(partial, "dp").astype(F32), axis=0)
    gate_pre = total[:, :hidden_width]
    up = total[:, hidden_width : 2 * hidden_width]
    hidden_grad = total[:, 2 * hidden_width :]
    sigmoid = jax.nn.sigmoid(gate_pre)
    silu = gate_pre * sigmoid
    slope = sigmoid * (1.0 + gate_pre * (1.0 - sigmoid))
    hidden = (silu * up).astype(BF)
    worth = jnp.sum(hidden_grad * hidden.astype(F32), axis=1)
    acts = jnp.concatenate(
        [(hidden_grad * up * slope).astype(BF), (hidden_grad * silu).astype(BF), hidden], axis=1
    )
    gathered = exchange(jnp.broadcast_to(acts[None], (replicas,) + acts.shape), "dp")
    gathered = gathered.reshape(-1, 3 * hidden_width)
    pre_grad = gathered[:, : 2 * hidden_width]
    hidden_all = gathered[:, 2 * hidden_width :]

    worth = jnp.pad(worth.reshape(experts, 1, slots), ((0, 0), (0, 0), (0, LANES - slots)))
    worth = exchange(worth, "expert")[:, 0, :slots].reshape(1, rows)
    gate_worth = jnp.sum(
        jnp.where(hits, worth, 0.0).reshape(tokens, experts, slots), axis=2
    )
    inner = jnp.sum(gate_worth, axis=1, keepdims=True)
    logit_grad = jnp.pad(gate_worth, ((0, 0), (0, router_width - experts))) - gates * inner
    logit_high, logit_low = two_terms(logit_grad)
    local_router = mm(normed, logit_high, ((0,), (0,))) + mm(normed, logit_low, ((0,), (0,)))
    router_part = exchange(local_router.astype(BF).reshape(replicas, part, router_width), "dp")
    router_part = jnp.sum(router_part.astype(F32), axis=0)

    out_rows = mm(hidden_all, second, ((1,), (0,))).astype(BF)
    back_rows = mm(pre_grad, first, ((1,), (1,))).astype(BF)
    message = jnp.concatenate(
        [out_rows.reshape(-1, slots, part), back_rows.reshape(-1, slots, part)], axis=1
    ).reshape(replicas * experts, 2 * slots * part // LANES, LANES)
    returned = exchange(message, ALL).reshape(replicas, experts, 2 * slots, part)

    first_grad = mm(expert_rows, pre_grad, ((0,), (0,)))
    second_grad = mm(hidden_all, grad_rows, ((0,), (0,)))
    gain_part = jnp.sum(first_grad * first.astype(F32), axis=1)

    piece = part // experts
    gain_rows = jnp.pad(gain_part.reshape(experts, 1, piece), ((0, 0), (0, 7), (0, LANES - piece)))
    owned = jnp.concatenate([router_part.reshape(experts, piece, router_width), gain_rows], axis=1)
    owned = jnp.sum(exchange(owned, "expert"), axis=0)
    router_own = owned[:piece]
    index = lax.axis_index("dp") * part + lax.axis_index("expert") * piece
    table_own = lax.dynamic_slice_in_dim(table, index, piece, axis=0).astype(F32)
    gain_here = lax.dynamic_slice_in_dim(gain[0], index, piece, axis=0)
    gain_own = (owned[piece, :piece] + jnp.sum(router_own * table_own, axis=1)) / gain_here
    gain_high = gain_own.astype(BF)
    gain_mid, gain_low = two_terms(gain_own - gain_high.astype(F32))
    gain_terms = jnp.stack([gain_high, gain_mid, gain_low])
    gain_terms = jnp.pad(gain_terms, ((0, 13), (0, LANES - piece)))
    block = jnp.concatenate([router_own.astype(BF), gain_terms], axis=0)
    joined = exchange(jnp.broadcast_to(block[None], (experts,) + block.shape), "expert")
    joined = exchange(jnp.broadcast_to(joined[None], (replicas,) + joined.shape), "dp")
    joined = joined.reshape(replicas * experts, piece + 16, LANES)
    router_total = joined[:, :piece].reshape(width, router_width)
    gain_total = jnp.sum(joined[:, piece : piece + 3, :piece].astype(F32), axis=1).reshape(width)

    def inbound(block):
        return block.transpose(1, 2, 0, 3).reshape(rows, width)

    mixed = mm_wide_left(combine, inbound(returned[:, :, :slots]), ((1,), (0,)))
    layer_out = (xw + mixed).astype(BF)
    normed_grad = mm(place, inbound(returned[:, :, slots:]), ((1,), (0,)))
    normed_grad = (
        normed_grad + mm(logit_high, table, ((1,), (1,))) + mm(logit_low, table, ((1,), (1,)))
    )
    weighted = gain * normed_grad
    in_grad = (
        grad_top.astype(F32)
        + inv_rms * weighted
        - xw * inv_rms * inv_rms * inv_rms * jnp.mean(xw * weighted, axis=1, keepdims=True)
    ).astype(BF)
    swap = [(0, 1), (1, 0)]
    handoff = lax.ppermute(layer_out, "section", swap)
    handback = lax.ppermute(in_grad, "section", swap)
    return (
        handoff[None],
        handback[None],
        first_grad.astype(BF)[None, None],
        second_grad.astype(BF)[None, None],
        router_total[None],
        gain_total[None],
    )


def solution(mesh):
    return jax.shard_map(
        shards,
        mesh=mesh,
        in_specs=(
            P("section", ("expert", "dp"), None),
            P("section", ("expert", "dp"), None),
            P("section", ("expert", "dp"), None),
            P("section", None),
            P("section", None, None),
            P("section", "expert", "dp", None),
            P("section", "expert", None, "dp"),
        ),
        out_specs=(
            P("section", ("expert", "dp"), None),
            P("section", ("expert", "dp"), None),
            P("section", "expert", "dp", None),
            P("section", "expert", None, "dp"),
            P("section", None, None),
            P("section", None),
        ),
        check_vma=False,
    )
```

```python
import functools

import jax
import jax.numpy as jnp
import numpy as np
from jax import lax
from jax.experimental import pallas as pl
from jax.experimental.pallas import tpu as pltpu
from jax.sharding import PartitionSpec as P

MOST = 10
LANES = 128
BF = jnp.bfloat16
F32 = jnp.float32
ALL = ("dp", "expert")
INTERPRET = False
HIDDEN_STEPS = 3


def exchange(blocks, axes):
    return lax.all_to_all(blocks, axes, split_axis=0, concat_axis=0, tiled=True)


def mm(left, right, contract=((1,), (0,))):
    return lax.dot_general(left, right, (contract, ((), ())), preferred_element_type=F32)


def two_terms(values):
    high = values.astype(BF)
    return high, (values - high.astype(F32)).astype(BF)


def three_terms(values):
    high = values.astype(BF)
    return (high,) + two_terms(values - high.astype(F32))


def kernel_call(body, outs, args, scratch=(), **grid):
    return pl.pallas_call(
        body,
        out_shape=outs,
        scratch_shapes=scratch,
        compiler_params=pltpu.CompilerParams(vmem_limit_bytes=52 * 2**20),
        interpret=INTERPRET,
        **grid,
    )(*args)


def iota(shape, dimension):
    return lax.broadcasted_iota(jnp.int32, shape, dimension)


def spread(values, owner):
    pick = (iota((values[0].shape[1], owner.shape[1]), 0) == owner).astype(BF)
    total = mm(values[0], pick)
    for term in values[1:]:
        total = total + mm(term, pick)
    return total


def send_kernel(experts, replicas, chunks, slots, x, ids, grad, gain, table, owner, chunk_of, slot_of,
                message, normed_out, gates_out, place_out, stack):
    tokens, width = x.shape
    part = width // replicas
    half = chunks * slots
    xw = x[...].astype(F32)
    inv_rms = lax.rsqrt(jnp.mean(xw * xw, axis=1, keepdims=True) + 1e-06)
    normed = (xw * inv_rms * gain[...]).astype(BF)
    normed_out[...] = normed
    logits = mm(normed, table[...])
    columns = iota(logits.shape, 1)
    named = columns == ids[:, 0:1]
    for k in range(1, ids.shape[1]):
        named = named | (columns == ids[:, k : k + 1])
    powers = jnp.where(named, jnp.exp(logits), 0.0)
    gates = powers / jnp.sum(powers, axis=1, keepdims=True)
    gates_out[...] = gates
    earlier = (iota((tokens, tokens), 1) < iota((tokens, tokens), 0)).astype(BF)
    rank = mm(earlier, named.astype(BF))
    place = jnp.where(named & (columns < experts), rank, -1.0)
    place_out[...] = place

    hits = spread((place.astype(BF),), owner[...]) == slot_of[...].astype(F32)
    weight = jnp.where(hits, spread(three_terms(gates), owner[...]), 0.0)
    slot_gate = jnp.sum(weight.T, axis=1, keepdims=True)
    hits_rows = jnp.where(hits, 1.0, 0.0).T
    pick = jnp.concatenate(
        [jnp.where(chunk_of[...] == c, hits_rows, 0.0).astype(BF) for c in range(chunks)], axis=1
    )

    def stacked(load):
        for c in range(chunks):
            for j in range(replicas):
                at = j * part + c * LANES
                stack[c * tokens : (c + 1) * tokens, j * LANES : (j + 1) * LANES] = load(at)
        return mm(pick, stack[...])

    sent = stacked(lambda at: normed_out[:, at : at + LANES])
    sent_grad = stacked(lambda at: grad[:, at : at + LANES]) * slot_gate
    for j in range(replicas):
        for e in range(experts):
            rows, lanes = slice(e * half, (e + 1) * half), slice(j * LANES, (j + 1) * LANES)
            message[j * experts + e] = jnp.concatenate(
                [sent[rows, lanes], sent_grad[rows, lanes]], axis=0
            ).astype(BF)


def products_kernel(group, chunks, slots, arrived, order, first, second, partial, rows_out, grads_out):
    step = pl.program_id(0)
    total, per_message, _ = arrived.shape
    size = group * per_message
    block = group * slots
    steps_first = 2 * HIDDEN_STEPS

    @pl.when(step == 0)
    def _():
        pick = (order[...] == iota((size, size), 1)).astype(BF)
        sets = total // group
        wide = 2 if sets % 2 == 0 else 1
        for pair in range(sets // wide):
            loaded = [
                arrived[(pair * wide + w) * group : (pair * wide + w + 1) * group].reshape(size, LANES)
                for w in range(wide)
            ]
            picked = mm(pick, jnp.concatenate(loaded, axis=1)).astype(BF)
            for w in range(wide):
                at = (pair * wide + w) * block
                for c in range(chunks):
                    lanes = slice(w * LANES, (w + 1) * LANES)
                    rows_out[at : at + block, c * LANES : (c + 1) * LANES] = picked[
                        c * block : (c + 1) * block, lanes
                    ]
                    grads_out[at : at + block, c * LANES : (c + 1) * LANES] = picked[
                        (chunks + c) * block : (chunks + c + 1) * block, lanes
                    ]

    @pl.when(step < steps_first)
    def _():
        partial[...] = mm(rows_out[...], first[...]).astype(BF)

    @pl.when(step >= steps_first)
    def _():
        partial[...] = mm(grads_out[...], second[...], ((1,), (1,))).astype(BF)


def act_kernel(slots, arrived, sender_of, slot_of, acts, worth):
    replicas, rows, width = arrived.shape
    hidden_width = width // 3
    total = arrived[0].astype(F32)
    for j in range(1, replicas):
        total = total + arrived[j].astype(F32)
    gate_pre = total[:, :hidden_width]
    up = total[:, hidden_width : 2 * hidden_width]
    hidden_grad = total[:, 2 * hidden_width :]
    sigmoid = 1.0 / (1.0 + jnp.exp(-gate_pre))
    silu = gate_pre * sigmoid
    slope = sigmoid * (1.0 + gate_pre * (1.0 - sigmoid))
    hidden = (silu * up).astype(BF)
    gate_grad = (hidden_grad * up * slope).astype(BF)
    up_grad = (hidden_grad * silu).astype(BF)
    for j in range(replicas):
        acts[j, :, :hidden_width] = gate_grad
        acts[j, :, hidden_width : 2 * hidden_width] = up_grad
        acts[j, :, 2 * hidden_width :] = hidden
    each = jnp.sum(hidden_grad * hidden.astype(F32), axis=1, keepdims=True)
    laid = jnp.where(slot_of[...] == iota((rows, LANES), 1), each, 0.0)
    pick = (sender_of[...] == iota((worth.shape[0], rows), 0)).astype(BF)
    terms = three_terms(laid)
    worth[...] = mm(pick, terms[0]) + mm(pick, terms[1]) + mm(pick, terms[2])


def back_kernel(group, chunks, slots, gathered, order, first, second, message):
    rows, width = gathered.shape
    hidden_width = width // 3
    block = group * slots
    size = 2 * chunks * block
    per_message = 2 * chunks * slots
    outs = mm(gathered[:, 2 * hidden_width :], second[...]).astype(BF)
    backs = mm(gathered[:, : 2 * hidden_width], first[...], ((1,), (1,))).astype(BF)
    pick = (order[...] == iota((size, size), 1)).astype(BF)
    sets = rows // block
    wide = 2 if sets % 2 == 0 else 1

    def column(at):
        return jnp.concatenate(
            [
                source[at : at + block, c * LANES : (c + 1) * LANES]
                for source in (outs, backs)
                for c in range(chunks)
            ],
            axis=0,
        )

    for pair in range(sets // wide):
        loaded = [column((pair * wide + w) * block) for w in range(wide)]
        picked = mm(pick, jnp.concatenate(loaded, axis=1)).astype(BF)
        for w in range(wide):
            at = (pair * wide + w) * group
            message[at : at + group] = picked[:, w * LANES : (w + 1) * LANES].reshape(
                group, per_message, LANES
            )


def combine_kernel(experts, replicas, chunks, slots, returned, x, grad, gain, table, gates, place, logit_grad,
                   owner, kind_of, chunk_of, slot_of, layer_out, in_grad, joined, normed_grad):
    tokens, width = x.shape
    part = width // replicas
    count, per_message, _ = returned.shape
    for j in range(replicas):
        block = returned[j * experts : (j + 1) * experts]
        joined[:, j * LANES : (j + 1) * LANES] = block.reshape(experts * per_message, LANES)
    hits = spread((place[...].astype(BF),), owner[...]) == slot_of[...].astype(F32)
    high, low = (
        jnp.where(hits, spread((term,), owner[...]), 0.0) for term in two_terms(gates[...])
    )
    ones = jnp.where(hits, 1.0, 0.0)
    kind = kind_of[...]
    chunk = chunk_of[...]

    def picks(values, which):
        return jnp.concatenate(
            [
                jnp.where((kind == which) & (chunk == c), values, 0.0).astype(BF)
                for c in range(chunks)
            ],
            axis=0,
        )

    source = joined[...]
    mixed = mm(picks(high, 0), source) + mm(picks(low, 0), source)
    back = mm(picks(ones, 1), source)
    logit_high, logit_low = two_terms(logit_grad[...])
    by_logits = mm(logit_high, table[...], ((1,), (1,))) + mm(logit_low, table[...], ((1,), (1,)))
    for c in range(chunks):
        rows = slice(c * tokens, (c + 1) * tokens)
        for j in range(replicas):
            lanes = slice(j * LANES, (j + 1) * LANES)
            at = slice(j * part + c * LANES, j * part + (c + 1) * LANES)
            layer_out[:, at] = (x[:, at].astype(F32) + mixed[rows, lanes]).astype(BF)
            normed_grad[:, at] = back[rows, lanes] + by_logits[:, at]
    xw = x[...].astype(F32)
    inv_rms = lax.rsqrt(jnp.mean(xw * xw, axis=1, keepdims=True) + 1e-06)
    weighted = gain[...] * normed_grad[...]
    mean = jnp.mean(xw * weighted, axis=1, keepdims=True)
    in_grad[...] = (
        grad[...].astype(F32) + inv_rms * weighted - xw * (inv_rms * inv_rms * inv_rms * mean)
    ).astype(BF)


def shards(section_input, routing, out_grad, norm_gain, router, w_in, w_out):
    experts = lax.axis_size("expert")
    replicas = lax.axis_size("dp")
    x = section_input[0]
    route_ids = routing[0]
    grad_top = out_grad[0]
    gain = norm_gain[0][None, :]
    table = router[0]
    first = w_in[0, 0]
    second = w_out[0, 0]
    tokens, width = x.shape
    part = width // replicas
    hidden_width = second.shape[0]
    slots = MOST
    rows = experts * slots
    router_width = table.shape[1]
    chunks = part // LANES
    half = chunks * slots
    peers = replicas * experts
    group = min(8, experts)
    message_shape = jax.ShapeDtypeStruct((peers, 2 * half, LANES), BF)

    at = np.arange(experts * half, dtype=np.int32)
    message, normed, gates, place = kernel_call(
        functools.partial(send_kernel, experts, replicas, chunks, slots),
        (
            message_shape,
            jax.ShapeDtypeStruct((tokens, width), BF),
            jax.ShapeDtypeStruct((tokens, router_width), F32),
            jax.ShapeDtypeStruct((tokens, router_width), F32),
        ),
        (x, route_ids, grad_top, gain, table, at[None] // half, (at % half // slots)[:, None], at[None] % slots),
        [pltpu.VMEM((chunks * tokens, replicas * LANES), BF)],
    )
    arrived = exchange(message, ALL)

    at = np.arange(group * 2 * half, dtype=np.int32)
    sender, inner_row, slot = at // (2 * half), at % (2 * half) // slots, at % slots
    into_rows = np.zeros_like(at)
    into_rows[(inner_row * group + sender) * slots + slot] = at
    into_messages = (inner_row * group + sender) * slots + slot
    step_width = hidden_width // HIDDEN_STEPS
    all_rows = peers * slots
    partial, expert_rows, grad_rows = kernel_call(
        functools.partial(products_kernel, group, chunks, slots),
        (
            jax.ShapeDtypeStruct((all_rows, 3 * hidden_width), BF),
            jax.ShapeDtypeStruct((all_rows, part), BF),
            jax.ShapeDtypeStruct((all_rows, part), BF),
        ),
        (arrived, into_rows[:, None], first, second),
        grid=(3 * HIDDEN_STEPS,),
        in_specs=[
            pl.BlockSpec(arrived.shape, lambda i: (0, 0, 0)),
            pl.BlockSpec((at.size, 1), lambda i: (0, 0)),
            pl.BlockSpec((part, step_width), lambda i: (0, jnp.minimum(i, 2 * HIDDEN_STEPS - 1))),
            pl.BlockSpec((step_width, part), lambda i: (jnp.maximum(i - 2 * HIDDEN_STEPS, 0), 0)),
        ],
        out_specs=[
            pl.BlockSpec((all_rows, step_width), lambda i: (0, i)),
            pl.BlockSpec((all_rows, part), lambda i: (0, 0)),
            pl.BlockSpec((all_rows, part), lambda i: (0, 0)),
        ],
    )
    summands = exchange(partial.reshape(replicas, rows, 3 * hidden_width), "dp")
    at = np.arange(rows, dtype=np.int32)
    acts, worth = kernel_call(
        functools.partial(act_kernel, slots),
        (
            jax.ShapeDtypeStruct(summands.shape, BF),
            jax.ShapeDtypeStruct((experts, LANES), F32),
        ),
        (summands, at[None] // slots, at[:, None] % slots),
    )
    gathered = exchange(acts, "dp").reshape(-1, 3 * hidden_width)
    pre_grad = gathered[:, : 2 * hidden_width]
    hidden_all = gathered[:, 2 * hidden_width :]

    worth = exchange(worth[:, None], "expert")[:, 0, :slots]
    slot_ids = jnp.arange(slots, dtype=F32)
    gate_worth = jnp.sum(
        jnp.where(place[:, :experts, None] == slot_ids, worth[None], 0.0), axis=2
    )
    inner = jnp.sum(gate_worth, axis=1, keepdims=True)
    logit_grad = jnp.pad(gate_worth, ((0, 0), (0, router_width - experts))) - gates * inner
    logit_high, logit_low = two_terms(logit_grad)
    local_router = mm(normed, logit_high, ((0,), (0,))) + mm(normed, logit_low, ((0,), (0,)))
    router_part = exchange(local_router.astype(BF).reshape(replicas, part, router_width), "dp")
    router_part = jnp.sum(router_part.astype(F32), axis=0)

    steps = 4 if replicas % 4 == 0 else 1
    message = kernel_call(
        functools.partial(back_kernel, group, chunks, slots),
        message_shape,
        (gathered, into_messages[:, None], first, second),
        grid=(steps,),
        in_specs=[
            pl.BlockSpec((all_rows // steps, 3 * hidden_width), lambda i: (i, 0)),
            pl.BlockSpec((into_messages.size, 1), lambda i: (0, 0)),
            pl.BlockSpec(first.shape, lambda i: (0, 0)),
            pl.BlockSpec(second.shape, lambda i: (0, 0)),
        ],
        out_specs=pl.BlockSpec((peers // steps, 2 * half, LANES), lambda i: (i, 0, 0)),
    )
    returned = exchange(message, ALL)

    first_grad = mm(expert_rows, pre_grad, ((0,), (0,)))
    second_grad = mm(hidden_all, grad_rows, ((0,), (0,)))
    gain_part = jnp.sum(first_grad * first.astype(F32), axis=1)

    piece = part // experts
    gain_rows = jnp.pad(gain_part.reshape(experts, 1, piece), ((0, 0), (0, 7), (0, LANES - piece)))
    owned = jnp.concatenate([router_part.reshape(experts, piece, router_width), gain_rows], axis=1)
    owned = jnp.sum(exchange(owned, "expert"), axis=0)
    router_own = owned[:piece]
    index = lax.axis_index("dp") * part + lax.axis_index("expert") * piece
    table_own = lax.dynamic_slice_in_dim(table, index, piece, axis=0).astype(F32)
    gain_here = lax.dynamic_slice_in_dim(gain[0], index, piece, axis=0)
    gain_own = (owned[piece, :piece] + jnp.sum(router_own * table_own, axis=1)) / gain_here
    gain_high = gain_own.astype(BF)
    gain_mid, gain_low = two_terms(gain_own - gain_high.astype(F32))
    gain_terms = jnp.stack([gain_high, gain_mid, gain_low])
    gain_terms = jnp.pad(gain_terms, ((0, 13), (0, LANES - piece)))
    block = jnp.concatenate([router_own.astype(BF), gain_terms], axis=0)
    joined = exchange(jnp.broadcast_to(block[None], (experts,) + block.shape), "expert")
    joined = exchange(jnp.broadcast_to(joined[None], (replicas,) + joined.shape), "dp")
    joined = joined.reshape(replicas * experts, piece + 16, LANES)
    router_total = joined[:, :piece].reshape(width, router_width)
    gain_total = jnp.sum(joined[:, piece : piece + 3, :piece].astype(F32), axis=1).reshape(width)

    at = np.arange(experts * 2 * half, dtype=np.int32)[None]
    layer_out, in_grad = kernel_call(
        functools.partial(combine_kernel, experts, replicas, chunks, slots),
        (
            jax.ShapeDtypeStruct((tokens, width), BF),
            jax.ShapeDtypeStruct((tokens, width), BF),
        ),
        (
            returned, x, grad_top, gain, table, gates, place, logit_grad,
            at // (2 * half), at % (2 * half) // half, at % half // slots, at % slots,
        ),
        [
            pltpu.VMEM((experts * 2 * half, replicas * LANES), BF),
            pltpu.VMEM((tokens, width), F32),
        ],
    )
    swap = [(0, 1), (1, 0)]
    handoff = lax.ppermute(layer_out, "section", swap)
    handback = lax.ppermute(in_grad, "section", swap)
    return (
        handoff[None],
        handback[None],
        first_grad.astype(BF)[None, None],
        second_grad.astype(BF)[None, None],
        router_total[None],
        gain_total[None],
    )


def solution(mesh):
    return jax.shard_map(
        shards,
        mesh=mesh,
        in_specs=(
            P("section", ("expert", "dp"), None),
            P("section", ("expert", "dp"), None),
            P("section", ("expert", "dp"), None),
            P("section", None),
            P("section", None, None),
            P("section", "expert", "dp", None),
            P("section", "expert", None, "dp"),
        ),
        out_specs=(
            P("section", ("expert", "dp"), None),
            P("section", ("expert", "dp"), None),
            P("section", "expert", "dp", None),
            P("section", "expert", None, "dp"),
            P("section", None, None),
            P("section", None),
        ),
        check_vma=False,
    )
```

```python
import functools

import jax
import jax.numpy as jnp
import numpy as np
from jax import lax
from jax.experimental import pallas as pl
from jax.experimental.pallas import tpu as pltpu
from jax.sharding import Mesh
from jax.sharding import PartitionSpec as P

MOST = 10
LANES = 128
BF = jnp.bfloat16
F32 = jnp.float32
SHARE = ("dp", "expert")
OWNERS = ("half", "expert")
INTERPRET = False
HIDDEN_STEPS = 3


def exchange(blocks, axes):
    return lax.all_to_all(blocks, axes, split_axis=0, concat_axis=0, tiled=True)


def mm(left, right, contract=((1,), (0,))):
    return lax.dot_general(left, right, (contract, ((), ())), preferred_element_type=F32)


def two_terms(values):
    high = values.astype(BF)
    return high, (values - high.astype(F32)).astype(BF)


def three_terms(values):
    high = values.astype(BF)
    return (high,) + two_terms(values - high.astype(F32))


def kernel_call(body, outs, args, scratch=(), **grid):
    return pl.pallas_call(
        body,
        out_shape=outs,
        scratch_shapes=scratch,
        compiler_params=pltpu.CompilerParams(vmem_limit_bytes=52 * 2**20),
        interpret=INTERPRET,
        **grid,
    )(*args)


def iota(shape, dimension):
    return lax.broadcasted_iota(jnp.int32, shape, dimension)


def spread(values, owner):
    pick = (iota((values[0].shape[1], owner.shape[1]), 0) == owner).astype(BF)
    total = mm(values[0], pick)
    for term in values[1:]:
        total = total + mm(term, pick)
    return total


def feature(replicas, width, c, j):
    part = width // (2 * replicas)
    block, inner = divmod(c * LANES, part)
    return (block * replicas + j) * part + inner


def send_kernel(experts, replicas, chunks, slots, x, ids, grad, gain, table, owner, chunk_of, slot_of,
                message, normed_out, gates_out, place_out, stack):
    tokens, width = x.shape
    half = chunks * slots
    xw = x[...].astype(F32)
    inv_rms = lax.rsqrt(jnp.mean(xw * xw, axis=1, keepdims=True) + 1e-06)
    normed = (xw * inv_rms * gain[...]).astype(BF)
    normed_out[...] = normed
    logits = mm(normed, table[...])
    columns = iota(logits.shape, 1)
    named = columns == ids[:, 0:1]
    for k in range(1, ids.shape[1]):
        named = named | (columns == ids[:, k : k + 1])
    powers = jnp.where(named, jnp.exp(logits), 0.0)
    gates = powers / jnp.sum(powers, axis=1, keepdims=True)
    gates_out[...] = gates
    earlier = (iota((tokens, tokens), 1) < iota((tokens, tokens), 0)).astype(BF)
    rank = mm(earlier, named.astype(BF))
    place = jnp.where(named & (columns < experts), rank, -1.0)
    place_out[...] = place

    hits = spread((place.astype(BF),), owner[...]) == slot_of[...].astype(F32)
    weight = jnp.where(hits, spread(three_terms(gates), owner[...]), 0.0)
    slot_gate = jnp.sum(weight.T, axis=1, keepdims=True)
    hits_rows = jnp.where(hits, 1.0, 0.0).T
    pick = jnp.concatenate(
        [jnp.where(chunk_of[...] == c, hits_rows, 0.0).astype(BF) for c in range(chunks)], axis=1
    )

    def stacked(source):
        for c in range(chunks):
            for j in range(replicas):
                at = feature(replicas, width, c, j)
                stack[c * tokens : (c + 1) * tokens, j * LANES : (j + 1) * LANES] = source[
                    :, at : at + LANES
                ]
        return mm(pick, stack[...])

    for kind, sent in enumerate((stacked(normed_out), stacked(grad) * slot_gate)):
        sent = sent.astype(BF)
        for j in range(replicas):
            for e in range(experts):
                message[j * experts + e, kind * half : (kind + 1) * half] = sent[
                    e * half : (e + 1) * half, j * LANES : (j + 1) * LANES
                ]


def products_kernel(group, chunks, slots, index, arrived, order, first, first_other, second, second_other,
                    partial, rows_out, grads_out):
    step = pl.program_id(0)
    half = chunks * slots
    size = group * half
    block = group * slots
    own_chunks = chunks // 2
    part = own_chunks * LANES

    @pl.when(step == 0)
    def _():
        lower = index[0] == 0
        pick = (order[...] == iota((size, size), 1)).astype(BF)
        for at in range(arrived.shape[0] // group):
            lanes = [
                arrived[at * group : (at + 1) * group, kind * half : (kind + 1) * half].reshape(size, LANES)
                for kind in range(2)
            ]
            picked = mm(pick, jnp.concatenate(lanes, axis=1)).astype(BF)
            rows = slice(at * block, (at + 1) * block)
            for c in range(own_chunks):
                low = picked[c * block : (c + 1) * block]
                high = picked[(own_chunks + c) * block : (own_chunks + c + 1) * block]
                own = jnp.where(lower, low, high)
                other = jnp.where(lower, high, low)
                here = slice(c * LANES, (c + 1) * LANES)
                there = slice(part + c * LANES, part + (c + 1) * LANES)
                rows_out[rows, here] = own[:, :LANES]
                rows_out[rows, there] = other[:, :LANES]
                grads_out[rows, here] = own[:, LANES:]
                grads_out[rows, there] = other[:, LANES:]

    @pl.when(step < 2 * HIDDEN_STEPS)
    def _():
        partial[...] = (
            mm(rows_out[:, :part], first[...]) + mm(rows_out[:, part:], first_other[...])
        ).astype(BF)

    @pl.when(step >= 2 * HIDDEN_STEPS)
    def _():
        partial[...] = (
            mm(grads_out[:, :part], second[...], ((1,), (1,)))
            + mm(grads_out[:, part:], second_other[...], ((1,), (1,)))
        ).astype(BF)


def act_kernel(slots, arrived, sender_of, slot_of, acts, worth):
    replicas, rows, width = arrived.shape
    hidden_width = width // 3
    total = arrived[0].astype(F32)
    for j in range(1, replicas):
        total = total + arrived[j].astype(F32)
    gate_pre = total[:, :hidden_width]
    up = total[:, hidden_width : 2 * hidden_width]
    hidden_grad = total[:, 2 * hidden_width :]
    sigmoid = 1.0 / (1.0 + jnp.exp(-gate_pre))
    silu = gate_pre * sigmoid
    slope = sigmoid * (1.0 + gate_pre * (1.0 - sigmoid))
    hidden = (silu * up).astype(BF)
    gate_grad = (hidden_grad * up * slope).astype(BF)
    up_grad = (hidden_grad * silu).astype(BF)
    for j in range(replicas):
        acts[j, :, :hidden_width] = gate_grad
        acts[j, :, hidden_width : 2 * hidden_width] = up_grad
        acts[j, :, 2 * hidden_width :] = hidden
    each = jnp.sum(hidden_grad * hidden.astype(F32), axis=1, keepdims=True)
    laid = jnp.where(slot_of[...] == iota((rows, LANES), 1), each, 0.0)
    pick = (sender_of[...] == iota((worth.shape[0], rows), 0)).astype(BF)
    terms = three_terms(laid)
    worth[...] = mm(pick, terms[0]) + mm(pick, terms[1]) + mm(pick, terms[2])


def back_kernel(group, chunks, slots, index, gathered, order, first, first_other, second, second_other, message):
    rows, width = gathered.shape
    hidden_width = width // 3
    block = group * slots
    half = chunks * slots
    size = group * half
    own_chunks = chunks // 2
    hidden = gathered[:, 2 * hidden_width :]
    pre_grad = gathered[:, : 2 * hidden_width]
    lower = index[0] == 0

    def ordered(own, other):
        own, other = own.astype(BF), other.astype(BF)
        return jnp.where(lower, own, other), jnp.where(lower, other, own)

    outs = ordered(mm(hidden, second[...]), mm(hidden, second_other[...]))
    backs = ordered(mm(pre_grad, first[...], ((1,), (1,))), mm(pre_grad, first_other[...], ((1,), (1,))))
    pick = (order[...] == iota((size, size), 1)).astype(BF)

    def column(source, at):
        return jnp.concatenate(
            [
                side[at : at + block, c * LANES : (c + 1) * LANES]
                for side in source
                for c in range(own_chunks)
            ],
            axis=0,
        )

    for at in range(rows // block):
        lanes = [column(source, at * block) for source in (outs, backs)]
        picked = mm(pick, jnp.concatenate(lanes, axis=1)).astype(BF)
        for kind in range(2):
            message[at * group : (at + 1) * group, kind * half : (kind + 1) * half] = picked[
                :, kind * LANES : (kind + 1) * LANES
            ].reshape(group, half, LANES)


def combine_kernel(experts, replicas, chunks, slots, returned, x, grad, gain, table, gates, place, logit_grad,
                   owner, chunk_of, slot_of, layer_out, in_grad, joined, normed_grad):
    tokens, width = x.shape
    half = chunks * slots

    def join(kind):
        for j in range(replicas):
            block = returned[j * experts : (j + 1) * experts, kind * half : (kind + 1) * half]
            joined[:, j * LANES : (j + 1) * LANES] = block.reshape(experts * half, LANES)
        return joined[...]

    hits = spread((place[...].astype(BF),), owner[...]) == slot_of[...].astype(F32)
    high, low = (
        jnp.where(hits, spread((term,), owner[...]), 0.0) for term in two_terms(gates[...])
    )
    ones = jnp.where(hits, 1.0, 0.0)
    chunk = chunk_of[...]

    def picks(values):
        return jnp.concatenate(
            [jnp.where(chunk == c, values, 0.0).astype(BF) for c in range(chunks)], axis=0
        )

    source = join(0)
    mixed = mm(picks(high), source) + mm(picks(low), source)
    back = mm(picks(ones), join(1))
    logit_high, logit_low = two_terms(logit_grad[...])
    by_logits = mm(logit_high, table[...], ((1,), (1,))) + mm(logit_low, table[...], ((1,), (1,)))
    for c in range(chunks):
        rows = slice(c * tokens, (c + 1) * tokens)
        for j in range(replicas):
            lanes = slice(j * LANES, (j + 1) * LANES)
            at = feature(replicas, width, c, j)
            at = slice(at, at + LANES)
            layer_out[:, at] = (x[:, at].astype(F32) + mixed[rows, lanes]).astype(BF)
            normed_grad[:, at] = back[rows, lanes] + by_logits[:, at]
    xw = x[...].astype(F32)
    inv_rms = lax.rsqrt(jnp.mean(xw * xw, axis=1, keepdims=True) + 1e-06)
    weighted = gain[...] * normed_grad[...]
    mean = jnp.mean(xw * weighted, axis=1, keepdims=True)
    in_grad[...] = (
        grad[...].astype(F32) + inv_rms * weighted - xw * (inv_rms * inv_rms * inv_rms * mean)
    ).astype(BF)


def swapped(block, axis):
    return lax.ppermute(block, axis, [(0, 1), (1, 0)])


def shards(section_input, routing, out_grad, norm_gain, router, w_in, w_out):
    experts = lax.axis_size("expert")
    replicas = lax.axis_size("dp")
    x = section_input[0]
    route_ids = routing[0]
    grad_top = out_grad[0]
    gain = norm_gain[0][None, :]
    table = router[0]
    first = w_in[0, 0]
    second = w_out[0, 0]
    tokens, width = x.shape
    part = first.shape[0]
    hidden_width = second.shape[0]
    slots = MOST
    rows = experts * slots
    router_width = table.shape[1]
    chunks = 2 * part // LANES
    half = chunks * slots
    peers = replicas * experts
    group = min(8, experts)
    message_shape = jax.ShapeDtypeStruct((peers, 2 * half, LANES), BF)
    side = lax.axis_index("half")
    index = side.astype(jnp.int32)[None]
    first_other = swapped(first, "half")
    second_other = swapped(second, "half")

    at = np.arange(experts * half, dtype=np.int32)
    owner, chunk_of, slot_of = at // half, at % half // slots, at % slots
    message, normed, gates, place = kernel_call(
        functools.partial(send_kernel, experts, replicas, chunks, slots),
        (
            message_shape,
            jax.ShapeDtypeStruct((tokens, width), BF),
            jax.ShapeDtypeStruct((tokens, router_width), F32),
            jax.ShapeDtypeStruct((tokens, router_width), F32),
        ),
        (x, route_ids, grad_top, gain, table, owner[None], chunk_of[:, None], slot_of[None]),
        [pltpu.VMEM((chunks * tokens, replicas * LANES), BF)],
    )
    arrived = exchange(message, SHARE)

    at = np.arange(group * half, dtype=np.int32)
    into_messages = (at % half // slots * group + at // half) * slots + at % slots
    into_rows = np.zeros_like(at)
    into_rows[into_messages] = at
    step_width = hidden_width // HIDDEN_STEPS
    all_rows = peers * slots
    whole = lambda shape: pl.BlockSpec(shape, lambda i: (0,) * len(shape))
    scalar = pl.BlockSpec(memory_space=pltpu.SMEM)
    by_column = pl.BlockSpec((part, step_width), lambda i: (0, jnp.minimum(i, 2 * HIDDEN_STEPS - 1)))
    by_row = pl.BlockSpec((step_width, part), lambda i: (jnp.maximum(i - 2 * HIDDEN_STEPS, 0), 0))
    partial, expert_rows, grad_rows = kernel_call(
        functools.partial(products_kernel, group, chunks, slots),
        (
            jax.ShapeDtypeStruct((all_rows, 3 * hidden_width), BF),
            jax.ShapeDtypeStruct((all_rows, 2 * part), BF),
            jax.ShapeDtypeStruct((all_rows, 2 * part), BF),
        ),
        (index, arrived, into_rows[:, None], first, first_other, second, second_other),
        grid=(3 * HIDDEN_STEPS,),
        in_specs=[scalar, whole(arrived.shape), whole((at.size, 1)), by_column, by_column, by_row, by_row],
        out_specs=[
            pl.BlockSpec((all_rows, step_width), lambda i: (0, i)),
            whole((all_rows, 2 * part)),
            whole((all_rows, 2 * part)),
        ],
    )
    summands = exchange(partial.reshape(replicas, rows, 3 * hidden_width), "dp")
    at = np.arange(rows, dtype=np.int32)
    acts, worth = kernel_call(
        functools.partial(act_kernel, slots),
        (
            jax.ShapeDtypeStruct(summands.shape, BF),
            jax.ShapeDtypeStruct((experts, LANES), F32),
        ),
        (summands, at[None] // slots, at[:, None] % slots),
    )
    gathered = exchange(acts, "dp").reshape(-1, 3 * hidden_width)
    pre_grad = gathered[:, : 2 * hidden_width]
    hidden_all = gathered[:, 2 * hidden_width :]

    worth = exchange(worth[:, None], "expert")[:, 0, :slots]
    slot_ids = jnp.arange(slots, dtype=F32)
    gate_worth = jnp.sum(
        jnp.where(place[:, :experts, None] == slot_ids, worth[None], 0.0), axis=2
    )
    inner = jnp.sum(gate_worth, axis=1, keepdims=True)
    logit_grad = jnp.pad(gate_worth, ((0, 0), (0, router_width - experts))) - gates * inner
    logit_high, logit_low = two_terms(logit_grad)
    local_router = mm(normed, logit_high, ((0,), (0,))) + mm(normed, logit_low, ((0,), (0,)))
    local_router = local_router.astype(BF).reshape(2, replicas, part, router_width).transpose(1, 0, 2, 3)
    router_part = exchange(local_router.reshape(replicas, 2 * part, router_width), "dp")
    router_part = jnp.sum(router_part.astype(F32), axis=0)

    steps = 2 if replicas % 2 == 0 else 1
    message = kernel_call(
        functools.partial(back_kernel, group, chunks, slots),
        message_shape,
        (index, gathered, into_messages[:, None], first, first_other, second, second_other),
        grid=(steps,),
        in_specs=[
            scalar,
            pl.BlockSpec((all_rows // steps, 3 * hidden_width), lambda i: (i, 0)),
            whole((into_messages.size, 1)),
            whole(first.shape),
            whole(first.shape),
            whole(second.shape),
            whole(second.shape),
        ],
        out_specs=pl.BlockSpec((peers // steps, 2 * half, LANES), lambda i: (i, 0, 0)),
    )
    returned = exchange(message, SHARE)

    rows_own, rows_other = expert_rows[:, :part], expert_rows[:, part:]
    first_other_grad = mm(rows_other, pre_grad, ((0,), (0,)))
    second_other_grad = mm(hidden_all, grad_rows[:, part:], ((0,), (0,)))
    first_sent = swapped(first_other_grad.astype(BF), "half")
    second_sent = swapped(second_other_grad.astype(BF), "half")
    first_own_grad = mm(rows_own, pre_grad, ((0,), (0,)))
    second_own_grad = mm(hidden_all, grad_rows[:, :part], ((0,), (0,)))
    first_grad = (first_own_grad + first_sent.astype(F32)).astype(BF)
    second_grad = (second_own_grad + second_sent.astype(F32)).astype(BF)
    gain_own = jnp.sum(first_own_grad * first.astype(F32), axis=1)
    gain_other = jnp.sum(first_other_grad * first_other.astype(F32), axis=1)
    gain_part = jnp.where(
        side == 0, jnp.stack([gain_own, gain_other]), jnp.stack([gain_other, gain_own])
    )

    owners = 2 * experts
    piece = 2 * part // owners
    gain_rows = jnp.pad(gain_part.reshape(owners, 1, piece), ((0, 0), (0, 7), (0, LANES - piece)))
    owned = jnp.concatenate([router_part.reshape(owners, piece, router_width), gain_rows], axis=1)
    owned = jnp.sum(exchange(owned, OWNERS), axis=0)
    router_own = owned[:piece]
    at = (side * replicas + lax.axis_index("dp")) * part + lax.axis_index("expert") * piece
    table_own = lax.dynamic_slice_in_dim(table, at, piece, axis=0).astype(F32)
    gain_here = lax.dynamic_slice_in_dim(gain[0], at, piece, axis=0)
    gain_sum = (owned[piece, :piece] + jnp.sum(router_own * table_own, axis=1)) / gain_here
    gain_terms = jnp.pad(jnp.stack(three_terms(gain_sum)), ((0, 13), (0, LANES - piece)))
    block = jnp.concatenate([router_own.astype(BF), gain_terms], axis=0)
    joined = exchange(jnp.broadcast_to(block[None], (owners,) + block.shape), OWNERS)
    joined = exchange(jnp.broadcast_to(joined[None], (replicas,) + joined.shape), "dp")
    joined = joined.reshape(replicas, 2, experts, piece + 16, LANES).transpose(1, 0, 2, 3, 4)
    router_total = joined[:, :, :, :piece].reshape(width, router_width)
    gain_total = jnp.sum(joined[:, :, :, piece : piece + 3, :piece].astype(F32), axis=3).reshape(width)

    layer_out, in_grad = kernel_call(
        functools.partial(combine_kernel, experts, replicas, chunks, slots),
        (
            jax.ShapeDtypeStruct((tokens, width), BF),
            jax.ShapeDtypeStruct((tokens, width), BF),
        ),
        (
            returned, x, grad_top, gain, table, gates, place, logit_grad,
            owner[None], chunk_of[None], slot_of[None],
        ),
        [
            pltpu.VMEM((experts * half, replicas * LANES), BF),
            pltpu.VMEM((tokens, width), F32),
        ],
    )
    handoff = swapped(layer_out, "section")
    handback = swapped(in_grad, "section")
    return (
        handoff[None],
        handback[None],
        first_grad[None, None],
        second_grad[None, None],
        router_total[None],
        gain_total[None],
    )


def solution(mesh):
    sizes = mesh.shape
    halves = (sizes["section"], sizes["expert"], 2, sizes["dp"] // 2)
    split = Mesh(mesh.devices.reshape(halves), ("section", "expert", "half", "dp"))
    blocks = ("half", "dp")
    tokens = ("expert",) + blocks
    return jax.shard_map(
        shards,
        mesh=split,
        in_specs=(
            P("section", tokens, None),
            P("section", tokens, None),
            P("section", tokens, None),
            P("section", None),
            P("section", None, None),
            P("section", "expert", blocks, None),
            P("section", "expert", None, blocks),
        ),
        out_specs=(
            P("section", tokens, None),
            P("section", tokens, None),
            P("section", "expert", blocks, None),
            P("section", "expert", None, blocks),
            P("section", None, None),
            P("section", None),
        ),
        check_vma=False,
    )
```

```python
import functools

import jax
import jax.numpy as jnp
import numpy as np
from jax import lax
from jax.experimental import pallas as pl
from jax.experimental.pallas import tpu as pltpu
from jax.sharding import Mesh
from jax.sharding import PartitionSpec as P

MOST = 10
LANES = 128
BF = jnp.bfloat16
F32 = jnp.float32
SHARE = ("dp", "expert")
OWNERS = ("half", "expert")
INTERPRET = False
HIDDEN_STEPS = 3


def exchange(blocks, axes):
    return lax.all_to_all(blocks, axes, split_axis=0, concat_axis=0, tiled=True)


def mm(left, right, contract=((1,), (0,))):
    return lax.dot_general(left, right, (contract, ((), ())), preferred_element_type=F32)


def two_terms(values):
    high = values.astype(BF)
    return high, (values - high.astype(F32)).astype(BF)


def three_terms(values):
    high = values.astype(BF)
    return (high,) + two_terms(values - high.astype(F32))


def kernel_call(body, outs, args, scratch=(), **grid):
    return pl.pallas_call(
        body,
        out_shape=outs,
        scratch_shapes=scratch,
        compiler_params=pltpu.CompilerParams(vmem_limit_bytes=52 * 2**20),
        interpret=INTERPRET,
        **grid,
    )(*args)


def iota(shape, dimension):
    return lax.broadcasted_iota(jnp.int32, shape, dimension)


def spread(values, owner):
    pick = (iota((values[0].shape[1], owner.shape[1]), 0) == owner).astype(BF)
    total = mm(values[0], pick)
    for term in values[1:]:
        total = total + mm(term, pick)
    return total


def feature(replicas, width, c, j):
    part = width // (2 * replicas)
    block, inner = divmod(c * LANES, part)
    return (block * replicas + j) * part + inner


def picks_of(chunks, hits, chunk_of):
    rows = jnp.where(hits, 1.0, 0.0).T
    return jnp.concatenate(
        [jnp.where(chunk_of == c, rows, 0.0).astype(BF) for c in range(chunks)], axis=1
    )


def stacked(chunks, replicas, source, stack):
    tokens, width = source.shape
    for c in range(chunks):
        for j in range(replicas):
            at = feature(replicas, width, c, j)
            stack[c * tokens : (c + 1) * tokens, j * LANES : (j + 1) * LANES] = source[:, at : at + LANES]
    return stack[...]


def write_messages(experts, replicas, half, sent, message):
    for j in range(replicas):
        for e in range(experts):
            message[j * experts + e] = sent[e * half : (e + 1) * half, j * LANES : (j + 1) * LANES]


def slot_hits(place, owner, slot_of):
    return spread((place[...].astype(BF),), owner[...]) == slot_of[...].astype(F32)


def named_by(ids, shape):
    columns = iota(shape, 1)
    named = columns == ids[:, 0:1]
    for k in range(1, ids.shape[1]):
        named = named | (columns == ids[:, k : k + 1])
    return named


def send_kernel(experts, replicas, chunks, slots, x, ids, gain, owner, chunk_of, slot_of,
                message, normed, place, stack):
    tokens, width = x.shape
    xw = x[...].astype(F32)
    inv_rms = lax.rsqrt(jnp.mean(xw * xw, axis=1, keepdims=True) + 1e-06)
    normed[...] = (xw * inv_rms * gain[...]).astype(BF)
    named = named_by(ids, place.shape)
    earlier = (iota((tokens, tokens), 1) < iota((tokens, tokens), 0)).astype(BF)
    rank = mm(earlier, named.astype(BF))
    place[...] = jnp.where(named & (iota(place.shape, 1) < experts), rank, -1.0)
    pick = picks_of(chunks, slot_hits(place, owner, slot_of), chunk_of[...])
    sent = mm(pick, stacked(chunks, replicas, normed, stack)).astype(BF)
    write_messages(experts, replicas, chunks * slots, sent, message)


def send_grad_kernel(experts, replicas, chunks, slots, normed, ids, grad, table, place, owner, chunk_of, slot_of,
                     message, gates_out, stack):
    logits = mm(normed[...], table[...])
    powers = jnp.where(named_by(ids, logits.shape), jnp.exp(logits), 0.0)
    gates = powers / jnp.sum(powers, axis=1, keepdims=True)
    gates_out[...] = gates
    hits = slot_hits(place, owner, slot_of)
    weight = jnp.where(hits, spread(three_terms(gates), owner[...]), 0.0)
    slot_gate = jnp.sum(weight.T, axis=1, keepdims=True)
    pick = picks_of(chunks, hits, chunk_of[...])
    sent = (mm(pick, stacked(chunks, replicas, grad, stack)) * slot_gate).astype(BF)
    write_messages(experts, replicas, chunks * slots, sent, message)


def products_kernel(group, chunks, slots, contract, index, arrived, order, weight, weight_other, partial, rows_out):
    half = chunks * slots
    size = group * half
    block = group * slots
    own_chunks = chunks // 2
    part = own_chunks * LANES

    @pl.when(pl.program_id(0) == 0)
    def _():
        lower = index[0] == 0
        pick = (order[...] == iota((size, size), 1)).astype(BF)
        for pair in range(arrived.shape[0] // group // 2):
            lanes = [
                arrived[(2 * pair + w) * group : (2 * pair + w + 1) * group].reshape(size, LANES)
                for w in range(2)
            ]
            picked = mm(pick, jnp.concatenate(lanes, axis=1)).astype(BF)
            for c in range(own_chunks):
                low = picked[c * block : (c + 1) * block]
                high = picked[(own_chunks + c) * block : (own_chunks + c + 1) * block]
                own = jnp.where(lower, low, high)
                other = jnp.where(lower, high, low)
                for w in range(2):
                    rows = slice((2 * pair + w) * block, (2 * pair + w + 1) * block)
                    lanes = slice(w * LANES, (w + 1) * LANES)
                    rows_out[rows, c * LANES : (c + 1) * LANES] = own[:, lanes]
                    rows_out[rows, part + c * LANES : part + (c + 1) * LANES] = other[:, lanes]

    partial[...] = (
        mm(rows_out[:, :part], weight[...], contract) + mm(rows_out[:, part:], weight_other[...], contract)
    ).astype(BF)


def act_kernel(slots, arrived, pre_act, hidden, sender_of, slot_of, pre_grad, worth):
    replicas, rows, hidden_width = arrived.shape
    hidden_grad = arrived[0].astype(F32)
    for j in range(1, replicas):
        hidden_grad = hidden_grad + arrived[j].astype(F32)
    gate_pre = pre_act[:, :hidden_width].astype(F32)
    up = pre_act[:, hidden_width:].astype(F32)
    sigmoid = 1.0 / (1.0 + jnp.exp(-gate_pre))
    silu = gate_pre * sigmoid
    slope = sigmoid * (1.0 + gate_pre * (1.0 - sigmoid))
    pre_grad[:, :hidden_width] = (hidden_grad * up * slope).astype(BF)
    pre_grad[:, hidden_width:] = (hidden_grad * silu).astype(BF)
    each = jnp.sum(hidden_grad * hidden[...].astype(F32), axis=1, keepdims=True)
    laid = jnp.where(slot_of[...] == iota((rows, LANES), 1), each, 0.0)
    pick = (sender_of[...] == iota((worth.shape[0], rows), 0)).astype(BF)
    terms = three_terms(laid)
    worth[...] = mm(pick, terms[0]) + mm(pick, terms[1]) + mm(pick, terms[2])


def return_rows(group, chunks, slots, lower, order, own, other, message):
    block = group * slots
    half = chunks * slots
    size = group * half
    own_chunks = chunks // 2
    own, other = own.astype(BF), other.astype(BF)
    sides = jnp.where(lower, own, other), jnp.where(lower, other, own)
    pick = (order[...] == iota((size, size), 1)).astype(BF)

    def column(at):
        return jnp.concatenate(
            [
                side[at : at + block, c * LANES : (c + 1) * LANES]
                for side in sides
                for c in range(own_chunks)
            ],
            axis=0,
        )

    for pair in range(own.shape[0] // block // 2):
        lanes = [column((2 * pair + w) * block) for w in range(2)]
        picked = mm(pick, jnp.concatenate(lanes, axis=1)).astype(BF)
        for w in range(2):
            message[(2 * pair + w) * group : (2 * pair + w + 1) * group] = picked[
                :, w * LANES : (w + 1) * LANES
            ].reshape(group, half, LANES)


def out_kernel(group, chunks, slots, index, hidden, order, second, second_other, message):
    own = mm(hidden[...], second[...])
    other = mm(hidden[...], second_other[...])
    return_rows(group, chunks, slots, index[0] == 0, order, own, other, message)


def back_kernel(group, chunks, slots, index, pre_grad, order, first, first_other, rows, message, gain):
    own = mm(pre_grad[...], first[...], ((1,), (1,)))
    other = mm(pre_grad[...], first_other[...], ((1,), (1,)))
    return_rows(group, chunks, slots, index[0] == 0, order, own, other, message)

    @pl.when(pl.program_id(0) == 0)
    def _():
        gain[...] = jnp.zeros_like(gain)

    part = own.shape[1]
    gain[:, :part] += jnp.sum(own * rows[:, :part].astype(F32), axis=0, keepdims=True)
    gain[:, part:] += jnp.sum(other * rows[:, part:].astype(F32), axis=0, keepdims=True)


def join(experts, replicas, returned, joined):
    half = returned.shape[1]
    for j in range(replicas):
        block = returned[j * experts : (j + 1) * experts]
        joined[:, j * LANES : (j + 1) * LANES] = block.reshape(experts * half, LANES)
    return joined[...]


def to_tokens(chunks, values, chunk_of):
    return jnp.concatenate(
        [jnp.where(chunk_of == c, values, 0.0).astype(BF) for c in range(chunks)], axis=0
    )


def layer_kernel(experts, replicas, chunks, returned, x, gates, place, owner, chunk_of, slot_of, layer_out, joined):
    tokens, width = x.shape
    hits = slot_hits(place, owner, slot_of)
    source = join(experts, replicas, returned, joined)
    mixed = 0.0
    for term in two_terms(gates[...]):
        weight = jnp.where(hits, spread((term,), owner[...]), 0.0)
        mixed = mixed + mm(to_tokens(chunks, weight, chunk_of[...]), source)
    for c in range(chunks):
        for j in range(replicas):
            at = feature(replicas, width, c, j)
            at = slice(at, at + LANES)
            here = mixed[c * tokens : (c + 1) * tokens, j * LANES : (j + 1) * LANES]
            layer_out[:, at] = (x[:, at].astype(F32) + here).astype(BF)


def in_grad_kernel(experts, replicas, chunks, returned, x, grad, gain, table, place, logit_grad,
                   owner, chunk_of, slot_of, in_grad, joined, normed_grad):
    tokens, width = x.shape
    ones = jnp.where(slot_hits(place, owner, slot_of), 1.0, 0.0)
    back = mm(to_tokens(chunks, ones, chunk_of[...]), join(experts, replicas, returned, joined))
    high, low = two_terms(logit_grad[...])
    by_logits = mm(high, table[...], ((1,), (1,))) + mm(low, table[...], ((1,), (1,)))
    for c in range(chunks):
        for j in range(replicas):
            at = feature(replicas, width, c, j)
            at = slice(at, at + LANES)
            here = back[c * tokens : (c + 1) * tokens, j * LANES : (j + 1) * LANES]
            normed_grad[:, at] = here + by_logits[:, at]
    xw = x[...].astype(F32)
    inv_rms = lax.rsqrt(jnp.mean(xw * xw, axis=1, keepdims=True) + 1e-06)
    weighted = gain[...] * normed_grad[...]
    mean = jnp.mean(xw * weighted, axis=1, keepdims=True)
    in_grad[...] = (
        grad[...].astype(F32) + inv_rms * weighted - xw * (inv_rms * inv_rms * inv_rms * mean)
    ).astype(BF)


def after(value, *earlier):
    return lax.optimization_barrier((value,) + earlier)[0]


def swapped(block, axis):
    return lax.ppermute(block, axis, [(0, 1), (1, 0)])


def shards(section_input, routing, out_grad, norm_gain, router, w_in, w_out):
    experts = lax.axis_size("expert")
    replicas = lax.axis_size("dp")
    x = section_input[0]
    route_ids = routing[0]
    grad_top = out_grad[0]
    gain = norm_gain[0][None, :]
    table = router[0]
    first = w_in[0, 0]
    second = w_out[0, 0]
    tokens, width = x.shape
    part = first.shape[0]
    hidden_width = second.shape[0]
    slots = MOST
    rows = experts * slots
    router_width = table.shape[1]
    chunks = 2 * part // LANES
    half = chunks * slots
    peers = replicas * experts
    group = min(8, experts)
    message_shape = jax.ShapeDtypeStruct((peers, half, LANES), BF)
    side = lax.axis_index("half")
    index = side.astype(jnp.int32)[None]
    first_other = swapped(first, "half")
    second_other = swapped(second, "half")

    at = np.arange(experts * half, dtype=np.int32)
    owner, chunk_of, slot_of = (at // half)[None], at % half // slots, (at % slots)[None]
    sizes = (experts, replicas, chunks, slots)
    token_scratch = [pltpu.VMEM((chunks * tokens, replicas * LANES), BF)]
    message, normed, place = kernel_call(
        functools.partial(send_kernel, *sizes),
        (
            message_shape,
            jax.ShapeDtypeStruct((tokens, width), BF),
            jax.ShapeDtypeStruct((tokens, router_width), F32),
        ),
        (x, route_ids, gain, owner, chunk_of[:, None], slot_of),
        token_scratch,
    )
    arrived = exchange(message, SHARE)

    message, gates = kernel_call(
        functools.partial(send_grad_kernel, *sizes),
        (message_shape, jax.ShapeDtypeStruct((tokens, router_width), F32)),
        (normed, route_ids, grad_top, table, place, owner, chunk_of[:, None], slot_of),
        token_scratch,
    )
    message, arrived = lax.optimization_barrier((message, arrived))
    arrived_grad = exchange(message, SHARE)

    at = np.arange(group * half, dtype=np.int32)
    into_messages = (at % half // slots * group + at // half) * slots + at % slots
    into_rows = np.zeros_like(at)
    into_rows[into_messages] = at
    step_width = hidden_width // HIDDEN_STEPS
    all_rows = peers * slots
    whole = lambda shape: pl.BlockSpec(shape, lambda i: (0,) * len(shape))
    scalar = pl.BlockSpec(memory_space=pltpu.SMEM)

    def products(arrived, weights, contract, steps, weight_spec):
        return kernel_call(
            functools.partial(products_kernel, group, chunks, slots, contract),
            (
                jax.ShapeDtypeStruct((all_rows, steps * step_width), BF),
                jax.ShapeDtypeStruct((all_rows, 2 * part), BF),
            ),
            (index, arrived, into_rows[:, None]) + weights,
            grid=(steps,),
            in_specs=[scalar, whole(arrived.shape), whole((at.size, 1)), weight_spec, weight_spec],
            out_specs=[pl.BlockSpec((all_rows, step_width), lambda i: (0, i)), whole((all_rows, 2 * part))],
        )

    partial, expert_rows = products(
        arrived,
        (first, first_other),
        ((1,), (0,)),
        2 * HIDDEN_STEPS,
        pl.BlockSpec((part, step_width), lambda i: (0, i)),
    )
    pre_act = lax.psum_scatter(partial, "dp", scatter_dimension=0, tiled=True)
    gate_pre = pre_act[:, :hidden_width].astype(F32)
    up = pre_act[:, hidden_width:].astype(F32)
    hidden = (gate_pre / (1.0 + jnp.exp(-gate_pre)) * up).astype(BF)
    hidden_all = lax.all_gather(hidden, "dp", axis=0, tiled=True)

    partial, grad_rows = products(
        arrived_grad,
        (second, second_other),
        ((1,), (1,)),
        HIDDEN_STEPS,
        pl.BlockSpec((step_width, part), lambda i: (i, 0)),
    )
    summands = exchange(partial.reshape(replicas, rows, hidden_width), "dp")
    at = np.arange(rows, dtype=np.int32)
    pre_grad, worth = kernel_call(
        functools.partial(act_kernel, slots),
        (
            jax.ShapeDtypeStruct((rows, 2 * hidden_width), BF),
            jax.ShapeDtypeStruct((experts, LANES), F32),
        ),
        (summands, pre_act, hidden, at[None] // slots, at[:, None] % slots),
    )
    pre_grad_all = lax.all_gather(pre_grad, "dp", axis=0, tiled=True)

    worth = exchange(worth[:, None], "expert")[:, 0, :slots]
    slot_ids = jnp.arange(slots, dtype=F32)
    gate_worth = jnp.sum(
        jnp.where(place[:, :experts, None] == slot_ids, worth[None], 0.0), axis=2
    )
    inner = jnp.sum(gate_worth, axis=1, keepdims=True)
    logit_grad = jnp.pad(gate_worth, ((0, 0), (0, router_width - experts))) - gates * inner
    logit_high, logit_low = two_terms(logit_grad)
    local_router = mm(normed, logit_high, ((0,), (0,))) + mm(normed, logit_low, ((0,), (0,)))
    local_router = local_router.astype(BF).reshape(2, replicas, part, router_width).transpose(1, 0, 2, 3)
    router_part = lax.psum_scatter(
        local_router.reshape(-1, router_width), "dp", scatter_dimension=0, tiled=True
    ).astype(F32)

    steps = 2 if all_rows // 2 % (2 * group * slots) == 0 else 1

    def by_rows(width):
        return pl.BlockSpec((all_rows // steps, width), lambda i: (i, 0))

    messages = pl.BlockSpec((peers // steps, half, LANES), lambda i: (i, 0, 0))
    order = into_messages[:, None]
    message = kernel_call(
        functools.partial(out_kernel, group, chunks, slots),
        message_shape,
        (index, hidden_all, order, second, second_other),
        grid=(steps,),
        in_specs=[scalar, by_rows(hidden_width), whole(order.shape), whole(second.shape), whole(second.shape)],
        out_specs=messages,
    )
    returned = exchange(after(message, worth), SHARE)
    second_other_grad = mm(hidden_all, grad_rows[:, part:], ((0,), (0,)))
    second_own_grad = mm(hidden_all, grad_rows[:, :part], ((0,), (0,)))
    second_sent = swapped(second_other_grad.astype(BF), "half")
    second_grad = (second_own_grad + second_sent.astype(F32)).astype(BF)

    message, gain_part = kernel_call(
        functools.partial(back_kernel, group, chunks, slots),
        (message_shape, jax.ShapeDtypeStruct((1, 2 * part), F32)),
        (index, pre_grad_all, order, first, first_other, expert_rows),
        grid=(steps,),
        in_specs=[
            scalar,
            by_rows(2 * hidden_width),
            whole(order.shape),
            whole(first.shape),
            whole(first.shape),
            by_rows(2 * part),
        ],
        out_specs=[messages, whole((1, 2 * part))],
    )
    gain_part = gain_part.reshape(2, part)
    gain_part = jnp.where(side == 0, gain_part, gain_part[::-1])

    owners = 2 * experts
    piece = 2 * part // owners
    gain_rows = jnp.pad(gain_part.reshape(owners, 1, piece), ((0, 0), (0, 7), (0, LANES - piece)))
    owned = jnp.concatenate([router_part.reshape(owners, piece, router_width), gain_rows], axis=1)
    owned = jnp.sum(exchange(after(owned, returned), OWNERS), axis=0)
    router_own = owned[:piece]
    at = (side * replicas + lax.axis_index("dp")) * part + lax.axis_index("expert") * piece
    table_own = lax.dynamic_slice_in_dim(table, at, piece, axis=0).astype(F32)
    gain_here = lax.dynamic_slice_in_dim(gain[0], at, piece, axis=0)
    gain_sum = (owned[piece, :piece] + jnp.sum(router_own * table_own, axis=1)) / gain_here
    gain_terms = jnp.pad(jnp.stack(three_terms(gain_sum)), ((0, 13), (0, LANES - piece)))
    block = jnp.concatenate([router_own.astype(BF), gain_terms], axis=0)
    joined = exchange(jnp.broadcast_to(block[None], (owners,) + block.shape), OWNERS)
    returned_back = exchange(after(message, joined), SHARE)
    joined = lax.all_gather(joined.reshape(-1, LANES), "dp", axis=0, tiled=True)
    joined = joined.reshape(replicas, 2, experts, piece + 16, LANES).transpose(1, 0, 2, 3, 4)
    router_total = joined[:, :, :, :piece].reshape(width, router_width)
    gain_total = jnp.sum(joined[:, :, :, piece : piece + 3, :piece].astype(F32), axis=3).reshape(width)

    first_other_grad = mm(expert_rows[:, part:], pre_grad_all, ((0,), (0,)))
    first_own_grad = mm(expert_rows[:, :part], pre_grad_all, ((0,), (0,)))
    first_sent = swapped(first_other_grad.astype(BF), "half")
    first_grad = (first_own_grad + first_sent.astype(F32)).astype(BF)

    token_shape = jax.ShapeDtypeStruct((tokens, width), BF)
    joined_scratch = pltpu.VMEM((experts * half, replicas * LANES), BF)
    layer_out = kernel_call(
        functools.partial(layer_kernel, experts, replicas, chunks),
        token_shape,
        (returned, x, gates, place, owner, chunk_of[None], slot_of),
        [joined_scratch],
    )
    in_grad = kernel_call(
        functools.partial(in_grad_kernel, experts, replicas, chunks),
        token_shape,
        (returned_back, x, grad_top, gain, table, place, logit_grad, owner, chunk_of[None], slot_of),
        [joined_scratch, pltpu.VMEM((tokens, width), F32)],
    )
    handoff = swapped(layer_out, "section")
    handback = swapped(in_grad, "section")
    return (
        handoff[None],
        handback[None],
        first_grad[None, None],
        second_grad[None, None],
        router_total[None],
        gain_total[None],
    )


def solution(mesh):
    sizes = mesh.shape
    halves = (sizes["section"], sizes["expert"], 2, sizes["dp"] // 2)
    split = Mesh(mesh.devices.reshape(halves), ("section", "expert", "half", "dp"))
    blocks = ("half", "dp")
    tokens = ("expert",) + blocks
    return jax.shard_map(
        shards,
        mesh=split,
        in_specs=(
            P("section", tokens, None),
            P("section", tokens, None),
            P("section", tokens, None),
            P("section", None),
            P("section", None, None),
            P("section", "expert", blocks, None),
            P("section", "expert", None, blocks),
        ),
        out_specs=(
            P("section", tokens, None),
            P("section", tokens, None),
            P("section", "expert", blocks, None),
            P("section", "expert", None, blocks),
            P("section", None, None),
            P("section", None),
        ),
        check_vma=False,
    )
```

```python
import functools

import jax
import jax.numpy as jnp
import numpy as np
from jax import lax
from jax.experimental import pallas as pl
from jax.experimental.pallas import tpu as pltpu
from jax.sharding import Mesh
from jax.sharding import PartitionSpec as P

MOST = 10
LANES = 128
BF = jnp.bfloat16
F32 = jnp.float32
SHARE = ("dp", "expert")
OWNERS = ("half", "expert")
INTERPRET = False
HIDDEN_STEPS = 3


def exchange(blocks, axes):
    return lax.all_to_all(blocks, axes, split_axis=0, concat_axis=0, tiled=True)


def mm(left, right, contract=((1,), (0,))):
    return lax.dot_general(left, right, (contract, ((), ())), preferred_element_type=F32)


def two_terms(values):
    high = values.astype(BF)
    return high, (values - high.astype(F32)).astype(BF)


def three_terms(values):
    high = values.astype(BF)
    return (high,) + two_terms(values - high.astype(F32))


def kernel_call(body, outs, args, scratch=(), **grid):
    return pl.pallas_call(
        body,
        out_shape=outs,
        scratch_shapes=scratch,
        compiler_params=pltpu.CompilerParams(vmem_limit_bytes=52 * 2**20),
        interpret=INTERPRET,
        **grid,
    )(*args)


def iota(shape, dimension):
    return lax.broadcasted_iota(jnp.int32, shape, dimension)


def spread(values, owner):
    pick = (iota((values[0].shape[1], owner.shape[1]), 0) == owner).astype(BF)
    total = mm(values[0], pick)
    for term in values[1:]:
        total = total + mm(term, pick)
    return total


def feature(replicas, width, c, j):
    part = width // (2 * replicas)
    block, inner = divmod(c * LANES, part)
    return (block * replicas + j) * part + inner


def picks_of(chunks, hits, chunk_of):
    rows = jnp.where(hits, 1.0, 0.0).T
    return jnp.concatenate(
        [jnp.where(chunk_of == c, rows, 0.0).astype(BF) for c in range(chunks)], axis=1
    )


def stacked(chunks, replicas, source, stack):
    tokens, width = source.shape
    for c in range(chunks):
        for j in range(replicas):
            at = feature(replicas, width, c, j)
            stack[c * tokens : (c + 1) * tokens, j * LANES : (j + 1) * LANES] = source[:, at : at + LANES]
    return stack[...]


def write_messages(experts, replicas, half, sent, message):
    for j in range(replicas):
        for e in range(experts):
            message[j * experts + e] = sent[e * half : (e + 1) * half, j * LANES : (j + 1) * LANES]


def slot_hits(place, owner, slot_of):
    return spread((place[...].astype(BF),), owner[...]) == slot_of[...].astype(F32)


def named_by(ids, shape):
    columns = iota(shape, 1)
    named = columns == ids[:, 0:1]
    for k in range(1, ids.shape[1]):
        named = named | (columns == ids[:, k : k + 1])
    return named


def send_kernel(experts, replicas, chunks, slots, x, ids, gain, owner, chunk_of, slot_of,
                message, normed, place, stack):
    tokens, width = x.shape
    xw = x[...].astype(F32)
    inv_rms = lax.rsqrt(jnp.mean(xw * xw, axis=1, keepdims=True) + 1e-06)
    normed[...] = (xw * inv_rms * gain[...]).astype(BF)
    named = named_by(ids, place.shape)
    earlier = (iota((tokens, tokens), 1) < iota((tokens, tokens), 0)).astype(BF)
    rank = mm(earlier, named.astype(BF))
    place[...] = jnp.where(named & (iota(place.shape, 1) < experts), rank, -1.0)
    pick = picks_of(chunks, slot_hits(place, owner, slot_of), chunk_of[...])
    sent = mm(pick, stacked(chunks, replicas, normed, stack)).astype(BF)
    write_messages(experts, replicas, chunks * slots, sent, message)


def send_grad_kernel(experts, replicas, chunks, slots, normed, ids, grad, table, place, owner, chunk_of, slot_of,
                     message, gates_out, stack):
    logits = mm(normed[...], table[...])
    powers = jnp.where(named_by(ids, logits.shape), jnp.exp(logits), 0.0)
    gates = powers / jnp.sum(powers, axis=1, keepdims=True)
    gates_out[...] = gates
    hits = slot_hits(place, owner, slot_of)
    weight = jnp.where(hits, spread(three_terms(gates), owner[...]), 0.0)
    slot_gate = jnp.sum(weight.T, axis=1, keepdims=True)
    pick = picks_of(chunks, hits, chunk_of[...])
    sent = (mm(pick, stacked(chunks, replicas, grad, stack)) * slot_gate).astype(BF)
    write_messages(experts, replicas, chunks * slots, sent, message)


def products_kernel(group, chunks, slots, side, index, arrived, order, *refs):
    weights, partial, rows_out = refs[:-2], refs[-2], refs[-1]
    half = chunks * slots
    size = group * half
    block = group * slots
    own_chunks = chunks // 2
    part = own_chunks * LANES

    @pl.when(pl.program_id(0) == 0)
    def _():
        lower = index[0] == 0
        pick = (order[...] == iota((size, size), 1)).astype(BF)
        for pair in range(arrived.shape[0] // group // 2):
            lanes = [
                arrived[(2 * pair + w) * group : (2 * pair + w + 1) * group].reshape(size, LANES)
                for w in range(2)
            ]
            picked = mm(pick, jnp.concatenate(lanes, axis=1)).astype(BF)
            for c in range(own_chunks):
                low = picked[c * block : (c + 1) * block]
                high = picked[(own_chunks + c) * block : (own_chunks + c + 1) * block]
                own = jnp.where(lower, low, high)
                other = jnp.where(lower, high, low)
                for w in range(2):
                    rows = slice((2 * pair + w) * block, (2 * pair + w + 1) * block)
                    lanes = slice(w * LANES, (w + 1) * LANES)
                    rows_out[rows, c * LANES : (c + 1) * LANES] = own[:, lanes]
                    rows_out[rows, part + c * LANES : part + (c + 1) * LANES] = other[:, lanes]

    total, at = 0.0, 0
    for weight in weights:
        end = at + weight.shape[side]
        total = total + mm(rows_out[:, at:end], weight[...], ((1,), (side,)))
        at = end
    partial[...] = total.astype(BF)


def act_kernel(slots, arrived, pre_act, hidden, sender_of, slot_of, pre_grad, worth):
    replicas, rows, hidden_width = arrived.shape
    hidden_grad = arrived[0].astype(F32)
    for j in range(1, replicas):
        hidden_grad = hidden_grad + arrived[j].astype(F32)
    gate_pre = pre_act[:, :hidden_width].astype(F32)
    up = pre_act[:, hidden_width:].astype(F32)
    sigmoid = 1.0 / (1.0 + jnp.exp(-gate_pre))
    silu = gate_pre * sigmoid
    slope = sigmoid * (1.0 + gate_pre * (1.0 - sigmoid))
    pre_grad[:, :hidden_width] = (hidden_grad * up * slope).astype(BF)
    pre_grad[:, hidden_width:] = (hidden_grad * silu).astype(BF)
    each = jnp.sum(hidden_grad * hidden[...].astype(F32), axis=1, keepdims=True)
    laid = jnp.where(slot_of[...] == iota((rows, LANES), 1), each, 0.0)
    pick = (sender_of[...] == iota((worth.shape[0], rows), 0)).astype(BF)
    terms = three_terms(laid)
    worth[...] = mm(pick, terms[0]) + mm(pick, terms[1]) + mm(pick, terms[2])


def return_rows(group, chunks, slots, lower, order, own, other, message, first_row=0):
    block = group * slots
    half = chunks * slots
    size = group * half
    own_chunks = chunks // 2
    own, other = own.astype(BF), other.astype(BF)
    sides = jnp.where(lower, own, other), jnp.where(lower, other, own)
    pick = (order[...] == iota((size, size), 1)).astype(BF)

    def column(at):
        return jnp.concatenate(
            [
                side[at : at + block, c * LANES : (c + 1) * LANES]
                for side in sides
                for c in range(own_chunks)
            ],
            axis=0,
        )

    for pair in range(own.shape[0] // block // 2):
        lanes = [column((2 * pair + w) * block) for w in range(2)]
        picked = mm(pick, jnp.concatenate(lanes, axis=1)).astype(BF)
        for w in range(2):
            to = slice((2 * pair + w) * group, (2 * pair + w + 1) * group)
            message[to, first_row : first_row + half] = picked[:, w * LANES : (w + 1) * LANES].reshape(
                group, half, LANES
            )


def out_kernel(group, chunks, slots, index, hidden, order, second, second_other, message):
    own = mm(hidden[...], second[...])
    other = mm(hidden[...], second_other[...])
    return_rows(group, chunks, slots, index[0] == 0, order, own, other, message)


def back_kernel(group, chunks, slots, index, pre_grad, order, first, first_early, first_late, rows, outs,
                message, gain):
    own = mm(pre_grad[...], first[...], ((1,), (1,)))
    other = jnp.concatenate(
        [mm(pre_grad[...], weight[...], ((1,), (1,))) for weight in (first_early, first_late)], axis=1
    )
    half = chunks * slots
    message[:, :half] = outs[...]
    return_rows(group, chunks, slots, index[0] == 0, order, own, other, message, half)

    @pl.when(pl.program_id(0) == 0)
    def _():
        gain[...] = jnp.zeros_like(gain)

    part = own.shape[1]
    gain[:, :part] += jnp.sum(own * rows[:, :part].astype(F32), axis=0, keepdims=True)
    gain[:, part:] += jnp.sum(other * rows[:, part:].astype(F32), axis=0, keepdims=True)


def join(experts, replicas, kind, returned, joined):
    half = returned.shape[1] // 2
    for j in range(replicas):
        block = returned[j * experts : (j + 1) * experts, kind * half : (kind + 1) * half]
        joined[:, j * LANES : (j + 1) * LANES] = block.reshape(experts * half, LANES)
    return joined[...]


def to_tokens(chunks, values, chunk_of):
    return jnp.concatenate(
        [jnp.where(chunk_of == c, values, 0.0).astype(BF) for c in range(chunks)], axis=0
    )


def layer_kernel(experts, replicas, chunks, returned, x, gates, place, owner, chunk_of, slot_of, layer_out, joined):
    tokens, width = x.shape
    hits = slot_hits(place, owner, slot_of)
    source = join(experts, replicas, 0, returned, joined)
    mixed = 0.0
    for term in two_terms(gates[...]):
        weight = jnp.where(hits, spread((term,), owner[...]), 0.0)
        mixed = mixed + mm(to_tokens(chunks, weight, chunk_of[...]), source)
    for c in range(chunks):
        for j in range(replicas):
            at = feature(replicas, width, c, j)
            at = slice(at, at + LANES)
            here = mixed[c * tokens : (c + 1) * tokens, j * LANES : (j + 1) * LANES]
            layer_out[:, at] = (x[:, at].astype(F32) + here).astype(BF)


def in_grad_kernel(experts, replicas, chunks, returned, x, grad, gain, table, place, logit_grad,
                   owner, chunk_of, slot_of, in_grad, joined, normed_grad):
    tokens, width = x.shape
    ones = jnp.where(slot_hits(place, owner, slot_of), 1.0, 0.0)
    back = mm(to_tokens(chunks, ones, chunk_of[...]), join(experts, replicas, 1, returned, joined))
    high, low = two_terms(logit_grad[...])
    by_logits = mm(high, table[...], ((1,), (1,))) + mm(low, table[...], ((1,), (1,)))
    for c in range(chunks):
        for j in range(replicas):
            at = feature(replicas, width, c, j)
            at = slice(at, at + LANES)
            here = back[c * tokens : (c + 1) * tokens, j * LANES : (j + 1) * LANES]
            normed_grad[:, at] = here + by_logits[:, at]
    xw = x[...].astype(F32)
    inv_rms = lax.rsqrt(jnp.mean(xw * xw, axis=1, keepdims=True) + 1e-06)
    weighted = gain[...] * normed_grad[...]
    mean = jnp.mean(xw * weighted, axis=1, keepdims=True)
    in_grad[...] = (
        grad[...].astype(F32) + inv_rms * weighted - xw * (inv_rms * inv_rms * inv_rms * mean)
    ).astype(BF)


def after(value, *earlier):
    return lax.optimization_barrier((value,) + earlier)[0]


def swapped(block, axis):
    return lax.ppermute(block, axis, [(0, 1), (1, 0)])


def shards(section_input, routing, out_grad, norm_gain, router, w_in, w_out):
    experts = lax.axis_size("expert")
    replicas = lax.axis_size("dp")
    x = section_input[0]
    route_ids = routing[0]
    grad_top = out_grad[0]
    gain = norm_gain[0][None, :]
    table = router[0]
    first = w_in[0, 0]
    second = w_out[0, 0]
    tokens, width = x.shape
    part = first.shape[0]
    hidden_width = second.shape[0]
    slots = MOST
    rows = experts * slots
    router_width = table.shape[1]
    chunks = 2 * part // LANES
    half = chunks * slots
    peers = replicas * experts
    group = min(8, experts)
    message_shape = jax.ShapeDtypeStruct((peers, half, LANES), BF)
    side = lax.axis_index("half")
    index = side.astype(jnp.int32)[None]
    early = part // 4
    first_early = swapped(first[:early], "half")
    first_late = swapped(first[early:], "half")
    second_other = swapped(second, "half")

    at = np.arange(experts * half, dtype=np.int32)
    owner, chunk_of, slot_of = (at // half)[None], at % half // slots, (at % slots)[None]
    sizes = (experts, replicas, chunks, slots)
    token_scratch = [pltpu.VMEM((chunks * tokens, replicas * LANES), BF)]
    message, normed, place = kernel_call(
        functools.partial(send_kernel, *sizes),
        (
            message_shape,
            jax.ShapeDtypeStruct((tokens, width), BF),
            jax.ShapeDtypeStruct((tokens, router_width), F32),
        ),
        (x, route_ids, gain, owner, chunk_of[:, None], slot_of),
        token_scratch,
    )
    arrived = exchange(after(message, first_early), SHARE)

    message, gates = kernel_call(
        functools.partial(send_grad_kernel, *sizes),
        (message_shape, jax.ShapeDtypeStruct((tokens, router_width), F32)),
        (normed, route_ids, grad_top, table, place, owner, chunk_of[:, None], slot_of),
        token_scratch,
    )
    message, arrived = lax.optimization_barrier((message, arrived))
    arrived_grad = exchange(message, SHARE)

    at = np.arange(group * half, dtype=np.int32)
    into_messages = (at % half // slots * group + at // half) * slots + at % slots
    into_rows = np.zeros_like(at)
    into_rows[into_messages] = at
    step_width = hidden_width // HIDDEN_STEPS
    all_rows = peers * slots
    whole = lambda shape: pl.BlockSpec(shape, lambda i: (0,) * len(shape))
    scalar = pl.BlockSpec(memory_space=pltpu.SMEM)

    def products(arrived, weights, side, steps, weight_specs):
        return kernel_call(
            functools.partial(products_kernel, group, chunks, slots, side),
            (
                jax.ShapeDtypeStruct((all_rows, steps * step_width), BF),
                jax.ShapeDtypeStruct((all_rows, 2 * part), BF),
            ),
            (index, arrived, into_rows[:, None]) + weights,
            grid=(steps,),
            in_specs=[scalar, whole(arrived.shape), whole((at.size, 1))] + weight_specs,
            out_specs=[pl.BlockSpec((all_rows, step_width), lambda i: (0, i)), whole((all_rows, 2 * part))],
        )

    partial, expert_rows = products(
        arrived,
        (first, first_early, first_late),
        0,
        2 * HIDDEN_STEPS,
        [pl.BlockSpec((size, step_width), lambda i: (0, i)) for size in (part, early, part - early)],
    )
    pre_act = lax.psum_scatter(partial, "dp", scatter_dimension=0, tiled=True)
    partial, grad_rows = products(
        arrived_grad,
        (second, second_other),
        1,
        HIDDEN_STEPS,
        [pl.BlockSpec((step_width, part), lambda i: (i, 0))] * 2,
    )
    partial, pre_act = lax.optimization_barrier((partial, pre_act))
    summands = exchange(partial.reshape(replicas, rows, hidden_width), "dp")
    gate_pre = pre_act[:, :hidden_width].astype(F32)
    up = pre_act[:, hidden_width:].astype(F32)
    hidden = (gate_pre / (1.0 + jnp.exp(-gate_pre)) * up).astype(BF)
    hidden_all = lax.all_gather(hidden, "dp", axis=0, tiled=True)
    at = np.arange(rows, dtype=np.int32)
    pre_grad, worth = kernel_call(
        functools.partial(act_kernel, slots),
        (
            jax.ShapeDtypeStruct((rows, 2 * hidden_width), BF),
            jax.ShapeDtypeStruct((experts, LANES), F32),
        ),
        (summands, pre_act, after(hidden, hidden_all), at[None] // slots, at[:, None] % slots),
    )
    pre_grad_all = lax.all_gather(pre_grad, "dp", axis=0, tiled=True)

    worth = exchange(worth[:, None], "expert")[:, 0, :slots]
    slot_ids = jnp.arange(slots, dtype=F32)
    gate_worth = jnp.sum(
        jnp.where(place[:, :experts, None] == slot_ids, worth[None], 0.0), axis=2
    )
    inner = jnp.sum(gate_worth, axis=1, keepdims=True)
    logit_grad = jnp.pad(gate_worth, ((0, 0), (0, router_width - experts))) - gates * inner
    logit_high, logit_low = two_terms(logit_grad)
    local_router = mm(normed, logit_high, ((0,), (0,))) + mm(normed, logit_low, ((0,), (0,)))
    local_router = local_router.astype(BF).reshape(2, replicas, part, router_width).transpose(1, 0, 2, 3)
    second_other_grad = mm(hidden_all, grad_rows[:, part:], ((0,), (0,))).astype(BF)
    second_sent = swapped(second_other_grad, "half")
    local_router = after(local_router, second_other_grad)
    router_part = exchange(local_router.reshape(replicas, 2 * part, router_width), "dp")
    router_part = jnp.sum(router_part.astype(F32), axis=0)

    steps = 2 if all_rows // 2 % (2 * group * slots) == 0 else 1

    def by_rows(width):
        return pl.BlockSpec((all_rows // steps, width), lambda i: (i, 0))

    messages = pl.BlockSpec((peers // steps, half, LANES), lambda i: (i, 0, 0))
    order = into_messages[:, None]
    out_message = kernel_call(
        functools.partial(out_kernel, group, chunks, slots),
        message_shape,
        (index, hidden_all, order, second, second_other),
        grid=(steps,),
        in_specs=[scalar, by_rows(hidden_width), whole(order.shape), whole(second.shape), whole(second.shape)],
        out_specs=messages,
    )
    message, gain_part = kernel_call(
        functools.partial(back_kernel, group, chunks, slots),
        (jax.ShapeDtypeStruct((peers, 2 * half, LANES), BF), jax.ShapeDtypeStruct((1, 2 * part), F32)),
        (index, pre_grad_all, order, first, first_early, first_late, expert_rows, after(out_message, second_sent)),
        grid=(steps,),
        in_specs=[
            scalar,
            by_rows(2 * hidden_width),
            whole(order.shape),
            whole(first.shape),
            whole(first_early.shape),
            whole(first_late.shape),
            by_rows(2 * part),
            messages,
        ],
        out_specs=[
            pl.BlockSpec((peers // steps, 2 * half, LANES), lambda i: (i, 0, 0)),
            whole((1, 2 * part)),
        ],
    )
    gain_part = gain_part.reshape(2, part)
    gain_part = jnp.where(side == 0, gain_part, gain_part[::-1])

    owners = 2 * experts
    piece = 2 * part // owners
    gain_rows = jnp.pad(gain_part.reshape(owners, 1, piece), ((0, 0), (0, 7), (0, LANES - piece)))
    owned = jnp.concatenate([router_part.reshape(owners, piece, router_width), gain_rows], axis=1)
    owned = jnp.sum(exchange(owned, OWNERS), axis=0)
    first_other_grad = mm(expert_rows[:, part:], pre_grad_all, ((0,), (0,))).astype(BF)
    first_sent = swapped(first_other_grad, "half")
    message, owned = lax.optimization_barrier((message, owned, first_other_grad))[:2]
    returned = exchange(message, SHARE)
    router_own = owned[:piece]
    at = (side * replicas + lax.axis_index("dp")) * part + lax.axis_index("expert") * piece
    table_own = lax.dynamic_slice_in_dim(table, at, piece, axis=0).astype(F32)
    gain_here = lax.dynamic_slice_in_dim(gain[0], at, piece, axis=0)
    gain_sum = (owned[piece, :piece] + jnp.sum(router_own * table_own, axis=1)) / gain_here
    gain_terms = jnp.pad(jnp.stack(three_terms(gain_sum)), ((0, 13), (0, LANES - piece)))
    block = jnp.concatenate([router_own.astype(BF), gain_terms], axis=0)
    block_other = swapped(block, "half")
    joined = jnp.where(side == 0, jnp.stack([block, block_other]), jnp.stack([block_other, block]))
    joined = lax.all_gather(joined, "expert", axis=0)
    joined = lax.all_gather(joined.reshape(-1, LANES), "dp", axis=0, tiled=True)
    joined = joined.reshape(replicas, experts, 2, piece + 16, LANES).transpose(2, 0, 1, 3, 4)
    router_total = joined[:, :, :, :piece].reshape(width, router_width)
    gain_total = jnp.sum(joined[:, :, :, piece : piece + 3, :piece].astype(F32), axis=3).reshape(width)

    second_own_grad = mm(hidden_all, grad_rows[:, :part], ((0,), (0,)))
    second_grad = (second_own_grad + second_sent.astype(F32)).astype(BF)
    first_own_grad = mm(expert_rows[:, :part], pre_grad_all, ((0,), (0,)))
    first_grad = (first_own_grad + first_sent.astype(F32)).astype(BF)

    token_shape = jax.ShapeDtypeStruct((tokens, width), BF)
    joined_scratch = pltpu.VMEM((experts * half, replicas * LANES), BF)
    layer_out = kernel_call(
        functools.partial(layer_kernel, experts, replicas, chunks),
        token_shape,
        (returned, after(x, first_grad, second_grad), gates, place, owner, chunk_of[None], slot_of),
        [joined_scratch],
    )
    in_grad = kernel_call(
        functools.partial(in_grad_kernel, experts, replicas, chunks),
        token_shape,
        (returned, x, grad_top, gain, table, place, logit_grad, owner, chunk_of[None], slot_of),
        [joined_scratch, pltpu.VMEM((tokens, width), F32)],
    )
    handoff = swapped(layer_out, "section")
    handback = swapped(in_grad, "section")
    return (
        handoff[None],
        handback[None],
        first_grad[None, None],
        second_grad[None, None],
        router_total[None],
        gain_total[None],
    )


def solution(mesh):
    sizes = mesh.shape
    halves = (sizes["section"], sizes["expert"], 2, sizes["dp"] // 2)
    split = Mesh(mesh.devices.reshape(halves), ("section", "expert", "half", "dp"))
    blocks = ("half", "dp")
    tokens = ("expert",) + blocks
    return jax.shard_map(
        shards,
        mesh=split,
        in_specs=(
            P("section", tokens, None),
            P("section", tokens, None),
            P("section", tokens, None),
            P("section", None),
            P("section", None, None),
            P("section", "expert", blocks, None),
            P("section", "expert", None, blocks),
        ),
        out_specs=(
            P("section", tokens, None),
            P("section", tokens, None),
            P("section", "expert", blocks, None),
            P("section", "expert", None, blocks),
            P("section", None, None),
            P("section", None),
        ),
        check_vma=False,
    )
```

```python
import functools

import jax
import jax.numpy as jnp
import numpy as np
from jax import lax
from jax.experimental import pallas as pl
from jax.experimental.pallas import tpu as pltpu
from jax.sharding import Mesh
from jax.sharding import PartitionSpec as P

MOST = 10
LANES = 128
BF = jnp.bfloat16
F32 = jnp.float32
SHARE = ("dp", "expert")
OWNERS = ("half", "expert")
INTERPRET = False
HIDDEN_STEPS = 3


def exchange(blocks, axes):
    return lax.all_to_all(blocks, axes, split_axis=0, concat_axis=0, tiled=True)


def mm(left, right, contract=((1,), (0,))):
    return lax.dot_general(left, right, (contract, ((), ())), preferred_element_type=F32)


def two_terms(values):
    high = values.astype(BF)
    return high, (values - high.astype(F32)).astype(BF)


def three_terms(values):
    high = values.astype(BF)
    return (high,) + two_terms(values - high.astype(F32))


def kernel_call(body, outs, args, scratch=(), **grid):
    return pl.pallas_call(
        body,
        out_shape=outs,
        scratch_shapes=scratch,
        compiler_params=pltpu.CompilerParams(vmem_limit_bytes=52 * 2**20),
        interpret=INTERPRET,
        **grid,
    )(*args)


def iota(shape, dimension):
    return lax.broadcasted_iota(jnp.int32, shape, dimension)


def spread(values, owner):
    pick = (iota((values[0].shape[1], owner.shape[1]), 0) == owner).astype(BF)
    total = mm(values[0], pick)
    for term in values[1:]:
        total = total + mm(term, pick)
    return total


def feature(replicas, width, c, j):
    part = width // (2 * replicas)
    block, inner = divmod(c * LANES, part)
    return (block * replicas + j) * part + inner


def picks_of(chunks, hits, chunk_of):
    rows = jnp.where(hits, 1.0, 0.0).T
    return jnp.concatenate(
        [jnp.where(chunk_of == c, rows, 0.0).astype(BF) for c in range(chunks)], axis=1
    )


def stacked(chunks, replicas, source, stack):
    tokens, width = source.shape
    for c in range(chunks):
        for j in range(replicas):
            at = feature(replicas, width, c, j)
            stack[c * tokens : (c + 1) * tokens, j * LANES : (j + 1) * LANES] = source[:, at : at + LANES]
    return stack[...]


def write_messages(experts, replicas, half, sent, message):
    for j in range(replicas):
        for e in range(experts):
            message[j * experts + e] = sent[e * half : (e + 1) * half, j * LANES : (j + 1) * LANES]


def slot_hits(place, owner, slot_of):
    return spread((place[...].astype(BF),), owner[...]) == slot_of[...].astype(F32)


def named_by(ids, shape):
    columns = iota(shape, 1)
    named = columns == ids[:, 0:1]
    for k in range(1, ids.shape[1]):
        named = named | (columns == ids[:, k : k + 1])
    return named


def send_kernel(experts, replicas, chunks, slots, x, ids, gain, owner, chunk_of, slot_of,
                message, normed, place, stack):
    tokens, width = x.shape
    xw = x[...].astype(F32)
    inv_rms = lax.rsqrt(jnp.mean(xw * xw, axis=1, keepdims=True) + 1e-06)
    normed[...] = (xw * inv_rms * gain[...]).astype(BF)
    named = named_by(ids, place.shape)
    earlier = (iota((tokens, tokens), 1) < iota((tokens, tokens), 0)).astype(BF)
    rank = mm(earlier, named.astype(BF))
    place[...] = jnp.where(named & (iota(place.shape, 1) < experts), rank, -1.0)
    pick = picks_of(chunks, slot_hits(place, owner, slot_of), chunk_of[...])
    sent = mm(pick, stacked(chunks, replicas, normed, stack)).astype(BF)
    write_messages(experts, replicas, chunks * slots, sent, message)


def send_grad_kernel(experts, replicas, chunks, slots, normed, ids, grad, table, place, owner, chunk_of, slot_of,
                     message, gates_out, stack):
    logits = mm(normed[...], table[...])
    powers = jnp.where(named_by(ids, logits.shape), jnp.exp(logits), 0.0)
    gates = powers / jnp.sum(powers, axis=1, keepdims=True)
    gates_out[...] = gates
    hits = slot_hits(place, owner, slot_of)
    weight = jnp.where(hits, spread(three_terms(gates), owner[...]), 0.0)
    slot_gate = jnp.sum(weight.T, axis=1, keepdims=True)
    pick = picks_of(chunks, hits, chunk_of[...])
    sent = (mm(pick, stacked(chunks, replicas, grad, stack)) * slot_gate).astype(BF)
    write_messages(experts, replicas, chunks * slots, sent, message)


def products_kernel(group, chunks, slots, side, index, arrived, order, *refs):
    weights, partial, rows_out = refs[:-2], refs[-2], refs[-1]
    half = chunks * slots
    size = group * half
    block = group * slots
    own_chunks = chunks // 2
    part = own_chunks * LANES

    @pl.when(pl.program_id(0) == 0)
    def _():
        lower = index[0] == 0
        pick = (order[...] == iota((size, size), 1)).astype(BF)
        for pair in range(arrived.shape[0] // group // 2):
            lanes = [
                arrived[(2 * pair + w) * group : (2 * pair + w + 1) * group].reshape(size, LANES)
                for w in range(2)
            ]
            picked = mm(pick, jnp.concatenate(lanes, axis=1)).astype(BF)
            for c in range(own_chunks):
                low = picked[c * block : (c + 1) * block]
                high = picked[(own_chunks + c) * block : (own_chunks + c + 1) * block]
                own = jnp.where(lower, low, high)
                other = jnp.where(lower, high, low)
                for w in range(2):
                    rows = slice((2 * pair + w) * block, (2 * pair + w + 1) * block)
                    lanes = slice(w * LANES, (w + 1) * LANES)
                    rows_out[rows, c * LANES : (c + 1) * LANES] = own[:, lanes]
                    rows_out[rows, part + c * LANES : part + (c + 1) * LANES] = other[:, lanes]

    weight = jnp.concatenate([piece[...] for piece in weights], axis=side)
    partial[...] = mm(rows_out[...], weight, ((1,), (side,))).astype(BF)


def act_kernel(slots, arrived, pre_act, hidden, sender_of, slot_of, pre_grad, worth):
    replicas, rows, hidden_width = arrived.shape
    hidden_grad = arrived[0].astype(F32)
    for j in range(1, replicas):
        hidden_grad = hidden_grad + arrived[j].astype(F32)
    gate_pre, up = pre_act[:, :hidden_width], pre_act[:, hidden_width:]
    sigmoid = 1.0 / (1.0 + jnp.exp(-gate_pre))
    silu = gate_pre * sigmoid
    slope = sigmoid * (1.0 + gate_pre * (1.0 - sigmoid))
    pre_grad[:, :hidden_width] = (hidden_grad * up * slope).astype(BF)
    pre_grad[:, hidden_width:] = (hidden_grad * silu).astype(BF)
    each = jnp.sum(hidden_grad * hidden[...].astype(F32), axis=1, keepdims=True)
    laid = jnp.where(slot_of[...] == iota((rows, LANES), 1), each, 0.0)
    pick = (sender_of[...] == iota((worth.shape[0], rows), 0)).astype(BF)
    terms = three_terms(laid)
    worth[...] = mm(pick, terms[0]) + mm(pick, terms[1]) + mm(pick, terms[2])


def return_rows(group, chunks, slots, lower, order, own, other, message, first_row=0):
    block = group * slots
    half = chunks * slots
    size = group * half
    own_chunks = chunks // 2
    own, other = own.astype(BF), other.astype(BF)
    sides = jnp.where(lower, own, other), jnp.where(lower, other, own)
    pick = (order[...] == iota((size, size), 1)).astype(BF)

    def column(at):
        return jnp.concatenate(
            [
                side[at : at + block, c * LANES : (c + 1) * LANES]
                for side in sides
                for c in range(own_chunks)
            ],
            axis=0,
        )

    for pair in range(own.shape[0] // block // 2):
        lanes = [column((2 * pair + w) * block) for w in range(2)]
        picked = mm(pick, jnp.concatenate(lanes, axis=1)).astype(BF)
        for w in range(2):
            to = slice((2 * pair + w) * group, (2 * pair + w + 1) * group)
            message[to, first_row : first_row + half] = picked[:, w * LANES : (w + 1) * LANES].reshape(
                group, half, LANES
            )


def out_kernel(group, chunks, slots, index, hidden, order, second, second_other, message):
    own = mm(hidden[...], second[...])
    other = mm(hidden[...], second_other[...])
    return_rows(group, chunks, slots, index[0] == 0, order, own, other, message)


def back_kernel(group, chunks, slots, index, pre_grad, order, first, rows, outs, *refs):
    message, gain = refs[-2:]
    own = mm(pre_grad[...], first[...], ((1,), (1,)))
    other = mm(pre_grad[...], jnp.concatenate([piece[...] for piece in refs[:-2]], axis=0), ((1,), (1,)))
    half = chunks * slots
    message[:, :half] = outs[...]
    return_rows(group, chunks, slots, index[0] == 0, order, own, other, message, half)

    @pl.when(pl.program_id(0) == 0)
    def _():
        gain[...] = jnp.zeros_like(gain)

    part = own.shape[1]
    gain[:, :part] += jnp.sum(own * rows[:, :part].astype(F32), axis=0, keepdims=True)
    gain[:, part:] += jnp.sum(other * rows[:, part:].astype(F32), axis=0, keepdims=True)


def join(experts, replicas, kind, returned, joined):
    half = returned.shape[1] // 2
    for j in range(replicas):
        block = returned[j * experts : (j + 1) * experts, kind * half : (kind + 1) * half]
        joined[:, j * LANES : (j + 1) * LANES] = block.reshape(experts * half, LANES)
    return joined[...]


def to_tokens(chunks, values, chunk_of):
    return jnp.concatenate(
        [jnp.where(chunk_of == c, values, 0.0).astype(BF) for c in range(chunks)], axis=0
    )


def layer_kernel(experts, replicas, chunks, returned, x, gates, place, owner, chunk_of, slot_of, layer_out, joined):
    tokens, width = x.shape
    hits = slot_hits(place, owner, slot_of)
    source = join(experts, replicas, 0, returned, joined)
    mixed = 0.0
    for term in two_terms(gates[...]):
        weight = jnp.where(hits, spread((term,), owner[...]), 0.0)
        mixed = mixed + mm(to_tokens(chunks, weight, chunk_of[...]), source)
    for c in range(chunks):
        for j in range(replicas):
            at = feature(replicas, width, c, j)
            at = slice(at, at + LANES)
            here = mixed[c * tokens : (c + 1) * tokens, j * LANES : (j + 1) * LANES]
            layer_out[:, at] = (x[:, at].astype(F32) + here).astype(BF)


def in_grad_kernel(experts, replicas, chunks, returned, x, grad, gain, table, place, logit_grad,
                   owner, chunk_of, slot_of, in_grad, joined, normed_grad):
    tokens, width = x.shape
    ones = jnp.where(slot_hits(place, owner, slot_of), 1.0, 0.0)
    back = mm(to_tokens(chunks, ones, chunk_of[...]), join(experts, replicas, 1, returned, joined))
    high, low = two_terms(logit_grad[...])
    by_logits = mm(high, table[...], ((1,), (1,))) + mm(low, table[...], ((1,), (1,)))
    for c in range(chunks):
        for j in range(replicas):
            at = feature(replicas, width, c, j)
            at = slice(at, at + LANES)
            here = back[c * tokens : (c + 1) * tokens, j * LANES : (j + 1) * LANES]
            normed_grad[:, at] = here + by_logits[:, at]
    xw = x[...].astype(F32)
    inv_rms = lax.rsqrt(jnp.mean(xw * xw, axis=1, keepdims=True) + 1e-06)
    weighted = gain[...] * normed_grad[...]
    mean = jnp.mean(xw * weighted, axis=1, keepdims=True)
    in_grad[...] = (
        grad[...].astype(F32) + inv_rms * weighted - xw * (inv_rms * inv_rms * inv_rms * mean)
    ).astype(BF)


def after(value, *earlier):
    return lax.optimization_barrier((value,) + earlier)[0]


def swapped(block, axis):
    return lax.ppermute(block, axis, [(0, 1), (1, 0)])


def shards(section_input, routing, out_grad, norm_gain, router, w_in, w_out):
    experts = lax.axis_size("expert")
    replicas = lax.axis_size("dp")
    x = section_input[0]
    route_ids = routing[0]
    grad_top = out_grad[0]
    gain = norm_gain[0][None, :]
    table = router[0]
    first = w_in[0, 0]
    second = w_out[0, 0]
    tokens, width = x.shape
    part = first.shape[0]
    hidden_width = second.shape[0]
    slots = MOST
    rows = experts * slots
    router_width = table.shape[1]
    chunks = 2 * part // LANES
    half = chunks * slots
    peers = replicas * experts
    group = min(8, experts)
    message_shape = jax.ShapeDtypeStruct((peers, half, LANES), BF)
    side = lax.axis_index("half")
    index = side.astype(jnp.int32)[None]
    cuts = (0, part // 4, 7 * part // 8, part)
    first_other = tuple(swapped(first[a:b], "half") for a, b in zip(cuts, cuts[1:]))
    second_other = swapped(second, "half")

    at = np.arange(experts * half, dtype=np.int32)
    owner, chunk_of, slot_of = (at // half)[None], at % half // slots, (at % slots)[None]
    sizes = (experts, replicas, chunks, slots)
    token_scratch = [pltpu.VMEM((chunks * tokens, replicas * LANES), BF)]
    message, normed, place = kernel_call(
        functools.partial(send_kernel, *sizes),
        (
            message_shape,
            jax.ShapeDtypeStruct((tokens, width), BF),
            jax.ShapeDtypeStruct((tokens, router_width), F32),
        ),
        (x, route_ids, gain, owner, chunk_of[:, None], slot_of),
        token_scratch,
    )
    arrived = exchange(after(message, first_other[0]), SHARE)

    message, gates = kernel_call(
        functools.partial(send_grad_kernel, *sizes),
        (message_shape, jax.ShapeDtypeStruct((tokens, router_width), F32)),
        (normed, route_ids, grad_top, table, place, owner, chunk_of[:, None], slot_of),
        token_scratch,
    )
    message, arrived = lax.optimization_barrier((message, arrived, first_other[1]))[:2]
    arrived_grad = exchange(message, SHARE)

    at = np.arange(group * half, dtype=np.int32)
    into_messages = (at % half // slots * group + at // half) * slots + at % slots
    into_rows = np.zeros_like(at)
    into_rows[into_messages] = at
    step_width = hidden_width // HIDDEN_STEPS
    all_rows = peers * slots
    whole = lambda shape: pl.BlockSpec(shape, lambda i: (0,) * len(shape))
    scalar = pl.BlockSpec(memory_space=pltpu.SMEM)

    sizes_other = tuple(piece.shape[0] for piece in first_other)

    def products(arrived, weights, side, steps, weight_specs):
        return kernel_call(
            functools.partial(products_kernel, group, chunks, slots, side),
            (
                jax.ShapeDtypeStruct((all_rows, steps * step_width), BF),
                jax.ShapeDtypeStruct((all_rows, 2 * part), BF),
            ),
            (index, arrived, into_rows[:, None]) + weights,
            grid=(steps,),
            in_specs=[scalar, whole(arrived.shape), whole((at.size, 1))] + weight_specs,
            out_specs=[pl.BlockSpec((all_rows, step_width), lambda i: (0, i)), whole((all_rows, 2 * part))],
        )

    partial, expert_rows = products(
        arrived,
        (first,) + first_other,
        0,
        2 * HIDDEN_STEPS,
        [pl.BlockSpec((size, step_width), lambda i: (0, i)) for size in (part,) + sizes_other],
    )
    partial = partial.reshape(replicas, rows, 2 * hidden_width)
    place_in_dp = lax.axis_index("dp")
    pre_act = lax.dynamic_index_in_dim(partial, place_in_dp, 0, False).astype(F32)
    for step in range(1, replicas):
        shift = [(j, (j + step) % replicas) for j in range(replicas)]
        block = lax.dynamic_index_in_dim(partial, (place_in_dp + step) % replicas, 0, False)
        pre_act = pre_act + lax.ppermute(block, "dp", shift).astype(F32)
    partial, grad_rows = products(
        arrived_grad,
        (second, second_other),
        1,
        HIDDEN_STEPS,
        [pl.BlockSpec((step_width, part), lambda i: (i, 0))] * 2,
    )
    summands = exchange(partial.reshape(replicas, rows, hidden_width), "dp")
    gate_pre, up = pre_act[:, :hidden_width], pre_act[:, hidden_width:]
    hidden = (gate_pre / (1.0 + jnp.exp(-gate_pre)) * up).astype(BF)
    hidden_all = jnp.zeros((all_rows, hidden_width), BF)
    for step in range(replicas):
        shift = [(j, (j + step) % replicas) for j in range(replicas)]
        block = lax.ppermute(hidden, "dp", shift) if step else hidden
        at_row = (place_in_dp + replicas - step) % replicas * rows
        hidden_all = lax.dynamic_update_slice(hidden_all, block, (at_row, 0))
    at = np.arange(rows, dtype=np.int32)
    pre_grad, worth = kernel_call(
        functools.partial(act_kernel, slots),
        (
            jax.ShapeDtypeStruct((rows, 2 * hidden_width), BF),
            jax.ShapeDtypeStruct((experts, LANES), F32),
        ),
        (summands, pre_act, hidden, at[None] // slots, at[:, None] % slots),
    )
    pre_grad_all = lax.all_gather(pre_grad, "dp", axis=0, tiled=True)

    worth = exchange(worth[:, None], "expert")[:, 0, :slots]
    slot_ids = jnp.arange(slots, dtype=F32)
    gate_worth = jnp.sum(
        jnp.where(place[:, :experts, None] == slot_ids, worth[None], 0.0), axis=2
    )
    inner = jnp.sum(gate_worth, axis=1, keepdims=True)
    logit_grad = jnp.pad(gate_worth, ((0, 0), (0, router_width - experts))) - gates * inner
    logit_high, logit_low = two_terms(logit_grad)
    local_router = mm(normed, logit_high, ((0,), (0,))) + mm(normed, logit_low, ((0,), (0,)))
    local_router = local_router.astype(BF).reshape(experts, -1, router_width)
    second_other_grad = mm(hidden_all, grad_rows[:, part:], ((0,), (0,))).astype(BF)
    second_sent = swapped(second_other_grad, "half")
    local_router = after(local_router, second_other_grad)
    router_part = jnp.sum(exchange(local_router, "expert").astype(F32), axis=0)
    piece = router_part.shape[0] // (2 * replicas)
    router_part = router_part.reshape(2 * replicas, piece, router_width)
    router_own = jnp.sum(exchange(router_part, ("half", "dp")), axis=0)
    at = lax.axis_index("expert") * 2 * replicas + side * replicas + place_in_dp
    table_own = lax.dynamic_slice_in_dim(table, at * piece, piece, axis=0).astype(F32)
    gain_own = jnp.sum(router_own * table_own, axis=1)

    steps = 2 if all_rows // 2 % (2 * group * slots) == 0 else 1

    def by_rows(width):
        return pl.BlockSpec((all_rows // steps, width), lambda i: (i, 0))

    messages = pl.BlockSpec((peers // steps, half, LANES), lambda i: (i, 0, 0))
    order = into_messages[:, None]
    out_message = kernel_call(
        functools.partial(out_kernel, group, chunks, slots),
        message_shape,
        (index, hidden_all, order, second, second_other),
        grid=(steps,),
        in_specs=[scalar, by_rows(hidden_width), whole(order.shape), whole(second.shape), whole(second.shape)],
        out_specs=messages,
    )
    message, gain_part = kernel_call(
        functools.partial(back_kernel, group, chunks, slots),
        (jax.ShapeDtypeStruct((peers, 2 * half, LANES), BF), jax.ShapeDtypeStruct((1, 2 * part), F32)),
        (index, pre_grad_all, order, first, expert_rows, after(out_message, second_sent)) + first_other,
        grid=(steps,),
        in_specs=[
            scalar,
            by_rows(2 * hidden_width),
            whole(order.shape),
            whole(first.shape),
            by_rows(2 * part),
            messages,
            *(whole(piece.shape) for piece in first_other),
        ],
        out_specs=[
            pl.BlockSpec((peers // steps, 2 * half, LANES), lambda i: (i, 0, 0)),
            whole((1, 2 * part)),
        ],
    )
    gain_part = gain_part.reshape(2, part)
    gain_part = jnp.where(side == 0, gain_part, gain_part[::-1])

    lines = 2 * part // LANES
    terms = three_terms(gain_part.reshape(lines, LANES))
    lone = [jnp.pad(term[None], ((0, 0), (0, LANES - piece))) for term in three_terms(gain_own)]
    block = jnp.concatenate([router_own.astype(BF), *terms, *lone], axis=0)
    block = jnp.pad(block, ((0, -block.shape[0] % 16), (0, 0)))
    owners = 2 * experts
    joined = exchange(jnp.broadcast_to(block[None], (owners,) + block.shape), OWNERS)
    first_other_grad = mm(expert_rows[:, part:], pre_grad_all, ((0,), (0,))).astype(BF)
    first_sent = swapped(first_other_grad, "half")
    message, joined = lax.optimization_barrier((message, joined, first_other_grad))[:2]
    returned = exchange(message, SHARE)
    end = piece + 3 * lines
    gain_rows = jnp.sum(joined[:, piece:end].astype(F32).reshape(owners, 3, lines, LANES), axis=(0, 1))
    lone = jnp.sum(joined[:, end : end + 3, :piece].astype(F32), axis=1).reshape(-1, LANES)
    sums = jnp.concatenate([*three_terms(gain_rows), *three_terms(lone)], axis=0)
    sums = jnp.pad(sums, ((0, -sums.shape[0] % 16), (0, 0)))
    packed = jnp.concatenate([joined[:, :piece].reshape(-1, LANES), sums], axis=0)
    packed = lax.all_gather(packed, "dp", axis=0)
    router_rows = owners * piece
    router_total = packed[:, :router_rows].reshape(replicas, 2, experts, piece, router_width)
    router_total = router_total.transpose(2, 1, 0, 3, 4).reshape(width, router_width)
    gain_rows = packed[:, router_rows : router_rows + 3 * lines].astype(F32)
    gain_rows = jnp.sum(gain_rows.reshape(replicas, 3, 2, part), axis=1)
    lone = packed[:, router_rows + 3 * lines : router_rows + 6 * lines].astype(F32)
    lone = jnp.sum(lone.reshape(replicas, 3, 2, experts, piece), axis=1)
    gain_total = gain_rows.transpose(1, 0, 2).reshape(width) + lone.transpose(2, 1, 0, 3).reshape(width)
    gain_total = gain_total / gain[0]

    second_own_grad = mm(hidden_all, grad_rows[:, :part], ((0,), (0,)))
    second_grad = (second_own_grad + second_sent.astype(F32)).astype(BF)
    first_own_grad = mm(expert_rows[:, :part], pre_grad_all, ((0,), (0,)))
    first_grad = (first_own_grad + first_sent.astype(F32)).astype(BF)

    token_shape = jax.ShapeDtypeStruct((tokens, width), BF)
    joined_scratch = pltpu.VMEM((experts * half, replicas * LANES), BF)
    layer_out = kernel_call(
        functools.partial(layer_kernel, experts, replicas, chunks),
        token_shape,
        (returned, after(x, first_grad, second_grad), gates, place, owner, chunk_of[None], slot_of),
        [joined_scratch],
    )
    in_grad = kernel_call(
        functools.partial(in_grad_kernel, experts, replicas, chunks),
        token_shape,
        (returned, x, grad_top, gain, table, place, logit_grad, owner, chunk_of[None], slot_of),
        [joined_scratch, pltpu.VMEM((tokens, width), F32)],
    )
    handoff = swapped(layer_out, "section")
    handback = swapped(in_grad, "section")
    return (
        handoff[None],
        handback[None],
        first_grad[None, None],
        second_grad[None, None],
        router_total[None],
        gain_total[None],
    )


def solution(mesh):
    sizes = mesh.shape
    halves = (sizes["section"], sizes["expert"], 2, sizes["dp"] // 2)
    split = Mesh(mesh.devices.reshape(halves), ("section", "expert", "half", "dp"))
    blocks = ("half", "dp")
    tokens = ("expert",) + blocks
    return jax.shard_map(
        shards,
        mesh=split,
        in_specs=(
            P("section", tokens, None),
            P("section", tokens, None),
            P("section", tokens, None),
            P("section", None),
            P("section", None, None),
            P("section", "expert", blocks, None),
            P("section", "expert", None, blocks),
        ),
        out_specs=(
            P("section", tokens, None),
            P("section", tokens, None),
            P("section", "expert", blocks, None),
            P("section", "expert", None, blocks),
            P("section", None, None),
            P("section", None),
        ),
        check_vma=False,
    )
```

```python
import functools

import jax
import jax.numpy as jnp
import numpy as np
from jax import lax
from jax.experimental import pallas as pl
from jax.experimental.pallas import tpu as pltpu
from jax.sharding import Mesh
from jax.sharding import PartitionSpec as P

MOST = 10
LANES = 128
BF = jnp.bfloat16
F32 = jnp.float32
SHARE = ("dp", "expert")
OWNERS = ("half", "expert")
INTERPRET = False
HIDDEN_STEPS = 3


def exchange(blocks, axes):
    return lax.all_to_all(blocks, axes, split_axis=0, concat_axis=0, tiled=True)


def mm(left, right, contract=((1,), (0,))):
    return lax.dot_general(left, right, (contract, ((), ())), preferred_element_type=F32)


def two_terms(values):
    high = values.astype(BF)
    return high, (values - high.astype(F32)).astype(BF)


def three_terms(values):
    high = values.astype(BF)
    return (high,) + two_terms(values - high.astype(F32))


def kernel_call(body, outs, args, scratch=(), **grid):
    return pl.pallas_call(
        body,
        out_shape=outs,
        scratch_shapes=scratch,
        compiler_params=pltpu.CompilerParams(vmem_limit_bytes=52 * 2**20),
        interpret=INTERPRET,
        **grid,
    )(*args)


def iota(shape, dimension):
    return lax.broadcasted_iota(jnp.int32, shape, dimension)


def spread(values, owner):
    pick = (iota((values[0].shape[1], owner.shape[1]), 0) == owner).astype(BF)
    total = mm(values[0], pick)
    for term in values[1:]:
        total = total + mm(term, pick)
    return total


def feature(replicas, width, c, j):
    part = width // (2 * replicas)
    block, inner = divmod(c * LANES, part)
    return (block * replicas + j) * part + inner


def picks_of(chunks, hits, chunk_of):
    rows = jnp.where(hits, 1.0, 0.0).T
    return jnp.concatenate(
        [jnp.where(chunk_of == c, rows, 0.0).astype(BF) for c in range(chunks)], axis=1
    )


def stacked(chunks, replicas, source, stack):
    tokens, width = source.shape
    for c in range(chunks):
        for j in range(replicas):
            at = feature(replicas, width, c, j)
            stack[c * tokens : (c + 1) * tokens, j * LANES : (j + 1) * LANES] = source[:, at : at + LANES]
    return stack[...]


def write_messages(experts, replicas, half, sent, message):
    for j in range(replicas):
        for e in range(experts):
            message[j * experts + e] = sent[e * half : (e + 1) * half, j * LANES : (j + 1) * LANES]


def slot_hits(place, owner, slot_of):
    return spread((place[...].astype(BF),), owner[...]) == slot_of[...].astype(F32)


def named_by(ids, shape):
    columns = iota(shape, 1)
    named = columns == ids[:, 0:1]
    for k in range(1, ids.shape[1]):
        named = named | (columns == ids[:, k : k + 1])
    return named


def send_kernel(experts, replicas, chunks, slots, x, ids, gain, owner, chunk_of, slot_of,
                message, normed, place, stack):
    tokens, width = x.shape
    xw = x[...].astype(F32)
    inv_rms = lax.rsqrt(jnp.mean(xw * xw, axis=1, keepdims=True) + 1e-06)
    normed[...] = (xw * inv_rms * gain[...]).astype(BF)
    named = named_by(ids, place.shape)
    earlier = (iota((tokens, tokens), 1) < iota((tokens, tokens), 0)).astype(BF)
    rank = mm(earlier, named.astype(BF))
    place[...] = jnp.where(named & (iota(place.shape, 1) < experts), rank, -1.0)
    pick = picks_of(chunks, slot_hits(place, owner, slot_of), chunk_of[...])
    sent = mm(pick, stacked(chunks, replicas, normed, stack)).astype(BF)
    write_messages(experts, replicas, chunks * slots, sent, message)


def send_grad_kernel(experts, replicas, chunks, slots, normed, ids, grad, table, place, owner, chunk_of, slot_of,
                     message, gates_out, stack):
    logits = mm(normed[...], table[...])
    powers = jnp.where(named_by(ids, logits.shape), jnp.exp(logits), 0.0)
    gates = powers / jnp.sum(powers, axis=1, keepdims=True)
    gates_out[...] = gates
    hits = slot_hits(place, owner, slot_of)
    weight = jnp.where(hits, spread(three_terms(gates), owner[...]), 0.0)
    slot_gate = jnp.sum(weight.T, axis=1, keepdims=True)
    pick = picks_of(chunks, hits, chunk_of[...])
    sent = (mm(pick, stacked(chunks, replicas, grad, stack)) * slot_gate).astype(BF)
    write_messages(experts, replicas, chunks * slots, sent, message)


def products_kernel(group, chunks, slots, side, index, arrived, order, *refs):
    weights, partial, rows_out = refs[:-2], refs[-2], refs[-1]
    half = chunks * slots
    size = group * half
    block = group * slots
    own_chunks = chunks // 2
    part = own_chunks * LANES

    @pl.when(pl.program_id(0) == 0)
    def _():
        lower = index[0] == 0
        pick = (order[...] == iota((size, size), 1)).astype(BF)
        for pair in range(arrived.shape[0] // group // 2):
            lanes = [
                arrived[(2 * pair + w) * group : (2 * pair + w + 1) * group].reshape(size, LANES)
                for w in range(2)
            ]
            picked = mm(pick, jnp.concatenate(lanes, axis=1)).astype(BF)
            for c in range(own_chunks):
                low = picked[c * block : (c + 1) * block]
                high = picked[(own_chunks + c) * block : (own_chunks + c + 1) * block]
                own = jnp.where(lower, low, high)
                other = jnp.where(lower, high, low)
                for w in range(2):
                    rows = slice((2 * pair + w) * block, (2 * pair + w + 1) * block)
                    lanes = slice(w * LANES, (w + 1) * LANES)
                    rows_out[rows, c * LANES : (c + 1) * LANES] = own[:, lanes]
                    rows_out[rows, part + c * LANES : part + (c + 1) * LANES] = other[:, lanes]

    if side == 0:
        weight = jnp.concatenate([piece[...] for piece in weights], axis=0)
    else:
        last = pl.program_id(0) == pl.num_programs(0) - 1
        own, early, late = weights
        weight = jnp.concatenate([own[...], jnp.where(last, late[...], early[...])], axis=1)
    partial[...] = mm(rows_out[...], weight, ((1,), (side,))).astype(BF)


def act_kernel(slots, arrived, pre_act, hidden, sender_of, slot_of, pre_grad, worth):
    replicas, rows, hidden_width = arrived.shape
    hidden_grad = arrived[0].astype(F32)
    for j in range(1, replicas):
        hidden_grad = hidden_grad + arrived[j].astype(F32)
    gate_pre, up = pre_act[:, :hidden_width], pre_act[:, hidden_width:]
    sigmoid = 1.0 / (1.0 + jnp.exp(-gate_pre))
    silu = gate_pre * sigmoid
    slope = sigmoid * (1.0 + gate_pre * (1.0 - sigmoid))
    pre_grad[:, :hidden_width] = (hidden_grad * up * slope).astype(BF)
    pre_grad[:, hidden_width:] = (hidden_grad * silu).astype(BF)
    each = jnp.sum(hidden_grad * hidden[...].astype(F32), axis=1, keepdims=True)
    laid = jnp.where(slot_of[...] == iota((rows, LANES), 1), each, 0.0)
    pick = (sender_of[...] == iota((worth.shape[0], rows), 0)).astype(BF)
    terms = three_terms(laid)
    worth[...] = mm(pick, terms[0]) + mm(pick, terms[1]) + mm(pick, terms[2])


def return_rows(group, chunks, slots, lower, order, own, other, message, first_row=0):
    block = group * slots
    half = chunks * slots
    size = group * half
    own_chunks = chunks // 2
    own, other = own.astype(BF), other.astype(BF)
    sides = jnp.where(lower, own, other), jnp.where(lower, other, own)
    pick = (order[...] == iota((size, size), 1)).astype(BF)

    def column(at):
        return jnp.concatenate(
            [
                side[at : at + block, c * LANES : (c + 1) * LANES]
                for side in sides
                for c in range(own_chunks)
            ],
            axis=0,
        )

    for pair in range(own.shape[0] // block // 2):
        lanes = [column((2 * pair + w) * block) for w in range(2)]
        picked = mm(pick, jnp.concatenate(lanes, axis=1)).astype(BF)
        for w in range(2):
            to = slice((2 * pair + w) * group, (2 * pair + w + 1) * group)
            message[to, first_row : first_row + half] = picked[:, w * LANES : (w + 1) * LANES].reshape(
                group, half, LANES
            )


def out_kernel(group, chunks, slots, index, hidden, order, second, early, late, message):
    own = mm(hidden[...], second[...])
    other = mm(hidden[...], jnp.concatenate([early[...], late[...]], axis=0))
    return_rows(group, chunks, slots, index[0] == 0, order, own, other, message)


def back_kernel(group, chunks, slots, index, pre_grad, order, first, rows, outs, *refs):
    message, gain = refs[-2:]
    own = mm(pre_grad[...], first[...], ((1,), (1,)))
    other = mm(pre_grad[...], jnp.concatenate([piece[...] for piece in refs[:-2]], axis=0), ((1,), (1,)))
    half = chunks * slots
    message[:, :half] = outs[...]
    return_rows(group, chunks, slots, index[0] == 0, order, own, other, message, half)

    @pl.when(pl.program_id(0) == 0)
    def _():
        gain[...] = jnp.zeros_like(gain)

    part = own.shape[1]
    gain[:, :part] += jnp.sum(own * rows[:, :part].astype(F32), axis=0, keepdims=True)
    gain[:, part:] += jnp.sum(other * rows[:, part:].astype(F32), axis=0, keepdims=True)


def join(experts, replicas, kind, returned, joined):
    half = returned.shape[1] // 2
    for j in range(replicas):
        block = returned[j * experts : (j + 1) * experts, kind * half : (kind + 1) * half]
        joined[:, j * LANES : (j + 1) * LANES] = block.reshape(experts * half, LANES)
    return joined[...]


def to_tokens(chunks, values, chunk_of):
    return jnp.concatenate(
        [jnp.where(chunk_of == c, values, 0.0).astype(BF) for c in range(chunks)], axis=0
    )


def layer_kernel(experts, replicas, chunks, returned, x, gates, place, owner, chunk_of, slot_of, layer_out, joined):
    tokens, width = x.shape
    hits = slot_hits(place, owner, slot_of)
    source = join(experts, replicas, 0, returned, joined)
    mixed = 0.0
    for term in two_terms(gates[...]):
        weight = jnp.where(hits, spread((term,), owner[...]), 0.0)
        mixed = mixed + mm(to_tokens(chunks, weight, chunk_of[...]), source)
    for c in range(chunks):
        for j in range(replicas):
            at = feature(replicas, width, c, j)
            at = slice(at, at + LANES)
            here = mixed[c * tokens : (c + 1) * tokens, j * LANES : (j + 1) * LANES]
            layer_out[:, at] = (x[:, at].astype(F32) + here).astype(BF)


def in_grad_kernel(experts, replicas, chunks, returned, x, grad, gain, table, place, logit_grad,
                   owner, chunk_of, slot_of, in_grad, joined, normed_grad):
    tokens, width = x.shape
    ones = jnp.where(slot_hits(place, owner, slot_of), 1.0, 0.0)
    back = mm(to_tokens(chunks, ones, chunk_of[...]), join(experts, replicas, 1, returned, joined))
    high, low = two_terms(logit_grad[...])
    by_logits = mm(high, table[...], ((1,), (1,))) + mm(low, table[...], ((1,), (1,)))
    for c in range(chunks):
        for j in range(replicas):
            at = feature(replicas, width, c, j)
            at = slice(at, at + LANES)
            here = back[c * tokens : (c + 1) * tokens, j * LANES : (j + 1) * LANES]
            normed_grad[:, at] = here + by_logits[:, at]
    xw = x[...].astype(F32)
    inv_rms = lax.rsqrt(jnp.mean(xw * xw, axis=1, keepdims=True) + 1e-06)
    weighted = gain[...] * normed_grad[...]
    mean = jnp.mean(xw * weighted, axis=1, keepdims=True)
    in_grad[...] = (
        grad[...].astype(F32) + inv_rms * weighted - xw * (inv_rms * inv_rms * inv_rms * mean)
    ).astype(BF)


def after(value, *earlier):
    return lax.optimization_barrier((value,) + earlier)[0]


def swapped(block, axis):
    return lax.ppermute(block, axis, [(0, 1), (1, 0)])


def shards(section_input, routing, out_grad, norm_gain, router, w_in, w_out):
    experts = lax.axis_size("expert")
    replicas = lax.axis_size("dp")
    x = section_input[0]
    route_ids = routing[0]
    grad_top = out_grad[0]
    gain = norm_gain[0][None, :]
    table = router[0]
    first = w_in[0, 0]
    second = w_out[0, 0]
    tokens, width = x.shape
    part = first.shape[0]
    hidden_width = second.shape[0]
    slots = MOST
    rows = experts * slots
    router_width = table.shape[1]
    chunks = 2 * part // LANES
    half = chunks * slots
    peers = replicas * experts
    group = min(8, experts)
    message_shape = jax.ShapeDtypeStruct((peers, half, LANES), BF)
    side = lax.axis_index("half")
    index = side.astype(jnp.int32)[None]
    cuts = (0, part // 4, 7 * part // 8, part)
    first_other = tuple(swapped(first[a:b], "half") for a, b in zip(cuts, cuts[1:]))
    step_width = hidden_width // HIDDEN_STEPS
    cut = hidden_width - step_width
    second_early = swapped(second[:cut], "half")
    second_other = (second_early, swapped(after(second[cut:], second_early), "half"))

    at = np.arange(experts * half, dtype=np.int32)
    owner, chunk_of, slot_of = (at // half)[None], at % half // slots, (at % slots)[None]
    sizes = (experts, replicas, chunks, slots)
    token_scratch = [pltpu.VMEM((chunks * tokens, replicas * LANES), BF)]
    message, normed, place = kernel_call(
        functools.partial(send_kernel, *sizes),
        (
            message_shape,
            jax.ShapeDtypeStruct((tokens, width), BF),
            jax.ShapeDtypeStruct((tokens, router_width), F32),
        ),
        (x, route_ids, gain, owner, chunk_of[:, None], slot_of),
        token_scratch,
    )
    arrived = exchange(after(message, first_other[0]), SHARE)

    message, gates = kernel_call(
        functools.partial(send_grad_kernel, *sizes),
        (message_shape, jax.ShapeDtypeStruct((tokens, router_width), F32)),
        (normed, route_ids, grad_top, table, place, owner, chunk_of[:, None], slot_of),
        token_scratch,
    )
    message, arrived = lax.optimization_barrier((message, arrived, first_other[1]))[:2]
    arrived_grad = exchange(message, SHARE)

    at = np.arange(group * half, dtype=np.int32)
    into_messages = (at % half // slots * group + at // half) * slots + at % slots
    into_rows = np.zeros_like(at)
    into_rows[into_messages] = at
    all_rows = peers * slots
    whole = lambda shape: pl.BlockSpec(shape, lambda i: (0,) * len(shape))
    scalar = pl.BlockSpec(memory_space=pltpu.SMEM)

    sizes_other = tuple(piece.shape[0] for piece in first_other)

    def products(arrived, weights, side, steps, weight_specs):
        return kernel_call(
            functools.partial(products_kernel, group, chunks, slots, side),
            (
                jax.ShapeDtypeStruct((all_rows, steps * step_width), BF),
                jax.ShapeDtypeStruct((all_rows, 2 * part), BF),
            ),
            (index, arrived, into_rows[:, None]) + weights,
            grid=(steps,),
            in_specs=[scalar, whole(arrived.shape), whole((at.size, 1))] + weight_specs,
            out_specs=[pl.BlockSpec((all_rows, step_width), lambda i: (0, i)), whole((all_rows, 2 * part))],
        )

    partial, expert_rows = products(
        arrived,
        (first,) + first_other,
        0,
        2 * HIDDEN_STEPS,
        [pl.BlockSpec((size, step_width), lambda i: (0, i)) for size in (part,) + sizes_other],
    )
    partial = partial.reshape(replicas, rows, 2 * hidden_width)
    place_in_dp = lax.axis_index("dp")
    terms = [lax.dynamic_index_in_dim(partial, place_in_dp, 0, False)]
    for step in range(1, replicas):
        shift = [(j, (j + step) % replicas) for j in range(replicas)]
        block = lax.dynamic_index_in_dim(partial, (place_in_dp + step) % replicas, 0, False)
        terms.append(lax.ppermute(block, "dp", shift))
    partial, grad_rows = products(
        arrived_grad,
        (second,) + second_other,
        1,
        HIDDEN_STEPS,
        [
            pl.BlockSpec((step_width, part), lambda i: (i, 0)),
            pl.BlockSpec((step_width, part), lambda i: (jnp.minimum(i, HIDDEN_STEPS - 2), 0)),
            whole((step_width, part)),
        ],
    )
    terms = [after(term, partial) for term in terms]
    summands = exchange(partial.reshape(replicas, rows, hidden_width), "dp")
    pre_act = sum(term.astype(F32) for term in terms)
    gate_pre, up = pre_act[:, :hidden_width], pre_act[:, hidden_width:]
    hidden = (gate_pre / (1.0 + jnp.exp(-gate_pre)) * up).astype(BF)
    hidden_blocks = [hidden]
    for step in range(1, replicas):
        shift = [(j, (j + step) % replicas) for j in range(replicas)]
        hidden_blocks.append(lax.ppermute(hidden, "dp", shift))
    at = np.arange(rows, dtype=np.int32)
    pre_grad, worth = kernel_call(
        functools.partial(act_kernel, slots),
        (
            jax.ShapeDtypeStruct((rows, 2 * hidden_width), BF),
            jax.ShapeDtypeStruct((experts, LANES), F32),
        ),
        (summands, pre_act, hidden, at[None] // slots, at[:, None] % slots),
    )
    pre_grad_all = lax.all_gather(pre_grad, "dp", axis=0, tiled=True)
    hidden_blocks = [after(block, worth) for block in hidden_blocks]
    hidden_all = jnp.zeros((all_rows, hidden_width), BF)
    for step, block in enumerate(hidden_blocks):
        at_row = (place_in_dp + replicas - step) % replicas * rows
        hidden_all = lax.dynamic_update_slice(hidden_all, block, (at_row, 0))

    worth = exchange(worth[:, None], "expert")[:, 0, :slots]
    slot_ids = jnp.arange(slots, dtype=F32)
    gate_worth = jnp.sum(
        jnp.where(place[:, :experts, None] == slot_ids, worth[None], 0.0), axis=2
    )
    inner = jnp.sum(gate_worth, axis=1, keepdims=True)
    logit_grad = jnp.pad(gate_worth, ((0, 0), (0, router_width - experts))) - gates * inner
    logit_high, logit_low = two_terms(logit_grad)
    local_router = mm(normed, logit_high, ((0,), (0,))) + mm(normed, logit_low, ((0,), (0,)))
    local_router = local_router.astype(BF).reshape(experts, -1, router_width)
    second_other_grad = mm(hidden_all, grad_rows[:, part:], ((0,), (0,))).astype(BF)
    second_sent = swapped(second_other_grad, "half")
    local_router = after(local_router, second_other_grad)
    steps = 2 if all_rows // 2 % (2 * group * slots) == 0 else 1

    def by_rows(width):
        return pl.BlockSpec((all_rows // steps, width), lambda i: (i, 0))

    messages = pl.BlockSpec((peers // steps, half, LANES), lambda i: (i, 0, 0))
    order = into_messages[:, None]
    out_message = kernel_call(
        functools.partial(out_kernel, group, chunks, slots),
        message_shape,
        (index, hidden_all, order, second) + second_other,
        grid=(steps,),
        in_specs=[scalar, by_rows(hidden_width), whole(order.shape), whole(second.shape)]
        + [whole(piece.shape) for piece in second_other],
        out_specs=messages,
    )
    summed = exchange(local_router, "expert")
    router_part = jnp.sum(after(summed, out_message).astype(F32), axis=0)
    piece = router_part.shape[0] // (2 * replicas)
    router_part = exchange(router_part.reshape(2 * replicas, piece, router_width), ("half", "dp"))

    message, gain_part = kernel_call(
        functools.partial(back_kernel, group, chunks, slots),
        (jax.ShapeDtypeStruct((peers, 2 * half, LANES), BF), jax.ShapeDtypeStruct((1, 2 * part), F32)),
        (index, pre_grad_all, order, first, expert_rows, after(out_message, second_sent)) + first_other,
        grid=(steps,),
        in_specs=[
            scalar,
            by_rows(2 * hidden_width),
            whole(order.shape),
            whole(first.shape),
            by_rows(2 * part),
            messages,
            *(whole(piece.shape) for piece in first_other),
        ],
        out_specs=[
            pl.BlockSpec((peers // steps, 2 * half, LANES), lambda i: (i, 0, 0)),
            whole((1, 2 * part)),
        ],
    )
    router_own = jnp.sum(after(router_part, gain_part), axis=0)
    at = lax.axis_index("expert") * 2 * replicas + side * replicas + place_in_dp
    table_own = lax.dynamic_slice_in_dim(table, at * piece, piece, axis=0).astype(F32)
    gain_own = jnp.sum(router_own * table_own, axis=1)
    gain_part = gain_part.reshape(2, part)
    gain_part = jnp.where(side == 0, gain_part, gain_part[::-1])

    lines = 2 * part // LANES
    terms = three_terms(gain_part.reshape(lines, LANES))
    lone = [jnp.pad(term[None], ((0, 0), (0, LANES - piece))) for term in three_terms(gain_own)]
    block = jnp.concatenate([router_own.astype(BF), *terms, *lone], axis=0)
    block = jnp.pad(block, ((0, -block.shape[0] % 16), (0, 0)))
    owners = 2 * experts
    joined = exchange(jnp.broadcast_to(block[None], (owners,) + block.shape), OWNERS)
    first_other_grad = mm(expert_rows[:, part:], pre_grad_all, ((0,), (0,))).astype(BF)
    first_sent = swapped(first_other_grad, "half")
    message, joined = lax.optimization_barrier((message, joined, first_other_grad))[:2]
    returned = exchange(message, SHARE)
    end = piece + 3 * lines
    gain_rows = jnp.sum(joined[:, piece:end].astype(F32).reshape(owners, 3, lines, LANES), axis=(0, 1))
    lone = jnp.sum(joined[:, end : end + 3, :piece].astype(F32), axis=1).reshape(-1, LANES)
    sums = jnp.concatenate([*three_terms(gain_rows), *three_terms(lone)], axis=0)
    sums = jnp.pad(sums, ((0, -sums.shape[0] % 16), (0, 0)))
    packed = jnp.concatenate([joined[:, :piece].reshape(-1, LANES), sums], axis=0)
    packed = lax.all_gather(packed, "dp", axis=0)
    router_rows = owners * piece
    router_total = packed[:, :router_rows].reshape(replicas, 2, experts, piece, router_width)
    router_total = router_total.transpose(2, 1, 0, 3, 4).reshape(width, router_width)
    gain_rows = packed[:, router_rows : router_rows + 3 * lines].astype(F32)
    gain_rows = jnp.sum(gain_rows.reshape(replicas, 3, 2, part), axis=1)
    lone = packed[:, router_rows + 3 * lines : router_rows + 6 * lines].astype(F32)
    lone = jnp.sum(lone.reshape(replicas, 3, 2, experts, piece), axis=1)
    gain_total = gain_rows.transpose(1, 0, 2).reshape(width) + lone.transpose(2, 1, 0, 3).reshape(width)
    gain_total = gain_total / gain[0]

    second_own_grad = mm(hidden_all, grad_rows[:, :part], ((0,), (0,)))
    second_grad = (second_own_grad + second_sent.astype(F32)).astype(BF)
    first_own_grad = mm(expert_rows[:, :part], pre_grad_all, ((0,), (0,)))
    first_grad = (first_own_grad + first_sent.astype(F32)).astype(BF)

    token_shape = jax.ShapeDtypeStruct((tokens, width), BF)
    joined_scratch = pltpu.VMEM((experts * half, replicas * LANES), BF)
    layer_out = kernel_call(
        functools.partial(layer_kernel, experts, replicas, chunks),
        token_shape,
        (returned, after(x, second_grad), gates, place, owner, chunk_of[None], slot_of),
        [joined_scratch],
    )
    in_grad = kernel_call(
        functools.partial(in_grad_kernel, experts, replicas, chunks),
        token_shape,
        (returned, after(x, first_sent), grad_top, gain, table, place, logit_grad, owner, chunk_of[None], slot_of),
        [joined_scratch, pltpu.VMEM((tokens, width), F32)],
    )
    handoff = swapped(layer_out, "section")
    handback = swapped(in_grad, "section")
    return (
        handoff[None],
        handback[None],
        first_grad[None, None],
        second_grad[None, None],
        router_total[None],
        gain_total[None],
    )


def solution(mesh):
    sizes = mesh.shape
    halves = (sizes["section"], sizes["expert"], 2, sizes["dp"] // 2)
    split = Mesh(mesh.devices.reshape(halves), ("section", "expert", "half", "dp"))
    blocks = ("half", "dp")
    tokens = ("expert",) + blocks
    return jax.shard_map(
        shards,
        mesh=split,
        in_specs=(
            P("section", tokens, None),
            P("section", tokens, None),
            P("section", tokens, None),
            P("section", None),
            P("section", None, None),
            P("section", "expert", blocks, None),
            P("section", "expert", None, blocks),
        ),
        out_specs=(
            P("section", tokens, None),
            P("section", tokens, None),
            P("section", "expert", blocks, None),
            P("section", "expert", None, blocks),
            P("section", None, None),
            P("section", None),
        ),
        check_vma=False,
    )
```

```python
import functools

import jax
import jax.numpy as jnp
import numpy as np
from jax import lax
from jax.experimental import pallas as pl
from jax.experimental.pallas import tpu as pltpu
from jax.sharding import Mesh
from jax.sharding import PartitionSpec as P

MOST = 10
LANES = 128
BF = jnp.bfloat16
F32 = jnp.float32
SHARE = ("dp", "expert")
OWNERS = ("half", "expert")
INTERPRET = False
HIDDEN_STEPS = 3


def exchange(blocks, axes):
    return lax.all_to_all(blocks, axes, split_axis=0, concat_axis=0, tiled=True)


def mm(left, right, contract=((1,), (0,))):
    return lax.dot_general(left, right, (contract, ((), ())), preferred_element_type=F32)


def two_terms(values):
    high = values.astype(BF)
    return high, (values - high.astype(F32)).astype(BF)


def three_terms(values):
    high = values.astype(BF)
    return (high,) + two_terms(values - high.astype(F32))


def kernel_call(body, outs, args, scratch=(), **grid):
    return pl.pallas_call(
        body,
        out_shape=outs,
        scratch_shapes=scratch,
        compiler_params=pltpu.CompilerParams(vmem_limit_bytes=52 * 2**20),
        interpret=INTERPRET,
        **grid,
    )(*args)


def iota(shape, dimension):
    return lax.broadcasted_iota(jnp.int32, shape, dimension)


def spread(values, owner):
    pick = (iota((values[0].shape[1], owner.shape[1]), 0) == owner).astype(BF)
    total = mm(values[0], pick)
    for term in values[1:]:
        total = total + mm(term, pick)
    return total


def feature(replicas, width, c, j):
    part = width // (2 * replicas)
    block, inner = divmod(c * LANES, part)
    return (block * replicas + j) * part + inner


def picks_of(chunks, hits, chunk_of):
    rows = jnp.where(hits, 1.0, 0.0).T
    return jnp.concatenate(
        [jnp.where(chunk_of == c, rows, 0.0).astype(BF) for c in range(chunks)], axis=1
    )


def stacked(chunks, replicas, source, stack):
    tokens, width = source.shape
    for c in range(chunks):
        for j in range(replicas):
            at = feature(replicas, width, c, j)
            stack[c * tokens : (c + 1) * tokens, j * LANES : (j + 1) * LANES] = source[:, at : at + LANES]
    return stack[...]


def write_messages(experts, replicas, half, sent, message):
    for j in range(replicas):
        for e in range(experts):
            message[j * experts + e] = sent[e * half : (e + 1) * half, j * LANES : (j + 1) * LANES]


def slot_hits(place, owner, slot_of):
    return spread((place[...].astype(BF),), owner[...]) == slot_of[...].astype(F32)


def named_by(ids, shape):
    columns = iota(shape, 1)
    named = columns == ids[:, 0:1]
    for k in range(1, ids.shape[1]):
        named = named | (columns == ids[:, k : k + 1])
    return named


def send_kernel(experts, replicas, chunks, slots, x, ids, gain, owner, chunk_of, slot_of,
                message, normed, place, stack):
    tokens, width = x.shape
    xw = x[...].astype(F32)
    inv_rms = lax.rsqrt(jnp.mean(xw * xw, axis=1, keepdims=True) + 1e-06)
    normed[...] = (xw * inv_rms * gain[...]).astype(BF)
    named = named_by(ids, place.shape)
    earlier = (iota((tokens, tokens), 1) < iota((tokens, tokens), 0)).astype(BF)
    rank = mm(earlier, named.astype(BF))
    place[...] = jnp.where(named & (iota(place.shape, 1) < experts), rank, -1.0)
    pick = picks_of(chunks, slot_hits(place, owner, slot_of), chunk_of[...])
    sent = mm(pick, stacked(chunks, replicas, normed, stack)).astype(BF)
    write_messages(experts, replicas, chunks * slots, sent, message)


def send_grad_kernel(experts, replicas, chunks, slots, normed, ids, grad, table, place, owner, chunk_of, slot_of,
                     message, gates_out, stack):
    logits = mm(normed[...], table[...])
    powers = jnp.where(named_by(ids, logits.shape), jnp.exp(logits), 0.0)
    gates = powers / jnp.sum(powers, axis=1, keepdims=True)
    gates_out[...] = gates
    hits = slot_hits(place, owner, slot_of)
    weight = jnp.where(hits, spread(three_terms(gates), owner[...]), 0.0)
    slot_gate = jnp.sum(weight.T, axis=1, keepdims=True)
    pick = picks_of(chunks, hits, chunk_of[...])
    sent = (mm(pick, stacked(chunks, replicas, grad, stack)) * slot_gate).astype(BF)
    write_messages(experts, replicas, chunks * slots, sent, message)


def products_kernel(group, chunks, slots, side, index, arrived, order, *refs):
    weights, partial, rows_out = refs[:-2], refs[-2], refs[-1]
    half = chunks * slots
    size = group * half
    block = group * slots
    own_chunks = chunks // 2
    part = own_chunks * LANES

    @pl.when(pl.program_id(0) == 0)
    def _():
        lower = index[0] == 0
        pick = (order[...] == iota((size, size), 1)).astype(BF)
        for pair in range(arrived.shape[0] // group // 2):
            lanes = [
                arrived[(2 * pair + w) * group : (2 * pair + w + 1) * group].reshape(size, LANES)
                for w in range(2)
            ]
            picked = mm(pick, jnp.concatenate(lanes, axis=1)).astype(BF)
            for c in range(own_chunks):
                low = picked[c * block : (c + 1) * block]
                high = picked[(own_chunks + c) * block : (own_chunks + c + 1) * block]
                own = jnp.where(lower, low, high)
                other = jnp.where(lower, high, low)
                for w in range(2):
                    rows = slice((2 * pair + w) * block, (2 * pair + w + 1) * block)
                    lanes = slice(w * LANES, (w + 1) * LANES)
                    rows_out[rows, c * LANES : (c + 1) * LANES] = own[:, lanes]
                    rows_out[rows, part + c * LANES : part + (c + 1) * LANES] = other[:, lanes]

    if side == 0:
        weight = jnp.concatenate([piece[...] for piece in weights], axis=0)
    else:
        last = pl.program_id(0) == pl.num_programs(0) - 1
        own, early, late = weights
        weight = jnp.concatenate([own[...], jnp.where(last, late[...], early[...])], axis=1)
    partial[...] = mm(rows_out[...], weight, ((1,), (side,))).astype(BF)


def act_kernel(slots, arrived, pre_act, hidden, sender_of, slot_of, pre_grad, worth):
    replicas, rows, hidden_width = arrived.shape
    hidden_grad = arrived[0].astype(F32)
    for j in range(1, replicas):
        hidden_grad = hidden_grad + arrived[j].astype(F32)
    gate_pre, up = pre_act[:, :hidden_width], pre_act[:, hidden_width:]
    sigmoid = 1.0 / (1.0 + jnp.exp(-gate_pre))
    silu = gate_pre * sigmoid
    slope = sigmoid * (1.0 + gate_pre * (1.0 - sigmoid))
    pre_grad[:, :hidden_width] = (hidden_grad * up * slope).astype(BF)
    pre_grad[:, hidden_width:] = (hidden_grad * silu).astype(BF)
    each = jnp.sum(hidden_grad * hidden[...].astype(F32), axis=1, keepdims=True)
    laid = jnp.where(slot_of[...] == iota((rows, LANES), 1), each, 0.0)
    pick = (sender_of[...] == iota((worth.shape[0], rows), 0)).astype(BF)
    terms = three_terms(laid)
    worth[...] = mm(pick, terms[0]) + mm(pick, terms[1]) + mm(pick, terms[2])


def return_rows(group, chunks, slots, lower, order, own, other, message, first_row=0):
    block = group * slots
    half = chunks * slots
    size = group * half
    own_chunks = chunks // 2
    own, other = own.astype(BF), other.astype(BF)
    sides = jnp.where(lower, own, other), jnp.where(lower, other, own)
    pick = (order[...] == iota((size, size), 1)).astype(BF)

    def column(at):
        return jnp.concatenate(
            [
                side[at : at + block, c * LANES : (c + 1) * LANES]
                for side in sides
                for c in range(own_chunks)
            ],
            axis=0,
        )

    for pair in range(own.shape[0] // block // 2):
        lanes = [column((2 * pair + w) * block) for w in range(2)]
        picked = mm(pick, jnp.concatenate(lanes, axis=1)).astype(BF)
        for w in range(2):
            to = slice((2 * pair + w) * group, (2 * pair + w + 1) * group)
            message[to, first_row : first_row + half] = picked[:, w * LANES : (w + 1) * LANES].reshape(
                group, half, LANES
            )


def out_kernel(group, chunks, slots, index, hidden, order, second, early, late, message):
    own = mm(hidden[...], second[...])
    other = mm(hidden[...], jnp.concatenate([early[...], late[...]], axis=0))
    return_rows(group, chunks, slots, index[0] == 0, order, own, other, message)


def back_kernel(group, chunks, slots, index, pre_grad, order, first, rows, outs, *refs):
    message, gain = refs[-2:]
    own = mm(pre_grad[...], first[...], ((1,), (1,)))
    other = mm(pre_grad[...], jnp.concatenate([piece[...] for piece in refs[:-2]], axis=0), ((1,), (1,)))
    half = chunks * slots
    message[:, :half] = outs[...]
    return_rows(group, chunks, slots, index[0] == 0, order, own, other, message, half)

    @pl.when(pl.program_id(0) == 0)
    def _():
        gain[...] = jnp.zeros_like(gain)

    part = own.shape[1]
    gain[:, :part] += jnp.sum(own * rows[:, :part].astype(F32), axis=0, keepdims=True)
    gain[:, part:] += jnp.sum(other * rows[:, part:].astype(F32), axis=0, keepdims=True)


def join(experts, replicas, kind, returned, joined):
    half = returned.shape[1] // 2
    for j in range(replicas):
        block = returned[j * experts : (j + 1) * experts, kind * half : (kind + 1) * half]
        joined[:, j * LANES : (j + 1) * LANES] = block.reshape(experts * half, LANES)
    return joined[...]


def to_tokens(chunks, values, chunk_of):
    return jnp.concatenate(
        [jnp.where(chunk_of == c, values, 0.0).astype(BF) for c in range(chunks)], axis=0
    )


def layer_kernel(experts, replicas, chunks, returned, x, gates, place, owner, chunk_of, slot_of, layer_out, joined):
    tokens, width = x.shape
    hits = slot_hits(place, owner, slot_of)
    source = join(experts, replicas, 0, returned, joined)
    mixed = 0.0
    for term in two_terms(gates[...]):
        weight = jnp.where(hits, spread((term,), owner[...]), 0.0)
        mixed = mixed + mm(to_tokens(chunks, weight, chunk_of[...]), source)
    for c in range(chunks):
        for j in range(replicas):
            at = feature(replicas, width, c, j)
            at = slice(at, at + LANES)
            here = mixed[c * tokens : (c + 1) * tokens, j * LANES : (j + 1) * LANES]
            layer_out[:, at] = (x[:, at].astype(F32) + here).astype(BF)


def in_grad_kernel(experts, replicas, chunks, returned, x, grad, gain, table, place, logit_grad,
                   owner, chunk_of, slot_of, in_grad, joined, normed_grad):
    tokens, width = x.shape
    ones = jnp.where(slot_hits(place, owner, slot_of), 1.0, 0.0)
    back = mm(to_tokens(chunks, ones, chunk_of[...]), join(experts, replicas, 1, returned, joined))
    high, low = two_terms(logit_grad[...])
    by_logits = mm(high, table[...], ((1,), (1,))) + mm(low, table[...], ((1,), (1,)))
    for c in range(chunks):
        for j in range(replicas):
            at = feature(replicas, width, c, j)
            at = slice(at, at + LANES)
            here = back[c * tokens : (c + 1) * tokens, j * LANES : (j + 1) * LANES]
            normed_grad[:, at] = here + by_logits[:, at]
    xw = x[...].astype(F32)
    inv_rms = lax.rsqrt(jnp.mean(xw * xw, axis=1, keepdims=True) + 1e-06)
    weighted = gain[...] * normed_grad[...]
    mean = jnp.mean(xw * weighted, axis=1, keepdims=True)
    in_grad[...] = (
        grad[...].astype(F32) + inv_rms * weighted - xw * (inv_rms * inv_rms * inv_rms * mean)
    ).astype(BF)


def after(value, *earlier):
    return lax.optimization_barrier((value,) + earlier)[0]


def swapped(block, axis):
    return lax.ppermute(block, axis, [(0, 1), (1, 0)])


def shards(section_input, routing, out_grad, norm_gain, router, w_in, w_out):
    experts = lax.axis_size("expert")
    replicas = lax.axis_size("dp")
    x = section_input[0]
    route_ids = routing[0]
    grad_top = out_grad[0]
    gain = norm_gain[0][None, :]
    table = router[0]
    first = w_in[0, 0]
    second = w_out[0, 0]
    tokens, width = x.shape
    part = first.shape[0]
    hidden_width = second.shape[0]
    slots = MOST
    rows = experts * slots
    router_width = table.shape[1]
    chunks = 2 * part // LANES
    half = chunks * slots
    peers = replicas * experts
    group = min(8, experts)
    message_shape = jax.ShapeDtypeStruct((peers, half, LANES), BF)
    side = lax.axis_index("half")
    index = side.astype(jnp.int32)[None]
    cuts = (0, part // 4, 7 * part // 8, part)
    first_other = tuple(swapped(first[a:b], "half") for a, b in zip(cuts, cuts[1:]))
    step_width = hidden_width // HIDDEN_STEPS
    cut = hidden_width - step_width
    second_early = swapped(second[:cut], "half")
    second_other = (second_early, swapped(after(second[cut:], second_early), "half"))

    at = np.arange(experts * half, dtype=np.int32)
    owner, chunk_of, slot_of = (at // half)[None], at % half // slots, (at % slots)[None]
    sizes = (experts, replicas, chunks, slots)
    token_scratch = [pltpu.VMEM((chunks * tokens, replicas * LANES), BF)]
    message, normed, place = kernel_call(
        functools.partial(send_kernel, *sizes),
        (
            message_shape,
            jax.ShapeDtypeStruct((tokens, width), BF),
            jax.ShapeDtypeStruct((tokens, router_width), F32),
        ),
        (x, route_ids, gain, owner, chunk_of[:, None], slot_of),
        token_scratch,
    )
    arrived = exchange(after(message, first_other[0]), SHARE)

    message, gates = kernel_call(
        functools.partial(send_grad_kernel, *sizes),
        (message_shape, jax.ShapeDtypeStruct((tokens, router_width), F32)),
        (normed, route_ids, grad_top, table, place, owner, chunk_of[:, None], slot_of),
        token_scratch,
    )
    message, arrived = lax.optimization_barrier((message, arrived, first_other[1]))[:2]
    arrived_grad = exchange(message, SHARE)

    at = np.arange(group * half, dtype=np.int32)
    into_messages = (at % half // slots * group + at // half) * slots + at % slots
    into_rows = np.zeros_like(at)
    into_rows[into_messages] = at
    all_rows = peers * slots
    whole = lambda shape: pl.BlockSpec(shape, lambda i: (0,) * len(shape))
    scalar = pl.BlockSpec(memory_space=pltpu.SMEM)

    sizes_other = tuple(piece.shape[0] for piece in first_other)

    def products(arrived, weights, side, steps, weight_specs):
        return kernel_call(
            functools.partial(products_kernel, group, chunks, slots, side),
            (
                jax.ShapeDtypeStruct((all_rows, steps * step_width), BF),
                jax.ShapeDtypeStruct((all_rows, 2 * part), BF),
            ),
            (index, arrived, into_rows[:, None]) + weights,
            grid=(steps,),
            in_specs=[scalar, whole(arrived.shape), whole((at.size, 1))] + weight_specs,
            out_specs=[pl.BlockSpec((all_rows, step_width), lambda i: (0, i)), whole((all_rows, 2 * part))],
        )

    partial, expert_rows = products(
        arrived,
        (first,) + first_other,
        0,
        2 * HIDDEN_STEPS,
        [pl.BlockSpec((size, step_width), lambda i: (0, i)) for size in (part,) + sizes_other],
    )
    partial = partial.reshape(replicas, rows, 2 * hidden_width)
    place_in_dp = lax.axis_index("dp")
    terms = [lax.dynamic_index_in_dim(partial, place_in_dp, 0, False)]
    for step in range(1, replicas):
        shift = [(j, (j + step) % replicas) for j in range(replicas)]
        block = lax.dynamic_index_in_dim(partial, (place_in_dp + step) % replicas, 0, False)
        terms.append(lax.ppermute(block, "dp", shift))
    partial, grad_rows = products(
        arrived_grad,
        (second,) + second_other,
        1,
        HIDDEN_STEPS,
        [
            pl.BlockSpec((step_width, part), lambda i: (i, 0)),
            pl.BlockSpec((step_width, part), lambda i: (jnp.minimum(i, HIDDEN_STEPS - 2), 0)),
            whole((step_width, part)),
        ],
    )
    terms = [after(term, partial) for term in terms]
    summands = exchange(partial.reshape(replicas, rows, hidden_width), "dp")
    pre_act = sum(term.astype(F32) for term in terms)
    gate_pre, up = pre_act[:, :hidden_width], pre_act[:, hidden_width:]
    hidden = (gate_pre / (1.0 + jnp.exp(-gate_pre)) * up).astype(BF)
    hidden_blocks = [hidden]
    for step in range(1, replicas):
        shift = [(j, (j + step) % replicas) for j in range(replicas)]
        hidden_blocks.append(lax.ppermute(hidden, "dp", shift))
    at = np.arange(rows, dtype=np.int32)
    pre_grad, worth = kernel_call(
        functools.partial(act_kernel, slots),
        (
            jax.ShapeDtypeStruct((rows, 2 * hidden_width), BF),
            jax.ShapeDtypeStruct((experts, LANES), F32),
        ),
        (summands, pre_act, hidden, at[None] // slots, at[:, None] % slots),
    )
    pre_grad_all = lax.all_gather(pre_grad, "dp", axis=0, tiled=True)
    hidden_blocks = [after(block, worth) for block in hidden_blocks]
    hidden_all = jnp.zeros((all_rows, hidden_width), BF)
    for step, block in enumerate(hidden_blocks):
        at_row = (place_in_dp + replicas - step) % replicas * rows
        hidden_all = lax.dynamic_update_slice(hidden_all, block, (at_row, 0))

    worth = exchange(worth[:, None], "expert")[:, 0, :slots]
    slot_ids = jnp.arange(slots, dtype=F32)
    gate_worth = jnp.sum(
        jnp.where(place[:, :experts, None] == slot_ids, worth[None], 0.0), axis=2
    )
    inner = jnp.sum(gate_worth, axis=1, keepdims=True)
    logit_grad = jnp.pad(gate_worth, ((0, 0), (0, router_width - experts))) - gates * inner
    logit_high, logit_low = two_terms(logit_grad)
    local_router = mm(normed, logit_high, ((0,), (0,))) + mm(normed, logit_low, ((0,), (0,)))
    local_router = local_router.astype(BF).reshape(experts, -1, router_width)
    second_other_grad = mm(hidden_all, grad_rows[:, part:], ((0,), (0,))).astype(BF)
    second_sent = swapped(second_other_grad, "half")
    local_router = after(local_router, second_other_grad)
    steps = 2 if all_rows // 2 % (2 * group * slots) == 0 else 1

    def by_rows(width):
        return pl.BlockSpec((all_rows // steps, width), lambda i: (i, 0))

    messages = pl.BlockSpec((peers // steps, half, LANES), lambda i: (i, 0, 0))
    order = into_messages[:, None]
    out_message = kernel_call(
        functools.partial(out_kernel, group, chunks, slots),
        message_shape,
        (index, hidden_all, order, second) + second_other,
        grid=(steps,),
        in_specs=[scalar, by_rows(hidden_width), whole(order.shape), whole(second.shape)]
        + [whole(piece.shape) for piece in second_other],
        out_specs=messages,
    )
    summed = exchange(local_router, "expert")
    message, gain_part = kernel_call(
        functools.partial(back_kernel, group, chunks, slots),
        (jax.ShapeDtypeStruct((peers, 2 * half, LANES), BF), jax.ShapeDtypeStruct((1, 2 * part), F32)),
        (index, pre_grad_all, order, first, expert_rows, after(out_message, second_sent)) + first_other,
        grid=(steps,),
        in_specs=[
            scalar,
            by_rows(2 * hidden_width),
            whole(order.shape),
            whole(first.shape),
            by_rows(2 * part),
            messages,
            *(whole(piece.shape) for piece in first_other),
        ],
        out_specs=[
            pl.BlockSpec((peers // steps, 2 * half, LANES), lambda i: (i, 0, 0)),
            whole((1, 2 * part)),
        ],
    )
    gain_part = gain_part.reshape(2, part)
    gain_part = jnp.where(side == 0, gain_part, gain_part[::-1])

    lines = 2 * part // LANES
    block_rows = summed.shape[1]
    blocks = 2 * replicas
    partly = jnp.sum(after(summed, out_message, gain_part).astype(F32), axis=0).astype(BF)
    partly = jnp.concatenate([partly, *three_terms(gain_part.reshape(lines, LANES))], axis=0)
    partly = jnp.pad(partly, ((0, -partly.shape[0] % 16), (0, 0)))
    partly = exchange(jnp.broadcast_to(partly[None], (blocks,) + partly.shape), ("half", "dp"))
    first_other_grad = mm(expert_rows[:, part:], pre_grad_all, ((0,), (0,))).astype(BF)
    first_sent = swapped(first_other_grad, "half")
    returned = exchange(after(message, partly, first_other_grad), SHARE)
    router_block = jnp.sum(partly[:, :block_rows].astype(F32), axis=0)
    gain_rows = partly[:, block_rows : block_rows + 3 * lines].astype(F32)
    gain_rows = jnp.sum(gain_rows.reshape(2, replicas, 3, 2, part), axis=(0, 2))
    gain_rows = gain_rows.transpose(1, 0, 2).reshape(width)
    at = lax.axis_index("expert") * block_rows
    table_own = lax.dynamic_slice_in_dim(table, at, block_rows, axis=0).astype(F32)
    lone = jnp.sum(router_block * table_own, axis=1)
    gain_rows = gain_rows + lax.dynamic_update_slice(jnp.zeros((width,), F32), lone, (at,))
    terms = two_terms(gain_rows.reshape(-1, LANES))
    payload = jnp.concatenate([router_block.astype(BF), *terms], axis=0)
    payload = jnp.broadcast_to(payload[None], (experts,) + payload.shape)
    joined = exchange(after(payload, returned), "expert")
    router_total = joined[:, :block_rows].reshape(width, router_width)
    gain_total = jnp.sum(joined[:, block_rows:].astype(F32).reshape(experts, 2, width), axis=(0, 1)) / gain[0]

    second_own_grad = mm(hidden_all, grad_rows[:, :part], ((0,), (0,)))
    second_grad = (second_own_grad + second_sent.astype(F32)).astype(BF)

    token_shape = jax.ShapeDtypeStruct((tokens, width), BF)
    joined_scratch = pltpu.VMEM((experts * half, replicas * LANES), BF)
    layer_out = kernel_call(
        functools.partial(layer_kernel, experts, replicas, chunks),
        token_shape,
        (returned, after(x, second_grad), gates, place, owner, chunk_of[None], slot_of),
        [joined_scratch],
    )
    in_grad = kernel_call(
        functools.partial(in_grad_kernel, experts, replicas, chunks),
        token_shape,
        (returned, after(x, first_sent), grad_top, gain, table, place, logit_grad, owner, chunk_of[None], slot_of),
        [joined_scratch, pltpu.VMEM((tokens, width), F32)],
    )
    handoff = swapped(layer_out, "section")
    handback = swapped(in_grad, "section")
    first_own_grad = mm(expert_rows[:, :part], pre_grad_all, ((0,), (0,)))
    first_grad = (first_own_grad + after(first_sent, in_grad).astype(F32)).astype(BF)
    return (
        handoff[None],
        handback[None],
        first_grad[None, None],
        second_grad[None, None],
        router_total[None],
        gain_total[None],
    )


def solution(mesh):
    sizes = mesh.shape
    halves = (sizes["section"], sizes["expert"], 2, sizes["dp"] // 2)
    split = Mesh(mesh.devices.reshape(halves), ("section", "expert", "half", "dp"))
    blocks = ("half", "dp")
    tokens = ("expert",) + blocks
    return jax.shard_map(
        shards,
        mesh=split,
        in_specs=(
            P("section", tokens, None),
            P("section", tokens, None),
            P("section", tokens, None),
            P("section", None),
            P("section", None, None),
            P("section", "expert", blocks, None),
            P("section", "expert", None, blocks),
        ),
        out_specs=(
            P("section", tokens, None),
            P("section", tokens, None),
            P("section", "expert", blocks, None),
            P("section", "expert", None, blocks),
            P("section", None, None),
            P("section", None),
        ),
        check_vma=False,
    )
```

```python
import functools

import jax
import jax.numpy as jnp
import numpy as np
from jax import lax
from jax.experimental import pallas as pl
from jax.experimental.pallas import tpu as pltpu
from jax.sharding import Mesh
from jax.sharding import PartitionSpec as P

MOST = 10
LANES = 128
BF = jnp.bfloat16
F32 = jnp.float32
SHARE = ("dp", "expert")
OWNERS = ("half", "expert")
INTERPRET = False
HIDDEN_STEPS = 3


def exchange(blocks, axes):
    return lax.all_to_all(blocks, axes, split_axis=0, concat_axis=0, tiled=True)


def mm(left, right, contract=((1,), (0,))):
    return lax.dot_general(left, right, (contract, ((), ())), preferred_element_type=F32)


def two_terms(values):
    high = values.astype(BF)
    return high, (values - high.astype(F32)).astype(BF)


def three_terms(values):
    high = values.astype(BF)
    return (high,) + two_terms(values - high.astype(F32))


def kernel_call(body, outs, args, scratch=(), **grid):
    return pl.pallas_call(
        body,
        out_shape=outs,
        scratch_shapes=scratch,
        compiler_params=pltpu.CompilerParams(vmem_limit_bytes=52 * 2**20),
        interpret=INTERPRET,
        **grid,
    )(*args)


def iota(shape, dimension):
    return lax.broadcasted_iota(jnp.int32, shape, dimension)


def spread(values, owner):
    pick = (iota((values[0].shape[1], owner.shape[1]), 0) == owner).astype(BF)
    total = mm(values[0], pick)
    for term in values[1:]:
        total = total + mm(term, pick)
    return total


def feature(replicas, width, c, j):
    part = width // (2 * replicas)
    block, inner = divmod(c * LANES, part)
    return (block * replicas + j) * part + inner


def picks_of(chunks, hits, chunk_of):
    rows = jnp.where(hits, 1.0, 0.0).T
    return jnp.concatenate(
        [jnp.where(chunk_of == c, rows, 0.0).astype(BF) for c in range(chunks)], axis=1
    )


def stacked(chunks, replicas, source, stack):
    tokens, width = source.shape
    for c in range(chunks):
        for j in range(replicas):
            at = feature(replicas, width, c, j)
            stack[c * tokens : (c + 1) * tokens, j * LANES : (j + 1) * LANES] = source[:, at : at + LANES]
    return stack[...]


def write_messages(experts, replicas, half, sent, message):
    for j in range(replicas):
        for e in range(experts):
            message[j * experts + e] = sent[e * half : (e + 1) * half, j * LANES : (j + 1) * LANES]


def slot_hits(place, owner, slot_of):
    return spread((place[...].astype(BF),), owner[...]) == slot_of[...].astype(F32)


def named_by(ids, shape):
    columns = iota(shape, 1)
    named = columns == ids[:, 0:1]
    for k in range(1, ids.shape[1]):
        named = named | (columns == ids[:, k : k + 1])
    return named


def send_kernel(experts, replicas, chunks, slots, x, ids, gain, owner, chunk_of, slot_of,
                message, normed, place, stack):
    tokens, width = x.shape
    xw = x[...].astype(F32)
    inv_rms = lax.rsqrt(jnp.mean(xw * xw, axis=1, keepdims=True) + 1e-06)
    normed[...] = (xw * inv_rms * gain[...]).astype(BF)
    named = named_by(ids, place.shape)
    earlier = (iota((tokens, tokens), 1) < iota((tokens, tokens), 0)).astype(BF)
    rank = mm(earlier, named.astype(BF))
    place[...] = jnp.where(named & (iota(place.shape, 1) < experts), rank, -1.0)
    pick = picks_of(chunks, slot_hits(place, owner, slot_of), chunk_of[...])
    sent = mm(pick, stacked(chunks, replicas, normed, stack)).astype(BF)
    write_messages(experts, replicas, chunks * slots, sent, message)


def send_grad_kernel(experts, replicas, chunks, slots, normed, ids, grad, table, place, owner, chunk_of, slot_of,
                     message, gates_out, stack):
    logits = mm(normed[...], table[...])
    powers = jnp.where(named_by(ids, logits.shape), jnp.exp(logits), 0.0)
    gates = powers / jnp.sum(powers, axis=1, keepdims=True)
    gates_out[...] = gates
    hits = slot_hits(place, owner, slot_of)
    weight = jnp.where(hits, spread(three_terms(gates), owner[...]), 0.0)
    slot_gate = jnp.sum(weight.T, axis=1, keepdims=True)
    pick = picks_of(chunks, hits, chunk_of[...])
    sent = (mm(pick, stacked(chunks, replicas, grad, stack)) * slot_gate).astype(BF)
    write_messages(experts, replicas, chunks * slots, sent, message)


def products_kernel(group, chunks, slots, side, index, arrived, order, *refs):
    weights, partial, rows_out = refs[:-2], refs[-2], refs[-1]
    half = chunks * slots
    size = group * half
    block = group * slots
    own_chunks = chunks // 2
    part = own_chunks * LANES

    @pl.when(pl.program_id(0) == 0)
    def _():
        lower = index[0] == 0
        pick = (order[...] == iota((size, size), 1)).astype(BF)
        for pair in range(arrived.shape[0] // group // 2):
            lanes = [
                arrived[(2 * pair + w) * group : (2 * pair + w + 1) * group].reshape(size, LANES)
                for w in range(2)
            ]
            picked = mm(pick, jnp.concatenate(lanes, axis=1)).astype(BF)
            for c in range(own_chunks):
                low = picked[c * block : (c + 1) * block]
                high = picked[(own_chunks + c) * block : (own_chunks + c + 1) * block]
                own = jnp.where(lower, low, high)
                other = jnp.where(lower, high, low)
                for w in range(2):
                    rows = slice((2 * pair + w) * block, (2 * pair + w + 1) * block)
                    lanes = slice(w * LANES, (w + 1) * LANES)
                    rows_out[rows, c * LANES : (c + 1) * LANES] = own[:, lanes]
                    rows_out[rows, part + c * LANES : part + (c + 1) * LANES] = other[:, lanes]

    if side == 0:
        weight = jnp.concatenate([piece[...] for piece in weights], axis=0)
    else:
        last = pl.program_id(0) == pl.num_programs(0) - 1
        own, early, late = weights
        weight = jnp.concatenate([own[...], jnp.where(last, late[...], early[...])], axis=1)
    partial[...] = mm(rows_out[...], weight, ((1,), (side,))).astype(BF)


def act_kernel(slots, arrived, pre_act, hidden, sender_of, slot_of, pre_grad, worth):
    replicas, rows, hidden_width = arrived.shape
    hidden_grad = arrived[0].astype(F32)
    for j in range(1, replicas):
        hidden_grad = hidden_grad + arrived[j].astype(F32)
    gate_pre, up = pre_act[:, :hidden_width], pre_act[:, hidden_width:]
    sigmoid = 1.0 / (1.0 + jnp.exp(-gate_pre))
    silu = gate_pre * sigmoid
    slope = sigmoid * (1.0 + gate_pre * (1.0 - sigmoid))
    pre_grad[:, :hidden_width] = (hidden_grad * up * slope).astype(BF)
    pre_grad[:, hidden_width:] = (hidden_grad * silu).astype(BF)
    each = jnp.sum(hidden_grad * hidden[...].astype(F32), axis=1, keepdims=True)
    laid = jnp.where(slot_of[...] == iota((rows, LANES), 1), each, 0.0)
    pick = (sender_of[...] == iota((worth.shape[0], rows), 0)).astype(BF)
    terms = three_terms(laid)
    worth[...] = mm(pick, terms[0]) + mm(pick, terms[1]) + mm(pick, terms[2])


def return_rows(group, chunks, slots, lower, order, own, other, message, first_row=0):
    block = group * slots
    half = chunks * slots
    size = group * half
    own_chunks = chunks // 2
    own, other = own.astype(BF), other.astype(BF)
    sides = jnp.where(lower, own, other), jnp.where(lower, other, own)
    pick = (order[...] == iota((size, size), 1)).astype(BF)

    def column(at):
        return jnp.concatenate(
            [
                side[at : at + block, c * LANES : (c + 1) * LANES]
                for side in sides
                for c in range(own_chunks)
            ],
            axis=0,
        )

    for pair in range(own.shape[0] // block // 2):
        lanes = [column((2 * pair + w) * block) for w in range(2)]
        picked = mm(pick, jnp.concatenate(lanes, axis=1)).astype(BF)
        for w in range(2):
            to = slice((2 * pair + w) * group, (2 * pair + w + 1) * group)
            message[to, first_row : first_row + half] = picked[:, w * LANES : (w + 1) * LANES].reshape(
                group, half, LANES
            )


def out_kernel(group, chunks, slots, index, hidden, order, second, early, late, message):
    own = mm(hidden[...], second[...])
    other = mm(hidden[...], jnp.concatenate([early[...], late[...]], axis=0))
    return_rows(group, chunks, slots, index[0] == 0, order, own, other, message)


def back_kernel(group, chunks, slots, index, pre_grad, order, first, rows, outs, *refs):
    message, gain = refs[-2:]
    own = mm(pre_grad[...], first[...], ((1,), (1,)))
    other = mm(pre_grad[...], jnp.concatenate([piece[...] for piece in refs[:-2]], axis=0), ((1,), (1,)))
    half = chunks * slots
    message[:, :half] = outs[...]
    return_rows(group, chunks, slots, index[0] == 0, order, own, other, message, half)

    @pl.when(pl.program_id(0) == 0)
    def _():
        gain[...] = jnp.zeros_like(gain)

    part = own.shape[1]
    gain[:, :part] += jnp.sum(own * rows[:, :part].astype(F32), axis=0, keepdims=True)
    gain[:, part:] += jnp.sum(other * rows[:, part:].astype(F32), axis=0, keepdims=True)


def join(experts, replicas, kind, returned, joined):
    half = returned.shape[1] // 2
    for j in range(replicas):
        block = returned[j * experts : (j + 1) * experts, kind * half : (kind + 1) * half]
        joined[:, j * LANES : (j + 1) * LANES] = block.reshape(experts * half, LANES)
    return joined[...]


def to_tokens(chunks, values, chunk_of):
    return jnp.concatenate(
        [jnp.where(chunk_of == c, values, 0.0).astype(BF) for c in range(chunks)], axis=0
    )


def layer_kernel(experts, replicas, chunks, returned, x, gates, place, owner, chunk_of, slot_of, layer_out, joined):
    tokens, width = x.shape
    hits = slot_hits(place, owner, slot_of)
    source = join(experts, replicas, 0, returned, joined)
    mixed = 0.0
    for term in two_terms(gates[...]):
        weight = jnp.where(hits, spread((term,), owner[...]), 0.0)
        mixed = mixed + mm(to_tokens(chunks, weight, chunk_of[...]), source)
    for c in range(chunks):
        for j in range(replicas):
            at = feature(replicas, width, c, j)
            at = slice(at, at + LANES)
            here = mixed[c * tokens : (c + 1) * tokens, j * LANES : (j + 1) * LANES]
            layer_out[:, at] = (x[:, at].astype(F32) + here).astype(BF)


def in_grad_kernel(experts, replicas, chunks, returned, x, grad, gain, table, place, logit_grad,
                   owner, chunk_of, slot_of, in_grad, joined, normed_grad):
    tokens, width = x.shape
    ones = jnp.where(slot_hits(place, owner, slot_of), 1.0, 0.0)
    back = mm(to_tokens(chunks, ones, chunk_of[...]), join(experts, replicas, 1, returned, joined))
    high, low = two_terms(logit_grad[...])
    by_logits = mm(high, table[...], ((1,), (1,))) + mm(low, table[...], ((1,), (1,)))
    for c in range(chunks):
        for j in range(replicas):
            at = feature(replicas, width, c, j)
            at = slice(at, at + LANES)
            here = back[c * tokens : (c + 1) * tokens, j * LANES : (j + 1) * LANES]
            normed_grad[:, at] = here + by_logits[:, at]
    xw = x[...].astype(F32)
    inv_rms = lax.rsqrt(jnp.mean(xw * xw, axis=1, keepdims=True) + 1e-06)
    weighted = gain[...] * normed_grad[...]
    mean = jnp.mean(xw * weighted, axis=1, keepdims=True)
    in_grad[...] = (
        grad[...].astype(F32) + inv_rms * weighted - xw * (inv_rms * inv_rms * inv_rms * mean)
    ).astype(BF)


def after(value, *earlier):
    return lax.optimization_barrier((value,) + earlier)[0]


def swapped(block, axis):
    return lax.ppermute(block, axis, [(0, 1), (1, 0)])


def shards(section_input, routing, out_grad, norm_gain, router, w_in, w_out):
    experts = lax.axis_size("expert")
    replicas = lax.axis_size("dp")
    x = section_input[0]
    route_ids = routing[0]
    grad_top = out_grad[0]
    gain = norm_gain[0][None, :]
    table = router[0]
    first = w_in[0, 0]
    second = w_out[0, 0]
    tokens, width = x.shape
    part = first.shape[0]
    hidden_width = second.shape[0]
    slots = MOST
    rows = experts * slots
    router_width = table.shape[1]
    chunks = 2 * part // LANES
    half = chunks * slots
    peers = replicas * experts
    group = min(8, experts)
    message_shape = jax.ShapeDtypeStruct((peers, half, LANES), BF)
    side = lax.axis_index("half")
    index = side.astype(jnp.int32)[None]
    cuts = (0, part // 4, 7 * part // 8, part)
    first_other = tuple(swapped(first[a:b], "half") for a, b in zip(cuts, cuts[1:]))
    step_width = hidden_width // HIDDEN_STEPS
    cut = hidden_width - step_width
    second_early = swapped(second[:cut], "half")
    second_other = (second_early, swapped(after(second[cut:], second_early), "half"))

    at = np.arange(experts * half, dtype=np.int32)
    owner, chunk_of, slot_of = (at // half)[None], at % half // slots, (at % slots)[None]
    sizes = (experts, replicas, chunks, slots)
    token_scratch = [pltpu.VMEM((chunks * tokens, replicas * LANES), BF)]
    message, normed, place = kernel_call(
        functools.partial(send_kernel, *sizes),
        (
            message_shape,
            jax.ShapeDtypeStruct((tokens, width), BF),
            jax.ShapeDtypeStruct((tokens, router_width), F32),
        ),
        (x, route_ids, gain, owner, chunk_of[:, None], slot_of),
        token_scratch,
    )
    arrived = exchange(after(message, first_other[0]), SHARE)

    message, gates = kernel_call(
        functools.partial(send_grad_kernel, *sizes),
        (message_shape, jax.ShapeDtypeStruct((tokens, router_width), F32)),
        (normed, route_ids, grad_top, table, place, owner, chunk_of[:, None], slot_of),
        token_scratch,
    )
    message, arrived = lax.optimization_barrier((message, arrived, first_other[1]))[:2]
    arrived_grad = exchange(message, SHARE)

    at = np.arange(group * half, dtype=np.int32)
    into_messages = (at % half // slots * group + at // half) * slots + at % slots
    into_rows = np.zeros_like(at)
    into_rows[into_messages] = at
    all_rows = peers * slots
    whole = lambda shape: pl.BlockSpec(shape, lambda i: (0,) * len(shape))
    scalar = pl.BlockSpec(memory_space=pltpu.SMEM)

    sizes_other = tuple(piece.shape[0] for piece in first_other)

    def products(arrived, weights, side, steps, weight_specs):
        return kernel_call(
            functools.partial(products_kernel, group, chunks, slots, side),
            (
                jax.ShapeDtypeStruct((all_rows, steps * step_width), BF),
                jax.ShapeDtypeStruct((all_rows, 2 * part), BF),
            ),
            (index, arrived, into_rows[:, None]) + weights,
            grid=(steps,),
            in_specs=[scalar, whole(arrived.shape), whole((at.size, 1))] + weight_specs,
            out_specs=[pl.BlockSpec((all_rows, step_width), lambda i: (0, i)), whole((all_rows, 2 * part))],
        )

    partial, expert_rows = products(
        arrived,
        (first,) + first_other,
        0,
        2 * HIDDEN_STEPS,
        [pl.BlockSpec((size, step_width), lambda i: (0, i)) for size in (part,) + sizes_other],
    )
    partial = partial.reshape(replicas, rows, 2 * hidden_width)
    place_in_dp = lax.axis_index("dp")
    terms = [lax.dynamic_index_in_dim(partial, place_in_dp, 0, False)]
    for step in range(1, replicas):
        shift = [(j, (j + step) % replicas) for j in range(replicas)]
        block = lax.dynamic_index_in_dim(partial, (place_in_dp + step) % replicas, 0, False)
        terms.append(lax.ppermute(block, "dp", shift))
    partial, grad_rows = products(
        arrived_grad,
        (second,) + second_other,
        1,
        HIDDEN_STEPS,
        [
            pl.BlockSpec((step_width, part), lambda i: (i, 0)),
            pl.BlockSpec((step_width, part), lambda i: (jnp.minimum(i, HIDDEN_STEPS - 2), 0)),
            whole((step_width, part)),
        ],
    )
    terms = [after(term, partial) for term in terms]
    summands = exchange(partial.reshape(replicas, rows, hidden_width), "dp")
    pre_act = sum(term.astype(F32) for term in terms)
    gate_pre, up = pre_act[:, :hidden_width], pre_act[:, hidden_width:]
    hidden = (gate_pre / (1.0 + jnp.exp(-gate_pre)) * up).astype(BF)
    hidden_blocks = [hidden]
    for step in range(1, replicas):
        shift = [(j, (j + step) % replicas) for j in range(replicas)]
        hidden_blocks.append(lax.ppermute(hidden, "dp", shift))
    at = np.arange(rows, dtype=np.int32)
    pre_grad, worth = kernel_call(
        functools.partial(act_kernel, slots),
        (
            jax.ShapeDtypeStruct((rows, 2 * hidden_width), BF),
            jax.ShapeDtypeStruct((experts, LANES), F32),
        ),
        (summands, pre_act, hidden, at[None] // slots, at[:, None] % slots),
    )
    pre_grad_all = lax.all_gather(pre_grad, "dp", axis=0, tiled=True)

    worth = exchange(worth[:, None], "expert")[:, 0, :slots]
    slot_ids = jnp.arange(slots, dtype=F32)
    gate_worth = jnp.sum(
        jnp.where(place[:, :experts, None] == slot_ids, worth[None], 0.0), axis=2
    )
    inner = jnp.sum(gate_worth, axis=1, keepdims=True)
    logit_grad = jnp.pad(gate_worth, ((0, 0), (0, router_width - experts))) - gates * inner
    logit_high, logit_low = two_terms(logit_grad)
    local_router = mm(normed, logit_high, ((0,), (0,))) + mm(normed, logit_low, ((0,), (0,)))
    local_router = local_router.astype(BF).reshape(experts, -1, router_width)
    hidden_blocks = [after(block, local_router) for block in hidden_blocks]
    hidden_all = jnp.zeros((all_rows, hidden_width), BF)
    for step, block in enumerate(hidden_blocks):
        at_row = (place_in_dp + replicas - step) % replicas * rows
        hidden_all = lax.dynamic_update_slice(hidden_all, block, (at_row, 0))
    second_other_grad = mm(hidden_all, grad_rows[:, part:], ((0,), (0,))).astype(BF)
    second_sent = swapped(second_other_grad, "half")
    steps = 2 if all_rows // 2 % (2 * group * slots) == 0 else 1

    def by_rows(width):
        return pl.BlockSpec((all_rows // steps, width), lambda i: (i, 0))

    messages = pl.BlockSpec((peers // steps, half, LANES), lambda i: (i, 0, 0))
    order = into_messages[:, None]
    out_message = kernel_call(
        functools.partial(out_kernel, group, chunks, slots),
        message_shape,
        (index, hidden_all, order, second) + second_other,
        grid=(steps,),
        in_specs=[scalar, by_rows(hidden_width), whole(order.shape), whole(second.shape)]
        + [whole(piece.shape) for piece in second_other],
        out_specs=messages,
    )
    summed = exchange(local_router, "expert")
    message, gain_part = kernel_call(
        functools.partial(back_kernel, group, chunks, slots),
        (jax.ShapeDtypeStruct((peers, 2 * half, LANES), BF), jax.ShapeDtypeStruct((1, 2 * part), F32)),
        (index, pre_grad_all, order, first, expert_rows, out_message) + first_other,
        grid=(steps,),
        in_specs=[
            scalar,
            by_rows(2 * hidden_width),
            whole(order.shape),
            whole(first.shape),
            by_rows(2 * part),
            messages,
            *(whole(piece.shape) for piece in first_other),
        ],
        out_specs=[
            pl.BlockSpec((peers // steps, 2 * half, LANES), lambda i: (i, 0, 0)),
            whole((1, 2 * part)),
        ],
    )
    gain_part = gain_part.reshape(2, part)
    gain_part = jnp.where(side == 0, gain_part, gain_part[::-1])

    lines = 2 * part // LANES
    block_rows = summed.shape[1]
    blocks = 2 * replicas
    partly = jnp.sum(after(summed, out_message, gain_part).astype(F32), axis=0).astype(BF)
    partly = jnp.concatenate([partly, *three_terms(gain_part.reshape(lines, LANES))], axis=0)
    partly = jnp.pad(partly, ((0, -partly.shape[0] % 16), (0, 0)))
    partly = exchange(jnp.broadcast_to(partly[None], (blocks,) + partly.shape), ("half", "dp"))
    first_other_grad = mm(expert_rows[:, part:], pre_grad_all, ((0,), (0,))).astype(BF)
    first_sent = swapped(first_other_grad, "half")
    returned = exchange(after(message, partly, first_other_grad, second_sent), SHARE)
    router_block = jnp.sum(partly[:, :block_rows].astype(F32), axis=0)
    gain_rows = partly[:, block_rows : block_rows + 3 * lines].astype(F32)
    gain_rows = jnp.sum(gain_rows.reshape(2, replicas, 3, 2, part), axis=(0, 2))
    gain_rows = gain_rows.transpose(1, 0, 2).reshape(width)
    at = lax.axis_index("expert") * block_rows
    table_own = lax.dynamic_slice_in_dim(table, at, block_rows, axis=0).astype(F32)
    lone = jnp.sum(router_block * table_own, axis=1)
    gain_rows = gain_rows + lax.dynamic_update_slice(jnp.zeros((width,), F32), lone, (at,))
    terms = two_terms(gain_rows.reshape(-1, LANES))
    payload = jnp.concatenate([router_block.astype(BF), *terms], axis=0)
    joined = lax.all_gather(payload, "expert")
    router_total = joined[:, :block_rows].reshape(width, router_width)
    gain_total = jnp.sum(joined[:, block_rows:].astype(F32).reshape(experts, 2, width), axis=(0, 1)) / gain[0]

    second_own_grad = mm(hidden_all, grad_rows[:, :part], ((0,), (0,)))
    second_grad = (second_own_grad + second_sent.astype(F32)).astype(BF)

    token_shape = jax.ShapeDtypeStruct((tokens, width), BF)
    joined_scratch = pltpu.VMEM((experts * half, replicas * LANES), BF)
    layer_out = kernel_call(
        functools.partial(layer_kernel, experts, replicas, chunks),
        token_shape,
        (returned, after(x, second_grad), gates, place, owner, chunk_of[None], slot_of),
        [joined_scratch],
    )
    in_grad = kernel_call(
        functools.partial(in_grad_kernel, experts, replicas, chunks),
        token_shape,
        (returned, after(x, first_sent), grad_top, gain, table, place, logit_grad, owner, chunk_of[None], slot_of),
        [joined_scratch, pltpu.VMEM((tokens, width), F32)],
    )
    handoff = swapped(layer_out, "section")
    handback = swapped(in_grad, "section")
    first_own_grad = mm(expert_rows[:, :part], pre_grad_all, ((0,), (0,)))
    first_grad = (first_own_grad + after(first_sent, in_grad).astype(F32)).astype(BF)
    return (
        handoff[None],
        handback[None],
        first_grad[None, None],
        second_grad[None, None],
        router_total[None],
        gain_total[None],
    )


def solution(mesh):
    sizes = mesh.shape
    halves = (sizes["section"], sizes["expert"], 2, sizes["dp"] // 2)
    split = Mesh(mesh.devices.reshape(halves), ("section", "expert", "half", "dp"))
    blocks = ("half", "dp")
    tokens = ("expert",) + blocks
    return jax.shard_map(
        shards,
        mesh=split,
        in_specs=(
            P("section", tokens, None),
            P("section", tokens, None),
            P("section", tokens, None),
            P("section", None),
            P("section", None, None),
            P("section", "expert", blocks, None),
            P("section", "expert", None, blocks),
        ),
        out_specs=(
            P("section", tokens, None),
            P("section", tokens, None),
            P("section", "expert", blocks, None),
            P("section", "expert", None, blocks),
            P("section", None, None),
            P("section", None),
        ),
        check_vma=False,
    )
```

```python
import functools

import jax
import jax.numpy as jnp
import numpy as np
from jax import lax
from jax.experimental import pallas as pl
from jax.experimental.pallas import tpu as pltpu
from jax.sharding import Mesh
from jax.sharding import PartitionSpec as P

MOST = 10
LANES = 128
BF = jnp.bfloat16
F32 = jnp.float32
SHARE = ("dp", "expert")
OWNERS = ("half", "expert")
INTERPRET = False
HIDDEN_STEPS = 3


def exchange(blocks, axes):
    return lax.all_to_all(blocks, axes, split_axis=0, concat_axis=0, tiled=True)


def mm(left, right, contract=((1,), (0,))):
    return lax.dot_general(left, right, (contract, ((), ())), preferred_element_type=F32)


def two_terms(values):
    high = values.astype(BF)
    return high, (values - high.astype(F32)).astype(BF)


def three_terms(values):
    high = values.astype(BF)
    return (high,) + two_terms(values - high.astype(F32))


def kernel_call(body, outs, args, scratch=(), **grid):
    return pl.pallas_call(
        body,
        out_shape=outs,
        scratch_shapes=scratch,
        compiler_params=pltpu.CompilerParams(vmem_limit_bytes=52 * 2**20),
        interpret=INTERPRET,
        **grid,
    )(*args)


def iota(shape, dimension):
    return lax.broadcasted_iota(jnp.int32, shape, dimension)


def spread(values, owner):
    pick = (iota((values[0].shape[1], owner.shape[1]), 0) == owner).astype(BF)
    total = mm(values[0], pick)
    for term in values[1:]:
        total = total + mm(term, pick)
    return total


def feature(replicas, width, c, j):
    part = width // (2 * replicas)
    block, inner = divmod(c * LANES, part)
    return (block * replicas + j) * part + inner


def picks_of(chunks, hits, chunk_of):
    rows = jnp.where(hits, 1.0, 0.0).T
    return jnp.concatenate(
        [jnp.where(chunk_of == c, rows, 0.0).astype(BF) for c in range(chunks)], axis=1
    )


def stacked(chunks, replicas, source, stack):
    tokens, width = source.shape
    for c in range(chunks):
        for j in range(replicas):
            at = feature(replicas, width, c, j)
            stack[c * tokens : (c + 1) * tokens, j * LANES : (j + 1) * LANES] = source[:, at : at + LANES]
    return stack[...]


def write_messages(experts, replicas, half, sent, message):
    for j in range(replicas):
        for e in range(experts):
            message[j * experts + e] = sent[e * half : (e + 1) * half, j * LANES : (j + 1) * LANES]


def slot_hits(place, owner, slot_of):
    return spread((place[...].astype(BF),), owner[...]) == slot_of[...].astype(F32)


def named_by(ids, shape):
    columns = iota(shape, 1)
    named = columns == ids[:, 0:1]
    for k in range(1, ids.shape[1]):
        named = named | (columns == ids[:, k : k + 1])
    return named


def send_kernel(experts, replicas, chunks, slots, x, ids, gain, owner, chunk_of, slot_of,
                message, normed, place, stack):
    tokens, width = x.shape
    xw = x[...].astype(F32)
    inv_rms = lax.rsqrt(jnp.mean(xw * xw, axis=1, keepdims=True) + 1e-06)
    normed[...] = (xw * inv_rms * gain[...]).astype(BF)
    named = named_by(ids, place.shape)
    earlier = (iota((tokens, tokens), 1) < iota((tokens, tokens), 0)).astype(BF)
    rank = mm(earlier, named.astype(BF))
    place[...] = jnp.where(named & (iota(place.shape, 1) < experts), rank, -1.0)
    pick = picks_of(chunks, slot_hits(place, owner, slot_of), chunk_of[...])
    sent = mm(pick, stacked(chunks, replicas, normed, stack)).astype(BF)
    write_messages(experts, replicas, chunks * slots, sent, message)


def send_grad_kernel(experts, replicas, chunks, slots, normed, ids, grad, table, place, owner, chunk_of, slot_of,
                     message, gates_out, stack):
    logits = mm(normed[...], table[...])
    powers = jnp.where(named_by(ids, logits.shape), jnp.exp(logits), 0.0)
    gates = powers / jnp.sum(powers, axis=1, keepdims=True)
    gates_out[...] = gates
    hits = slot_hits(place, owner, slot_of)
    weight = jnp.where(hits, spread(three_terms(gates), owner[...]), 0.0)
    slot_gate = jnp.sum(weight.T, axis=1, keepdims=True)
    pick = picks_of(chunks, hits, chunk_of[...])
    sent = (mm(pick, stacked(chunks, replicas, grad, stack)) * slot_gate).astype(BF)
    write_messages(experts, replicas, chunks * slots, sent, message)


def products_kernel(group, chunks, slots, side, index, arrived, order, *refs):
    weights, partial, rows_out = refs[:-2], refs[-2], refs[-1]
    half = chunks * slots
    size = group * half
    block = group * slots
    own_chunks = chunks // 2
    part = own_chunks * LANES

    @pl.when(pl.program_id(0) == 0)
    def _():
        lower = index[0] == 0
        pick = (order[...] == iota((size, size), 1)).astype(BF)
        for pair in range(arrived.shape[0] // group // 2):
            lanes = [
                arrived[(2 * pair + w) * group : (2 * pair + w + 1) * group].reshape(size, LANES)
                for w in range(2)
            ]
            picked = mm(pick, jnp.concatenate(lanes, axis=1)).astype(BF)
            for c in range(own_chunks):
                low = picked[c * block : (c + 1) * block]
                high = picked[(own_chunks + c) * block : (own_chunks + c + 1) * block]
                own = jnp.where(lower, low, high)
                other = jnp.where(lower, high, low)
                for w in range(2):
                    rows = slice((2 * pair + w) * block, (2 * pair + w + 1) * block)
                    lanes = slice(w * LANES, (w + 1) * LANES)
                    rows_out[rows, c * LANES : (c + 1) * LANES] = own[:, lanes]
                    rows_out[rows, part + c * LANES : part + (c + 1) * LANES] = other[:, lanes]

    if side == 0:
        weight = jnp.concatenate([piece[...] for piece in weights], axis=0)
    else:
        last = pl.program_id(0) == pl.num_programs(0) - 1
        own, early, late = weights
        weight = jnp.concatenate([own[...], jnp.where(last, late[...], early[...])], axis=1)
    partial[...] = mm(rows_out[...], weight, ((1,), (side,))).astype(BF)


def act_kernel(slots, arrived, pre_act, hidden, sender_of, slot_of, pre_grad, worth):
    replicas, rows, hidden_width = arrived.shape
    hidden_grad = arrived[0].astype(F32)
    for j in range(1, replicas):
        hidden_grad = hidden_grad + arrived[j].astype(F32)
    gate_pre, up = pre_act[:, :hidden_width], pre_act[:, hidden_width:]
    sigmoid = 1.0 / (1.0 + jnp.exp(-gate_pre))
    silu = gate_pre * sigmoid
    slope = sigmoid * (1.0 + gate_pre * (1.0 - sigmoid))
    pre_grad[:, :hidden_width] = (hidden_grad * up * slope).astype(BF)
    pre_grad[:, hidden_width:] = (hidden_grad * silu).astype(BF)
    each = jnp.sum(hidden_grad * hidden[...].astype(F32), axis=1, keepdims=True)
    laid = jnp.where(slot_of[...] == iota((rows, LANES), 1), each, 0.0)
    pick = (sender_of[...] == iota((worth.shape[0], rows), 0)).astype(BF)
    terms = three_terms(laid)
    worth[...] = mm(pick, terms[0]) + mm(pick, terms[1]) + mm(pick, terms[2])


def return_rows(group, chunks, slots, lower, order, own, other, message, first_row=0):
    block = group * slots
    half = chunks * slots
    size = group * half
    own_chunks = chunks // 2
    own, other = own.astype(BF), other.astype(BF)
    sides = jnp.where(lower, own, other), jnp.where(lower, other, own)
    pick = (order[...] == iota((size, size), 1)).astype(BF)

    def column(at):
        return jnp.concatenate(
            [
                side[at : at + block, c * LANES : (c + 1) * LANES]
                for side in sides
                for c in range(own_chunks)
            ],
            axis=0,
        )

    for pair in range(own.shape[0] // block // 2):
        lanes = [column((2 * pair + w) * block) for w in range(2)]
        picked = mm(pick, jnp.concatenate(lanes, axis=1)).astype(BF)
        for w in range(2):
            to = slice((2 * pair + w) * group, (2 * pair + w + 1) * group)
            message[to, first_row : first_row + half] = picked[:, w * LANES : (w + 1) * LANES].reshape(
                group, half, LANES
            )


def out_kernel(group, chunks, slots, index, hidden, order, second, early, late, message):
    own = mm(hidden[...], second[...])
    other = mm(hidden[...], jnp.concatenate([early[...], late[...]], axis=0))
    return_rows(group, chunks, slots, index[0] == 0, order, own, other, message)


def back_kernel(group, chunks, slots, index, pre_grad, order, first, rows, outs, *refs):
    message, gain = refs[-2:]
    own = mm(pre_grad[...], first[...], ((1,), (1,)))
    other = mm(pre_grad[...], jnp.concatenate([piece[...] for piece in refs[:-2]], axis=0), ((1,), (1,)))
    half = chunks * slots
    message[:, :half] = outs[...]
    return_rows(group, chunks, slots, index[0] == 0, order, own, other, message, half)

    @pl.when(pl.program_id(0) == 0)
    def _():
        gain[...] = jnp.zeros_like(gain)

    part = own.shape[1]
    gain[:, :part] += jnp.sum(own * rows[:, :part].astype(F32), axis=0, keepdims=True)
    gain[:, part:] += jnp.sum(other * rows[:, part:].astype(F32), axis=0, keepdims=True)


def join(experts, replicas, kind, returned, joined):
    half = returned.shape[1] // 2
    for j in range(replicas):
        block = returned[j * experts : (j + 1) * experts, kind * half : (kind + 1) * half]
        joined[:, j * LANES : (j + 1) * LANES] = block.reshape(experts * half, LANES)
    return joined[...]


def to_tokens(chunks, values, chunk_of):
    return jnp.concatenate(
        [jnp.where(chunk_of == c, values, 0.0).astype(BF) for c in range(chunks)], axis=0
    )


def layer_kernel(experts, replicas, chunks, returned, x, gates, place, owner, chunk_of, slot_of, layer_out, joined):
    tokens, width = x.shape
    hits = slot_hits(place, owner, slot_of)
    source = join(experts, replicas, 0, returned, joined)
    mixed = 0.0
    for term in two_terms(gates[...]):
        weight = jnp.where(hits, spread((term,), owner[...]), 0.0)
        mixed = mixed + mm(to_tokens(chunks, weight, chunk_of[...]), source)
    for c in range(chunks):
        for j in range(replicas):
            at = feature(replicas, width, c, j)
            at = slice(at, at + LANES)
            here = mixed[c * tokens : (c + 1) * tokens, j * LANES : (j + 1) * LANES]
            layer_out[:, at] = (x[:, at].astype(F32) + here).astype(BF)


def in_grad_kernel(experts, replicas, chunks, returned, x, grad, gain, table, place, logit_grad,
                   owner, chunk_of, slot_of, in_grad, joined, normed_grad):
    tokens, width = x.shape
    ones = jnp.where(slot_hits(place, owner, slot_of), 1.0, 0.0)
    back = mm(to_tokens(chunks, ones, chunk_of[...]), join(experts, replicas, 1, returned, joined))
    high, low = two_terms(logit_grad[...])
    by_logits = mm(high, table[...], ((1,), (1,))) + mm(low, table[...], ((1,), (1,)))
    for c in range(chunks):
        for j in range(replicas):
            at = feature(replicas, width, c, j)
            at = slice(at, at + LANES)
            here = back[c * tokens : (c + 1) * tokens, j * LANES : (j + 1) * LANES]
            normed_grad[:, at] = here + by_logits[:, at]
    xw = x[...].astype(F32)
    inv_rms = lax.rsqrt(jnp.mean(xw * xw, axis=1, keepdims=True) + 1e-06)
    weighted = gain[...] * normed_grad[...]
    mean = jnp.mean(xw * weighted, axis=1, keepdims=True)
    in_grad[...] = (
        grad[...].astype(F32) + inv_rms * weighted - xw * (inv_rms * inv_rms * inv_rms * mean)
    ).astype(BF)


def after(value, *earlier):
    return lax.optimization_barrier((value,) + earlier)[0]


def swapped(block, axis):
    return lax.ppermute(block, axis, [(0, 1), (1, 0)])


def shards(section_input, routing, out_grad, norm_gain, router, w_in, w_out):
    experts = lax.axis_size("expert")
    replicas = lax.axis_size("dp")
    x = section_input[0]
    route_ids = routing[0]
    grad_top = out_grad[0]
    gain = norm_gain[0][None, :]
    table = router[0]
    first = w_in[0, 0]
    second = w_out[0, 0]
    tokens, width = x.shape
    part = first.shape[0]
    hidden_width = second.shape[0]
    slots = MOST
    rows = experts * slots
    router_width = table.shape[1]
    chunks = 2 * part // LANES
    half = chunks * slots
    peers = replicas * experts
    group = min(8, experts)
    message_shape = jax.ShapeDtypeStruct((peers, half, LANES), BF)
    side = lax.axis_index("half")
    index = side.astype(jnp.int32)[None]
    cuts = (0, part // 4, 7 * part // 8, part)
    first_other = tuple(swapped(first[a:b], "half") for a, b in zip(cuts, cuts[1:]))
    step_width = hidden_width // HIDDEN_STEPS
    cut = hidden_width - step_width
    second_early = swapped(second[:cut], "half")
    second_other = (second_early, swapped(after(second[cut:], second_early), "half"))

    at = np.arange(experts * half, dtype=np.int32)
    owner, chunk_of, slot_of = (at // half)[None], at % half // slots, (at % slots)[None]
    sizes = (experts, replicas, chunks, slots)
    token_scratch = [pltpu.VMEM((chunks * tokens, replicas * LANES), BF)]
    message, normed, place = kernel_call(
        functools.partial(send_kernel, *sizes),
        (
            message_shape,
            jax.ShapeDtypeStruct((tokens, width), BF),
            jax.ShapeDtypeStruct((tokens, router_width), F32),
        ),
        (x, route_ids, gain, owner, chunk_of[:, None], slot_of),
        token_scratch,
    )
    arrived = exchange(after(message, first_other[0]), SHARE)

    message, gates = kernel_call(
        functools.partial(send_grad_kernel, *sizes),
        (message_shape, jax.ShapeDtypeStruct((tokens, router_width), F32)),
        (normed, route_ids, grad_top, table, place, owner, chunk_of[:, None], slot_of),
        token_scratch,
    )
    message, arrived = lax.optimization_barrier((message, arrived, first_other[1]))[:2]
    arrived_grad = exchange(message, SHARE)

    at = np.arange(group * half, dtype=np.int32)
    into_messages = (at % half // slots * group + at // half) * slots + at % slots
    into_rows = np.zeros_like(at)
    into_rows[into_messages] = at
    all_rows = peers * slots
    whole = lambda shape: pl.BlockSpec(shape, lambda i: (0,) * len(shape))
    scalar = pl.BlockSpec(memory_space=pltpu.SMEM)

    sizes_other = tuple(piece.shape[0] for piece in first_other)

    def products(arrived, weights, side, steps, weight_specs):
        return kernel_call(
            functools.partial(products_kernel, group, chunks, slots, side),
            (
                jax.ShapeDtypeStruct((all_rows, steps * step_width), BF),
                jax.ShapeDtypeStruct((all_rows, 2 * part), BF),
            ),
            (index, arrived, into_rows[:, None]) + weights,
            grid=(steps,),
            in_specs=[scalar, whole(arrived.shape), whole((at.size, 1))] + weight_specs,
            out_specs=[pl.BlockSpec((all_rows, step_width), lambda i: (0, i)), whole((all_rows, 2 * part))],
        )

    partial, expert_rows = products(
        arrived,
        (first,) + first_other,
        0,
        2 * HIDDEN_STEPS,
        [pl.BlockSpec((size, step_width), lambda i: (0, i)) for size in (part,) + sizes_other],
    )
    partial = partial.reshape(replicas, rows, 2 * hidden_width)
    place_in_dp = lax.axis_index("dp")
    terms = [lax.dynamic_index_in_dim(partial, place_in_dp, 0, False)]
    for step in range(1, replicas):
        shift = [(j, (j + step) % replicas) for j in range(replicas)]
        block = lax.dynamic_index_in_dim(partial, (place_in_dp + step) % replicas, 0, False)
        terms.append(lax.ppermute(block, "dp", shift))
    partial, grad_rows = products(
        arrived_grad,
        (second,) + second_other,
        1,
        HIDDEN_STEPS,
        [
            pl.BlockSpec((step_width, part), lambda i: (i, 0)),
            pl.BlockSpec((step_width, part), lambda i: (jnp.minimum(i, HIDDEN_STEPS - 2), 0)),
            whole((step_width, part)),
        ],
    )
    terms = [after(term, partial) for term in terms]
    summands = exchange(partial.reshape(replicas, rows, hidden_width), "dp")
    pre_act = sum(term.astype(F32) for term in terms)
    gate_pre, up = pre_act[:, :hidden_width], pre_act[:, hidden_width:]
    hidden = (gate_pre / (1.0 + jnp.exp(-gate_pre)) * up).astype(BF)
    hidden_blocks = [hidden]
    for step in range(1, replicas):
        shift = [(j, (j + step) % replicas) for j in range(replicas)]
        hidden_blocks.append(lax.ppermute(hidden, "dp", shift))
    at = np.arange(rows, dtype=np.int32)
    pre_grad, worth = kernel_call(
        functools.partial(act_kernel, slots),
        (
            jax.ShapeDtypeStruct((rows, 2 * hidden_width), BF),
            jax.ShapeDtypeStruct((experts, LANES), F32),
        ),
        (summands, pre_act, hidden, at[None] // slots, at[:, None] % slots),
    )
    pre_grad_all = lax.all_gather(pre_grad, "dp", axis=0, tiled=True)

    hidden_blocks = [after(block, worth) for block in hidden_blocks]
    hidden_all = jnp.zeros((all_rows, hidden_width), BF)
    for step, block in enumerate(hidden_blocks):
        at_row = (place_in_dp + replicas - step) % replicas * rows
        hidden_all = lax.dynamic_update_slice(hidden_all, block, (at_row, 0))
    second_other_grad = mm(hidden_all, grad_rows[:, part:], ((0,), (0,))).astype(BF)
    second_sent = swapped(second_other_grad, "half")

    worth = exchange(worth[:, None], "expert")
    worth = after(worth, second_other_grad)[:, 0, :slots]
    slot_ids = jnp.arange(slots, dtype=F32)
    gate_worth = jnp.sum(
        jnp.where(place[:, :experts, None] == slot_ids, worth[None], 0.0), axis=2
    )
    inner = jnp.sum(gate_worth, axis=1, keepdims=True)
    logit_grad = jnp.pad(gate_worth, ((0, 0), (0, router_width - experts))) - gates * inner
    logit_high, logit_low = two_terms(logit_grad)
    local_router = mm(normed, logit_high, ((0,), (0,))) + mm(normed, logit_low, ((0,), (0,)))
    local_router = local_router.astype(BF).reshape(experts, -1, router_width)
    steps = 2 if all_rows // 2 % (2 * group * slots) == 0 else 1

    def by_rows(width):
        return pl.BlockSpec((all_rows // steps, width), lambda i: (i, 0))

    messages = pl.BlockSpec((peers // steps, half, LANES), lambda i: (i, 0, 0))
    order = into_messages[:, None]
    out_message = kernel_call(
        functools.partial(out_kernel, group, chunks, slots),
        message_shape,
        (index, hidden_all, order, second) + second_other,
        grid=(steps,),
        in_specs=[scalar, by_rows(hidden_width), whole(order.shape), whole(second.shape)]
        + [whole(piece.shape) for piece in second_other],
        out_specs=messages,
    )
    summed = exchange(local_router, "expert")

    message, gain_part = kernel_call(
        functools.partial(back_kernel, group, chunks, slots),
        (jax.ShapeDtypeStruct((peers, 2 * half, LANES), BF), jax.ShapeDtypeStruct((1, 2 * part), F32)),
        (index, pre_grad_all, order, first, expert_rows, out_message) + first_other,
        grid=(steps,),
        in_specs=[
            scalar,
            by_rows(2 * hidden_width),
            whole(order.shape),
            whole(first.shape),
            by_rows(2 * part),
            messages,
            *(whole(piece.shape) for piece in first_other),
        ],
        out_specs=[
            pl.BlockSpec((peers // steps, 2 * half, LANES), lambda i: (i, 0, 0)),
            whole((1, 2 * part)),
        ],
    )
    router_part = jnp.sum(after(summed, out_message, gain_part).astype(F32), axis=0)
    piece = router_part.shape[0] // (2 * replicas)
    router_part = exchange(router_part.reshape(2 * replicas, piece, router_width), ("half", "dp"))
    router_own = jnp.sum(after(router_part, second_sent), axis=0)
    at = lax.axis_index("expert") * 2 * replicas + side * replicas + place_in_dp
    table_own = lax.dynamic_slice_in_dim(table, at * piece, piece, axis=0).astype(F32)
    gain_own = jnp.sum(router_own * table_own, axis=1)
    gain_part = gain_part.reshape(2, part)
    gain_part = jnp.where(side == 0, gain_part, gain_part[::-1])

    lines = 2 * part // LANES
    terms = three_terms(gain_part.reshape(lines, LANES))
    lone = [jnp.pad(term[None], ((0, 0), (0, LANES - piece))) for term in three_terms(gain_own)]
    block = jnp.concatenate([router_own.astype(BF), *terms, *lone], axis=0)
    block = jnp.pad(block, ((0, -block.shape[0] % 16), (0, 0)))
    owners = 2 * experts
    joined = exchange(jnp.broadcast_to(block[None], (owners,) + block.shape), OWNERS)
    first_other_grad = mm(expert_rows[:, part:], pre_grad_all, ((0,), (0,))).astype(BF)
    first_sent = swapped(first_other_grad, "half")
    returned = exchange(after(message, joined, first_other_grad), SHARE)
    end = piece + 3 * lines
    gain_rows = jnp.sum(joined[:, piece:end].astype(F32).reshape(owners, 3, lines, LANES), axis=(0, 1))
    lone = jnp.sum(joined[:, end : end + 3, :piece].astype(F32), axis=1).reshape(-1, LANES)
    sums = jnp.concatenate([*three_terms(gain_rows), *three_terms(lone)], axis=0)
    sums = jnp.pad(sums, ((0, -sums.shape[0] % 16), (0, 0)))
    packed = jnp.concatenate([joined[:, :piece].reshape(-1, LANES), sums], axis=0)
    packed = lax.all_gather(packed, "dp", axis=0)

    second_own_grad = mm(hidden_all, grad_rows[:, :part], ((0,), (0,)))
    second_grad = (second_own_grad + second_sent.astype(F32)).astype(BF)
    first_own_grad = lax.optimization_barrier(mm(expert_rows[:, :part], pre_grad_all, ((0,), (0,))))

    token_shape = jax.ShapeDtypeStruct((tokens, width), BF)
    joined_scratch = pltpu.VMEM((experts * half, replicas * LANES), BF)
    layer_out = kernel_call(
        functools.partial(layer_kernel, experts, replicas, chunks),
        token_shape,
        (returned, after(x, second_grad, first_own_grad), gates, place, owner, chunk_of[None], slot_of),
        [joined_scratch],
    )
    in_grad = kernel_call(
        functools.partial(in_grad_kernel, experts, replicas, chunks),
        token_shape,
        (returned, after(x, first_sent), grad_top, gain, table, place, logit_grad, owner, chunk_of[None], slot_of),
        [joined_scratch, pltpu.VMEM((tokens, width), F32)],
    )
    handoff = swapped(layer_out, "section")
    handback = swapped(in_grad, "section")
    packed = after(packed, in_grad)
    router_rows = owners * piece
    router_total = packed[:, :router_rows].reshape(replicas, 2, experts, piece, router_width)
    router_total = router_total.transpose(2, 1, 0, 3, 4).reshape(width, router_width)
    gain_rows = packed[:, router_rows : router_rows + 3 * lines].astype(F32)
    gain_rows = jnp.sum(gain_rows.reshape(replicas, 3, 2, part), axis=1)
    lone = packed[:, router_rows + 3 * lines : router_rows + 6 * lines].astype(F32)
    lone = jnp.sum(lone.reshape(replicas, 3, 2, experts, piece), axis=1)
    gain_total = gain_rows.transpose(1, 0, 2).reshape(width) + lone.transpose(2, 1, 0, 3).reshape(width)
    gain_total = gain_total / gain[0]
    first_grad = (first_own_grad + after(first_sent, in_grad).astype(F32)).astype(BF)
    return (
        handoff[None],
        handback[None],
        first_grad[None, None],
        second_grad[None, None],
        router_total[None],
        gain_total[None],
    )


def solution(mesh):
    sizes = mesh.shape
    halves = (sizes["section"], sizes["expert"], 2, sizes["dp"] // 2)
    split = Mesh(mesh.devices.reshape(halves), ("section", "expert", "half", "dp"))
    blocks = ("half", "dp")
    tokens = ("expert",) + blocks
    return jax.shard_map(
        shards,
        mesh=split,
        in_specs=(
            P("section", tokens, None),
            P("section", tokens, None),
            P("section", tokens, None),
            P("section", None),
            P("section", None, None),
            P("section", "expert", blocks, None),
            P("section", "expert", None, blocks),
        ),
        out_specs=(
            P("section", tokens, None),
            P("section", tokens, None),
            P("section", "expert", blocks, None),
            P("section", "expert", None, blocks),
            P("section", None, None),
            P("section", None),
        ),
        check_vma=False,
    )
```

```python
import functools

import jax
import jax.numpy as jnp
import numpy as np
from jax import lax
from jax.experimental import pallas as pl
from jax.experimental.pallas import tpu as pltpu
from jax.sharding import Mesh
from jax.sharding import PartitionSpec as P

MOST = 10
LANES = 128
BF = jnp.bfloat16
F32 = jnp.float32
SHARE = ("dp", "expert")
OWNERS = ("half", "expert")
INTERPRET = False
HIDDEN_STEPS = 3


def exchange(blocks, axes):
    return lax.all_to_all(blocks, axes, split_axis=0, concat_axis=0, tiled=True)


def mm(left, right, contract=((1,), (0,))):
    return lax.dot_general(left, right, (contract, ((), ())), preferred_element_type=F32)


def two_terms(values):
    high = values.astype(BF)
    return high, (values - high.astype(F32)).astype(BF)


def three_terms(values):
    high = values.astype(BF)
    return (high,) + two_terms(values - high.astype(F32))


def kernel_call(body, outs, args, scratch=(), **grid):
    return pl.pallas_call(
        body,
        out_shape=outs,
        scratch_shapes=scratch,
        compiler_params=pltpu.CompilerParams(vmem_limit_bytes=52 * 2**20),
        interpret=INTERPRET,
        **grid,
    )(*args)


def iota(shape, dimension):
    return lax.broadcasted_iota(jnp.int32, shape, dimension)


def spread(values, owner):
    pick = (iota((values[0].shape[1], owner.shape[1]), 0) == owner).astype(BF)
    total = mm(values[0], pick)
    for term in values[1:]:
        total = total + mm(term, pick)
    return total


def feature(replicas, width, c, j):
    part = width // (2 * replicas)
    block, inner = divmod(c * LANES, part)
    return (block * replicas + j) * part + inner


def picks_of(chunks, hits, chunk_of):
    rows = jnp.where(hits, 1.0, 0.0).T
    return jnp.concatenate(
        [jnp.where(chunk_of == c, rows, 0.0).astype(BF) for c in range(chunks)], axis=1
    )


def stacked(chunks, replicas, source, stack):
    tokens, width = source.shape
    for c in range(chunks):
        for j in range(replicas):
            at = feature(replicas, width, c, j)
            stack[c * tokens : (c + 1) * tokens, j * LANES : (j + 1) * LANES] = source[:, at : at + LANES]
    return stack[...]


def write_messages(experts, replicas, half, sent, message):
    for j in range(replicas):
        for e in range(experts):
            message[j * experts + e] = sent[e * half : (e + 1) * half, j * LANES : (j + 1) * LANES]


def slot_hits(place, owner, slot_of):
    return spread((place[...].astype(BF),), owner[...]) == slot_of[...].astype(F32)


def named_by(ids, shape):
    columns = iota(shape, 1)
    named = columns == ids[:, 0:1]
    for k in range(1, ids.shape[1]):
        named = named | (columns == ids[:, k : k + 1])
    return named


def send_kernel(experts, replicas, chunks, slots, x, ids, gain, owner, chunk_of, slot_of,
                message, normed, place, stack):
    tokens, width = x.shape
    xw = x[...].astype(F32)
    inv_rms = lax.rsqrt(jnp.mean(xw * xw, axis=1, keepdims=True) + 1e-06)
    normed[...] = (xw * inv_rms * gain[...]).astype(BF)
    named = named_by(ids, place.shape)
    earlier = (iota((tokens, tokens), 1) < iota((tokens, tokens), 0)).astype(BF)
    rank = mm(earlier, named.astype(BF))
    place[...] = jnp.where(named & (iota(place.shape, 1) < experts), rank, -1.0)
    pick = picks_of(chunks, slot_hits(place, owner, slot_of), chunk_of[...])
    sent = mm(pick, stacked(chunks, replicas, normed, stack)).astype(BF)
    write_messages(experts, replicas, chunks * slots, sent, message)


def send_grad_kernel(experts, replicas, chunks, slots, normed, ids, grad, table, place, owner, chunk_of, slot_of,
                     message, gates_out, stack):
    logits = mm(normed[...], table[...])
    powers = jnp.where(named_by(ids, logits.shape), jnp.exp(logits), 0.0)
    gates = powers / jnp.sum(powers, axis=1, keepdims=True)
    gates_out[...] = gates
    hits = slot_hits(place, owner, slot_of)
    weight = jnp.where(hits, spread(three_terms(gates), owner[...]), 0.0)
    slot_gate = jnp.sum(weight.T, axis=1, keepdims=True)
    pick = picks_of(chunks, hits, chunk_of[...])
    sent = (mm(pick, stacked(chunks, replicas, grad, stack)) * slot_gate).astype(BF)
    write_messages(experts, replicas, chunks * slots, sent, message)


def products_kernel(group, chunks, slots, side, index, arrived, order, *refs):
    weights, partial, rows_out = refs[:-2], refs[-2], refs[-1]
    half = chunks * slots
    size = group * half
    block = group * slots
    own_chunks = chunks // 2
    part = own_chunks * LANES

    @pl.when(pl.program_id(0) == 0)
    def _():
        lower = index[0] == 0
        pick = (order[...] == iota((size, size), 1)).astype(BF)
        for pair in range(arrived.shape[0] // group // 2):
            lanes = [
                arrived[(2 * pair + w) * group : (2 * pair + w + 1) * group].reshape(size, LANES)
                for w in range(2)
            ]
            picked = mm(pick, jnp.concatenate(lanes, axis=1)).astype(BF)
            for c in range(own_chunks):
                low = picked[c * block : (c + 1) * block]
                high = picked[(own_chunks + c) * block : (own_chunks + c + 1) * block]
                own = jnp.where(lower, low, high)
                other = jnp.where(lower, high, low)
                for w in range(2):
                    rows = slice((2 * pair + w) * block, (2 * pair + w + 1) * block)
                    lanes = slice(w * LANES, (w + 1) * LANES)
                    rows_out[rows, c * LANES : (c + 1) * LANES] = own[:, lanes]
                    rows_out[rows, part + c * LANES : part + (c + 1) * LANES] = other[:, lanes]

    if side == 0:
        weight = jnp.concatenate([piece[...] for piece in weights], axis=0)
    else:
        last = pl.program_id(0) == pl.num_programs(0) - 1
        own, early, late = weights
        weight = jnp.concatenate([own[...], jnp.where(last, late[...], early[...])], axis=1)
    partial[...] = mm(rows_out[...], weight, ((1,), (side,))).astype(BF)


def act_kernel(slots, arrived, pre_act, hidden, sender_of, slot_of, pre_grad, worth):
    replicas, rows, hidden_width = arrived.shape
    hidden_grad = arrived[0].astype(F32)
    for j in range(1, replicas):
        hidden_grad = hidden_grad + arrived[j].astype(F32)
    gate_pre, up = pre_act[:, :hidden_width], pre_act[:, hidden_width:]
    sigmoid = 1.0 / (1.0 + jnp.exp(-gate_pre))
    silu = gate_pre * sigmoid
    slope = sigmoid * (1.0 + gate_pre * (1.0 - sigmoid))
    pre_grad[:, :hidden_width] = (hidden_grad * up * slope).astype(BF)
    pre_grad[:, hidden_width:] = (hidden_grad * silu).astype(BF)
    each = jnp.sum(hidden_grad * hidden[...].astype(F32), axis=1, keepdims=True)
    laid = jnp.where(slot_of[...] == iota((rows, LANES), 1), each, 0.0)
    pick = (sender_of[...] == iota((worth.shape[0], rows), 0)).astype(BF)
    terms = three_terms(laid)
    worth[...] = mm(pick, terms[0]) + mm(pick, terms[1]) + mm(pick, terms[2])


def return_rows(group, chunks, slots, lower, order, own, other, message, first_row=0):
    block = group * slots
    half = chunks * slots
    size = group * half
    own_chunks = chunks // 2
    own, other = own.astype(BF), other.astype(BF)
    sides = jnp.where(lower, own, other), jnp.where(lower, other, own)
    pick = (order[...] == iota((size, size), 1)).astype(BF)

    def column(at):
        return jnp.concatenate(
            [
                side[at : at + block, c * LANES : (c + 1) * LANES]
                for side in sides
                for c in range(own_chunks)
            ],
            axis=0,
        )

    for pair in range(own.shape[0] // block // 2):
        lanes = [column((2 * pair + w) * block) for w in range(2)]
        picked = mm(pick, jnp.concatenate(lanes, axis=1)).astype(BF)
        for w in range(2):
            to = slice((2 * pair + w) * group, (2 * pair + w + 1) * group)
            message[to, first_row : first_row + half] = picked[:, w * LANES : (w + 1) * LANES].reshape(
                group, half, LANES
            )


def out_kernel(group, chunks, slots, index, hidden, order, second, early, late, message):
    own = mm(hidden[...], second[...])
    other = mm(hidden[...], jnp.concatenate([early[...], late[...]], axis=0))
    return_rows(group, chunks, slots, index[0] == 0, order, own, other, message)


def back_kernel(group, chunks, slots, index, pre_grad, order, first, rows, outs, *refs):
    message, gain = refs[-2:]
    own = mm(pre_grad[...], first[...], ((1,), (1,)))
    other = mm(pre_grad[...], jnp.concatenate([piece[...] for piece in refs[:-2]], axis=0), ((1,), (1,)))
    half = chunks * slots
    message[:, :half] = outs[...]
    return_rows(group, chunks, slots, index[0] == 0, order, own, other, message, half)

    @pl.when(pl.program_id(0) == 0)
    def _():
        gain[...] = jnp.zeros_like(gain)

    part = own.shape[1]
    gain[:, :part] += jnp.sum(own * rows[:, :part].astype(F32), axis=0, keepdims=True)
    gain[:, part:] += jnp.sum(other * rows[:, part:].astype(F32), axis=0, keepdims=True)


def join(experts, replicas, kind, returned, joined):
    half = returned.shape[1] // 2
    for j in range(replicas):
        block = returned[j * experts : (j + 1) * experts, kind * half : (kind + 1) * half]
        joined[:, j * LANES : (j + 1) * LANES] = block.reshape(experts * half, LANES)
    return joined[...]


def to_tokens(chunks, values, chunk_of):
    return jnp.concatenate(
        [jnp.where(chunk_of == c, values, 0.0).astype(BF) for c in range(chunks)], axis=0
    )


def layer_kernel(experts, replicas, chunks, returned, x, gates, place, owner, chunk_of, slot_of, layer_out, joined):
    tokens, width = x.shape
    hits = slot_hits(place, owner, slot_of)
    source = join(experts, replicas, 0, returned, joined)
    mixed = 0.0
    for term in two_terms(gates[...]):
        weight = jnp.where(hits, spread((term,), owner[...]), 0.0)
        mixed = mixed + mm(to_tokens(chunks, weight, chunk_of[...]), source)
    for c in range(chunks):
        for j in range(replicas):
            at = feature(replicas, width, c, j)
            at = slice(at, at + LANES)
            here = mixed[c * tokens : (c + 1) * tokens, j * LANES : (j + 1) * LANES]
            layer_out[:, at] = (x[:, at].astype(F32) + here).astype(BF)


def in_grad_kernel(experts, replicas, chunks, returned, x, grad, gain, table, place, logit_grad,
                   owner, chunk_of, slot_of, in_grad, joined, normed_grad):
    tokens, width = x.shape
    ones = jnp.where(slot_hits(place, owner, slot_of), 1.0, 0.0)
    back = mm(to_tokens(chunks, ones, chunk_of[...]), join(experts, replicas, 1, returned, joined))
    high, low = two_terms(logit_grad[...])
    by_logits = mm(high, table[...], ((1,), (1,))) + mm(low, table[...], ((1,), (1,)))
    for c in range(chunks):
        for j in range(replicas):
            at = feature(replicas, width, c, j)
            at = slice(at, at + LANES)
            here = back[c * tokens : (c + 1) * tokens, j * LANES : (j + 1) * LANES]
            normed_grad[:, at] = here + by_logits[:, at]
    xw = x[...].astype(F32)
    inv_rms = lax.rsqrt(jnp.mean(xw * xw, axis=1, keepdims=True) + 1e-06)
    weighted = gain[...] * normed_grad[...]
    mean = jnp.mean(xw * weighted, axis=1, keepdims=True)
    in_grad[...] = (
        grad[...].astype(F32) + inv_rms * weighted - xw * (inv_rms * inv_rms * inv_rms * mean)
    ).astype(BF)


def after(value, *earlier):
    return lax.optimization_barrier((value,) + earlier)[0]


def swapped(block, axis):
    return lax.ppermute(block, axis, [(0, 1), (1, 0)])


def shards(section_input, routing, out_grad, norm_gain, router, w_in, w_out):
    experts = lax.axis_size("expert")
    replicas = lax.axis_size("dp")
    x = section_input[0]
    route_ids = routing[0]
    grad_top = out_grad[0]
    gain = norm_gain[0][None, :]
    table = router[0]
    first = w_in[0, 0]
    second = w_out[0, 0]
    tokens, width = x.shape
    part = first.shape[0]
    hidden_width = second.shape[0]
    slots = MOST
    rows = experts * slots
    router_width = table.shape[1]
    chunks = 2 * part // LANES
    half = chunks * slots
    peers = replicas * experts
    group = min(8, experts)
    message_shape = jax.ShapeDtypeStruct((peers, half, LANES), BF)
    side = lax.axis_index("half")
    index = side.astype(jnp.int32)[None]
    cuts = (0, part // 4, 7 * part // 8, part)
    first_other = tuple(swapped(first[a:b], "half") for a, b in zip(cuts, cuts[1:]))
    step_width = hidden_width // HIDDEN_STEPS
    cut = hidden_width - step_width
    second_early = swapped(second[:cut], "half")
    second_other = (second_early, swapped(after(second[cut:], second_early), "half"))

    at = np.arange(experts * half, dtype=np.int32)
    owner, chunk_of, slot_of = (at // half)[None], at % half // slots, (at % slots)[None]
    sizes = (experts, replicas, chunks, slots)
    token_scratch = [pltpu.VMEM((chunks * tokens, replicas * LANES), BF)]
    message, normed, place = kernel_call(
        functools.partial(send_kernel, *sizes),
        (
            message_shape,
            jax.ShapeDtypeStruct((tokens, width), BF),
            jax.ShapeDtypeStruct((tokens, router_width), F32),
        ),
        (x, route_ids, gain, owner, chunk_of[:, None], slot_of),
        token_scratch,
    )
    arrived = exchange(after(message, first_other[0]), SHARE)

    message, gates = kernel_call(
        functools.partial(send_grad_kernel, *sizes),
        (message_shape, jax.ShapeDtypeStruct((tokens, router_width), F32)),
        (normed, route_ids, grad_top, table, place, owner, chunk_of[:, None], slot_of),
        token_scratch,
    )
    message, arrived = lax.optimization_barrier((message, arrived, first_other[1]))[:2]
    arrived_grad = exchange(message, SHARE)

    at = np.arange(group * half, dtype=np.int32)
    into_messages = (at % half // slots * group + at // half) * slots + at % slots
    into_rows = np.zeros_like(at)
    into_rows[into_messages] = at
    all_rows = peers * slots
    whole = lambda shape: pl.BlockSpec(shape, lambda i: (0,) * len(shape))
    scalar = pl.BlockSpec(memory_space=pltpu.SMEM)

    sizes_other = tuple(piece.shape[0] for piece in first_other)

    def products(arrived, weights, side, steps, weight_specs):
        return kernel_call(
            functools.partial(products_kernel, group, chunks, slots, side),
            (
                jax.ShapeDtypeStruct((all_rows, steps * step_width), BF),
                jax.ShapeDtypeStruct((all_rows, 2 * part), BF),
            ),
            (index, arrived, into_rows[:, None]) + weights,
            grid=(steps,),
            in_specs=[scalar, whole(arrived.shape), whole((at.size, 1))] + weight_specs,
            out_specs=[pl.BlockSpec((all_rows, step_width), lambda i: (0, i)), whole((all_rows, 2 * part))],
        )

    partial, expert_rows = products(
        arrived,
        (first,) + first_other,
        0,
        2 * HIDDEN_STEPS,
        [pl.BlockSpec((size, step_width), lambda i: (0, i)) for size in (part,) + sizes_other],
    )
    partial = partial.reshape(replicas, rows, 2 * hidden_width)
    place_in_dp = lax.axis_index("dp")
    terms = [lax.dynamic_index_in_dim(partial, place_in_dp, 0, False)]
    for step in range(1, replicas):
        shift = [(j, (j + step) % replicas) for j in range(replicas)]
        block = lax.dynamic_index_in_dim(partial, (place_in_dp + step) % replicas, 0, False)
        terms.append(lax.ppermute(block, "dp", shift))
    partial, grad_rows = products(
        arrived_grad,
        (second,) + second_other,
        1,
        HIDDEN_STEPS,
        [
            pl.BlockSpec((step_width, part), lambda i: (i, 0)),
            pl.BlockSpec((step_width, part), lambda i: (jnp.minimum(i, HIDDEN_STEPS - 2), 0)),
            whole((step_width, part)),
        ],
    )
    terms = [after(term, partial) for term in terms]
    summands = exchange(partial.reshape(replicas, rows, hidden_width), "dp")
    pre_act = sum(term.astype(F32) for term in terms)
    gate_pre, up = pre_act[:, :hidden_width], pre_act[:, hidden_width:]
    hidden = (gate_pre / (1.0 + jnp.exp(-gate_pre)) * up).astype(BF)
    hidden_blocks = [hidden]
    for step in range(1, replicas):
        shift = [(j, (j + step) % replicas) for j in range(replicas)]
        hidden_blocks.append(lax.ppermute(hidden, "dp", shift))
    at = np.arange(rows, dtype=np.int32)
    pre_grad, worth = kernel_call(
        functools.partial(act_kernel, slots),
        (
            jax.ShapeDtypeStruct((rows, 2 * hidden_width), BF),
            jax.ShapeDtypeStruct((experts, LANES), F32),
        ),
        (summands, pre_act, hidden, at[None] // slots, at[:, None] % slots),
    )
    pre_grad_all = lax.all_gather(pre_grad, "dp", axis=0, tiled=True)

    hidden_blocks = [after(block, worth) for block in hidden_blocks]
    hidden_all = jnp.zeros((all_rows, hidden_width), BF)
    for step, block in enumerate(hidden_blocks):
        at_row = (place_in_dp + replicas - step) % replicas * rows
        hidden_all = lax.dynamic_update_slice(hidden_all, block, (at_row, 0))
    second_other_grad = mm(hidden_all, grad_rows[:, part:], ((0,), (0,))).astype(BF)
    second_sent = swapped(second_other_grad, "half")

    worth = exchange(worth[:, None], "expert")
    worth = after(worth, second_other_grad)[:, 0, :slots]
    slot_ids = jnp.arange(slots, dtype=F32)
    gate_worth = jnp.sum(
        jnp.where(place[:, :experts, None] == slot_ids, worth[None], 0.0), axis=2
    )
    inner = jnp.sum(gate_worth, axis=1, keepdims=True)
    logit_grad = jnp.pad(gate_worth, ((0, 0), (0, router_width - experts))) - gates * inner
    logit_high, logit_low = two_terms(logit_grad)
    local_router = mm(normed, logit_high, ((0,), (0,))) + mm(normed, logit_low, ((0,), (0,)))
    local_router = local_router.astype(BF).reshape(experts, -1, router_width)
    steps = 2 if all_rows // 2 % (2 * group * slots) == 0 else 1

    def by_rows(width):
        return pl.BlockSpec((all_rows // steps, width), lambda i: (i, 0))

    messages = pl.BlockSpec((peers // steps, half, LANES), lambda i: (i, 0, 0))
    order = into_messages[:, None]
    out_message = kernel_call(
        functools.partial(out_kernel, group, chunks, slots),
        message_shape,
        (index, hidden_all, order, second) + second_other,
        grid=(steps,),
        in_specs=[scalar, by_rows(hidden_width), whole(order.shape), whole(second.shape)]
        + [whole(piece.shape) for piece in second_other],
        out_specs=messages,
    )
    summed = exchange(local_router, "expert")

    message, gain_part = kernel_call(
        functools.partial(back_kernel, group, chunks, slots),
        (jax.ShapeDtypeStruct((peers, 2 * half, LANES), BF), jax.ShapeDtypeStruct((1, 2 * part), F32)),
        (index, pre_grad_all, order, first, expert_rows, out_message) + first_other,
        grid=(steps,),
        in_specs=[
            scalar,
            by_rows(2 * hidden_width),
            whole(order.shape),
            whole(first.shape),
            by_rows(2 * part),
            messages,
            *(whole(piece.shape) for piece in first_other),
        ],
        out_specs=[
            pl.BlockSpec((peers // steps, 2 * half, LANES), lambda i: (i, 0, 0)),
            whole((1, 2 * part)),
        ],
    )
    first_other_grad = mm(expert_rows[:, part:], pre_grad_all, ((0,), (0,))).astype(BF)
    first_sent = swapped(first_other_grad, "half")
    summed = after(summed, out_message, gain_part, first_other_grad)
    returned = exchange(after(message, summed, second_sent), SHARE)
    router_part = jnp.sum(summed.astype(F32), axis=0)
    piece = router_part.shape[0] // (2 * replicas)
    second_own_grad = mm(hidden_all, grad_rows[:, :part], ((0,), (0,)))
    second_grad = (second_own_grad + second_sent.astype(F32)).astype(BF)
    first_own_grad = lax.optimization_barrier(mm(expert_rows[:, :part], pre_grad_all, ((0,), (0,))))

    token_shape = jax.ShapeDtypeStruct((tokens, width), BF)
    joined_scratch = pltpu.VMEM((experts * half, replicas * LANES), BF)
    layer_out = kernel_call(
        functools.partial(layer_kernel, experts, replicas, chunks),
        token_shape,
        (returned, after(x, second_grad, first_own_grad), gates, place, owner, chunk_of[None], slot_of),
        [joined_scratch],
    )
    router_part = after(router_part, returned, second_grad, first_own_grad).reshape(2 * replicas, piece, router_width)
    router_part = exchange(router_part, ("half", "dp"))
    router_own = jnp.sum(after(router_part, layer_out), axis=0)
    at = lax.axis_index("expert") * 2 * replicas + side * replicas + place_in_dp
    table_own = lax.dynamic_slice_in_dim(table, at * piece, piece, axis=0).astype(F32)
    gain_own = jnp.sum(router_own * table_own, axis=1)
    gain_part = gain_part.reshape(2, part)
    gain_part = jnp.where(side == 0, gain_part, gain_part[::-1])

    lines = 2 * part // LANES
    terms = three_terms(gain_part.reshape(lines, LANES))
    lone = [jnp.pad(term[None], ((0, 0), (0, LANES - piece))) for term in three_terms(gain_own)]
    block = jnp.concatenate([router_own.astype(BF), *terms, *lone], axis=0)
    block = jnp.pad(block, ((0, -block.shape[0] % 16), (0, 0)))
    owners = 2 * experts
    joined = exchange(jnp.broadcast_to(block[None], (owners,) + block.shape), OWNERS)
    end = piece + 3 * lines
    gain_rows = jnp.sum(joined[:, piece:end].astype(F32).reshape(owners, 3, lines, LANES), axis=(0, 1))
    lone = jnp.sum(joined[:, end : end + 3, :piece].astype(F32), axis=1).reshape(-1, LANES)
    sums = jnp.concatenate([*three_terms(gain_rows), *three_terms(lone)], axis=0)
    sums = jnp.pad(sums, ((0, -sums.shape[0] % 16), (0, 0)))
    packed = jnp.concatenate([joined[:, :piece].reshape(-1, LANES), sums], axis=0)
    packed = exchange(jnp.broadcast_to(packed[None], (replicas,) + packed.shape), "dp")

    in_grad = kernel_call(
        functools.partial(in_grad_kernel, experts, replicas, chunks),
        token_shape,
        (returned, after(x, first_sent), grad_top, gain, table, place, logit_grad, owner, chunk_of[None], slot_of),
        [joined_scratch, pltpu.VMEM((tokens, width), F32)],
    )
    handoff = swapped(layer_out, "section")
    handback = swapped(in_grad, "section")
    router_rows = owners * piece
    router_total = packed[:, :router_rows].reshape(replicas, 2, experts, piece, router_width)
    router_total = router_total.transpose(2, 1, 0, 3, 4).reshape(width, router_width)
    gain_rows = packed[:, router_rows : router_rows + 3 * lines].astype(F32)
    gain_rows = jnp.sum(gain_rows.reshape(replicas, 3, 2, part), axis=1)
    lone = packed[:, router_rows + 3 * lines : router_rows + 6 * lines].astype(F32)
    lone = jnp.sum(lone.reshape(replicas, 3, 2, experts, piece), axis=1)
    gain_total = gain_rows.transpose(1, 0, 2).reshape(width) + lone.transpose(2, 1, 0, 3).reshape(width)
    gain_total = gain_total / gain[0]
    first_grad = (first_own_grad + after(first_sent, in_grad).astype(F32)).astype(BF)
    return (
        handoff[None],
        handback[None],
        first_grad[None, None],
        second_grad[None, None],
        router_total[None],
        gain_total[None],
    )


def solution(mesh):
    sizes = mesh.shape
    halves = (sizes["section"], sizes["expert"], 2, sizes["dp"] // 2)
    split = Mesh(mesh.devices.reshape(halves), ("section", "expert", "half", "dp"))
    blocks = ("half", "dp")
    tokens = ("expert",) + blocks
    return jax.shard_map(
        shards,
        mesh=split,
        in_specs=(
            P("section", tokens, None),
            P("section", tokens, None),
            P("section", tokens, None),
            P("section", None),
            P("section", None, None),
            P("section", "expert", blocks, None),
            P("section", "expert", None, blocks),
        ),
        out_specs=(
            P("section", tokens, None),
            P("section", tokens, None),
            P("section", "expert", blocks, None),
            P("section", "expert", None, blocks),
            P("section", None, None),
            P("section", None),
        ),
        check_vma=False,
    )
```

```python
import functools

import jax
import jax.numpy as jnp
import numpy as np
from jax import lax
from jax.experimental import pallas as pl
from jax.experimental.pallas import tpu as pltpu
from jax.sharding import Mesh
from jax.sharding import PartitionSpec as P

MOST = 10
LANES = 128
BF = jnp.bfloat16
F32 = jnp.float32
SHARE = ("dp", "expert")
OWNERS = ("half", "expert")
INTERPRET = False
HIDDEN_STEPS = 3


def exchange(blocks, axes):
    return lax.all_to_all(blocks, axes, split_axis=0, concat_axis=0, tiled=True)


def mm(left, right, contract=((1,), (0,))):
    return lax.dot_general(left, right, (contract, ((), ())), preferred_element_type=F32)


def two_terms(values):
    high = values.astype(BF)
    return high, (values - high.astype(F32)).astype(BF)


def three_terms(values):
    high = values.astype(BF)
    return (high,) + two_terms(values - high.astype(F32))


def kernel_call(body, outs, args, scratch=(), **grid):
    return pl.pallas_call(
        body,
        out_shape=outs,
        scratch_shapes=scratch,
        compiler_params=pltpu.CompilerParams(vmem_limit_bytes=52 * 2**20),
        interpret=INTERPRET,
        **grid,
    )(*args)


def iota(shape, dimension):
    return lax.broadcasted_iota(jnp.int32, shape, dimension)


def spread(values, owner):
    pick = (iota((values[0].shape[1], owner.shape[1]), 0) == owner).astype(BF)
    total = mm(values[0], pick)
    for term in values[1:]:
        total = total + mm(term, pick)
    return total


def feature(replicas, width, c, j):
    part = width // (2 * replicas)
    block, inner = divmod(c * LANES, part)
    return (block * replicas + j) * part + inner


def picks_of(chunks, hits, chunk_of):
    rows = jnp.where(hits, 1.0, 0.0).T
    return jnp.concatenate(
        [jnp.where(chunk_of == c, rows, 0.0).astype(BF) for c in range(chunks)], axis=1
    )


def stacked(chunks, replicas, source, stack):
    tokens, width = source.shape
    for c in range(chunks):
        for j in range(replicas):
            at = feature(replicas, width, c, j)
            stack[c * tokens : (c + 1) * tokens, j * LANES : (j + 1) * LANES] = source[:, at : at + LANES]
    return stack[...]


def write_messages(experts, replicas, half, sent, message):
    for j in range(replicas):
        for e in range(experts):
            message[j * experts + e] = sent[e * half : (e + 1) * half, j * LANES : (j + 1) * LANES]


def slot_hits(place, owner, slot_of):
    return spread((place[...].astype(BF),), owner[...]) == slot_of[...].astype(F32)


def named_by(ids, shape):
    columns = iota(shape, 1)
    named = columns == ids[:, 0:1]
    for k in range(1, ids.shape[1]):
        named = named | (columns == ids[:, k : k + 1])
    return named


def send_kernel(experts, replicas, chunks, slots, x, ids, gain, owner, chunk_of, slot_of,
                message, normed, place, stack):
    tokens, width = x.shape
    xw = x[...].astype(F32)
    inv_rms = lax.rsqrt(jnp.mean(xw * xw, axis=1, keepdims=True) + 1e-06)
    normed[...] = (xw * inv_rms * gain[...]).astype(BF)
    named = named_by(ids, place.shape)
    earlier = (iota((tokens, tokens), 1) < iota((tokens, tokens), 0)).astype(BF)
    rank = mm(earlier, named.astype(BF))
    place[...] = jnp.where(named & (iota(place.shape, 1) < experts), rank, -1.0)
    pick = picks_of(chunks, slot_hits(place, owner, slot_of), chunk_of[...])
    sent = mm(pick, stacked(chunks, replicas, normed, stack)).astype(BF)
    write_messages(experts, replicas, chunks * slots, sent, message)


def send_grad_kernel(experts, replicas, chunks, slots, normed, ids, grad, table, place, owner, chunk_of, slot_of,
                     message, gates_out, stack):
    logits = mm(normed[...], table[...])
    powers = jnp.where(named_by(ids, logits.shape), jnp.exp(logits), 0.0)
    gates = powers / jnp.sum(powers, axis=1, keepdims=True)
    gates_out[...] = gates
    hits = slot_hits(place, owner, slot_of)
    weight = jnp.where(hits, spread(three_terms(gates), owner[...]), 0.0)
    slot_gate = jnp.sum(weight.T, axis=1, keepdims=True)
    pick = picks_of(chunks, hits, chunk_of[...])
    sent = (mm(pick, stacked(chunks, replicas, grad, stack)) * slot_gate).astype(BF)
    write_messages(experts, replicas, chunks * slots, sent, message)


def products_kernel(group, chunks, slots, side, index, arrived, order, *refs):
    weights, partial, rows_out = refs[:-2], refs[-2], refs[-1]
    half = chunks * slots
    size = group * half
    block = group * slots
    own_chunks = chunks // 2
    part = own_chunks * LANES

    @pl.when(pl.program_id(0) == 0)
    def _():
        lower = index[0] == 0
        pick = (order[...] == iota((size, size), 1)).astype(BF)
        for pair in range(arrived.shape[0] // group // 2):
            lanes = [
                arrived[(2 * pair + w) * group : (2 * pair + w + 1) * group].reshape(size, LANES)
                for w in range(2)
            ]
            picked = mm(pick, jnp.concatenate(lanes, axis=1)).astype(BF)
            for c in range(own_chunks):
                low = picked[c * block : (c + 1) * block]
                high = picked[(own_chunks + c) * block : (own_chunks + c + 1) * block]
                own = jnp.where(lower, low, high)
                other = jnp.where(lower, high, low)
                for w in range(2):
                    rows = slice((2 * pair + w) * block, (2 * pair + w + 1) * block)
                    lanes = slice(w * LANES, (w + 1) * LANES)
                    rows_out[rows, c * LANES : (c + 1) * LANES] = own[:, lanes]
                    rows_out[rows, part + c * LANES : part + (c + 1) * LANES] = other[:, lanes]

    if side == 0:
        weight = jnp.concatenate([piece[...] for piece in weights], axis=0)
    else:
        last = pl.program_id(0) == pl.num_programs(0) - 1
        own, early, late = weights
        weight = jnp.concatenate([own[...], jnp.where(last, late[...], early[...])], axis=1)
    partial[...] = mm(rows_out[...], weight, ((1,), (side,))).astype(BF)


def act_kernel(slots, arrived, pre_act, hidden, sender_of, slot_of, pre_grad, worth):
    replicas, rows, hidden_width = arrived.shape
    hidden_grad = arrived[0].astype(F32)
    for j in range(1, replicas):
        hidden_grad = hidden_grad + arrived[j].astype(F32)
    gate_pre, up = pre_act[:, :hidden_width], pre_act[:, hidden_width:]
    sigmoid = 1.0 / (1.0 + jnp.exp(-gate_pre))
    silu = gate_pre * sigmoid
    slope = sigmoid * (1.0 + gate_pre * (1.0 - sigmoid))
    pre_grad[:, :hidden_width] = (hidden_grad * up * slope).astype(BF)
    pre_grad[:, hidden_width:] = (hidden_grad * silu).astype(BF)
    each = jnp.sum(hidden_grad * hidden[...].astype(F32), axis=1, keepdims=True)
    laid = jnp.where(slot_of[...] == iota((rows, LANES), 1), each, 0.0)
    pick = (sender_of[...] == iota((worth.shape[0], rows), 0)).astype(BF)
    terms = three_terms(laid)
    worth[...] = mm(pick, terms[0]) + mm(pick, terms[1]) + mm(pick, terms[2])


def return_rows(group, chunks, slots, lower, order, own, other, message, first_row=0):
    block = group * slots
    half = chunks * slots
    size = group * half
    own_chunks = chunks // 2
    own, other = own.astype(BF), other.astype(BF)
    sides = jnp.where(lower, own, other), jnp.where(lower, other, own)
    pick = (order[...] == iota((size, size), 1)).astype(BF)

    def column(at):
        return jnp.concatenate(
            [
                side[at : at + block, c * LANES : (c + 1) * LANES]
                for side in sides
                for c in range(own_chunks)
            ],
            axis=0,
        )

    for pair in range(own.shape[0] // block // 2):
        lanes = [column((2 * pair + w) * block) for w in range(2)]
        picked = mm(pick, jnp.concatenate(lanes, axis=1)).astype(BF)
        for w in range(2):
            to = slice((2 * pair + w) * group, (2 * pair + w + 1) * group)
            message[to, first_row : first_row + half] = picked[:, w * LANES : (w + 1) * LANES].reshape(
                group, half, LANES
            )


def out_kernel(group, chunks, slots, index, hidden, order, second, early, late, message):
    own = mm(hidden[...], second[...])
    other = mm(hidden[...], jnp.concatenate([early[...], late[...]], axis=0))
    return_rows(group, chunks, slots, index[0] == 0, order, own, other, message)


def back_kernel(group, chunks, slots, index, pre_grad, order, first, rows, outs, *refs):
    message, gain = refs[-2:]
    own = mm(pre_grad[...], first[...], ((1,), (1,)))
    other = mm(pre_grad[...], jnp.concatenate([piece[...] for piece in refs[:-2]], axis=0), ((1,), (1,)))
    half = chunks * slots
    message[:, :half] = outs[...]
    return_rows(group, chunks, slots, index[0] == 0, order, own, other, message, half)

    @pl.when(pl.program_id(0) == 0)
    def _():
        gain[...] = jnp.zeros_like(gain)

    part = own.shape[1]
    gain[:, :part] += jnp.sum(own * rows[:, :part].astype(F32), axis=0, keepdims=True)
    gain[:, part:] += jnp.sum(other * rows[:, part:].astype(F32), axis=0, keepdims=True)


def join(experts, replicas, kind, returned, joined):
    half = returned.shape[1] // 2
    for j in range(replicas):
        block = returned[j * experts : (j + 1) * experts, kind * half : (kind + 1) * half]
        joined[:, j * LANES : (j + 1) * LANES] = block.reshape(experts * half, LANES)
    return joined[...]


def to_tokens(chunks, values, chunk_of):
    return jnp.concatenate(
        [jnp.where(chunk_of == c, values, 0.0).astype(BF) for c in range(chunks)], axis=0
    )


def layer_kernel(experts, replicas, chunks, returned, x, gates, place, owner, chunk_of, slot_of, layer_out, joined):
    tokens, width = x.shape
    hits = slot_hits(place, owner, slot_of)
    source = join(experts, replicas, 0, returned, joined)
    mixed = 0.0
    for term in two_terms(gates[...]):
        weight = jnp.where(hits, spread((term,), owner[...]), 0.0)
        mixed = mixed + mm(to_tokens(chunks, weight, chunk_of[...]), source)
    for c in range(chunks):
        for j in range(replicas):
            at = feature(replicas, width, c, j)
            at = slice(at, at + LANES)
            here = mixed[c * tokens : (c + 1) * tokens, j * LANES : (j + 1) * LANES]
            layer_out[:, at] = (x[:, at].astype(F32) + here).astype(BF)


def in_grad_kernel(experts, replicas, chunks, returned, x, grad, gain, table, place, logit_grad,
                   owner, chunk_of, slot_of, in_grad, joined, normed_grad):
    tokens, width = x.shape
    ones = jnp.where(slot_hits(place, owner, slot_of), 1.0, 0.0)
    back = mm(to_tokens(chunks, ones, chunk_of[...]), join(experts, replicas, 1, returned, joined))
    high, low = two_terms(logit_grad[...])
    by_logits = mm(high, table[...], ((1,), (1,))) + mm(low, table[...], ((1,), (1,)))
    for c in range(chunks):
        for j in range(replicas):
            at = feature(replicas, width, c, j)
            at = slice(at, at + LANES)
            here = back[c * tokens : (c + 1) * tokens, j * LANES : (j + 1) * LANES]
            normed_grad[:, at] = here + by_logits[:, at]
    xw = x[...].astype(F32)
    inv_rms = lax.rsqrt(jnp.mean(xw * xw, axis=1, keepdims=True) + 1e-06)
    weighted = gain[...] * normed_grad[...]
    mean = jnp.mean(xw * weighted, axis=1, keepdims=True)
    in_grad[...] = (
        grad[...].astype(F32) + inv_rms * weighted - xw * (inv_rms * inv_rms * inv_rms * mean)
    ).astype(BF)


def after(value, *earlier):
    return lax.optimization_barrier((value,) + earlier)[0]


def swapped(block, axis):
    return lax.ppermute(block, axis, [(0, 1), (1, 0)])


def shards(section_input, routing, out_grad, norm_gain, router, w_in, w_out):
    experts = lax.axis_size("expert")
    replicas = lax.axis_size("dp")
    x = section_input[0]
    route_ids = routing[0]
    grad_top = out_grad[0]
    gain = norm_gain[0][None, :]
    table = router[0]
    first = w_in[0, 0]
    second = w_out[0, 0]
    tokens, width = x.shape
    part = first.shape[0]
    hidden_width = second.shape[0]
    slots = MOST
    rows = experts * slots
    router_width = table.shape[1]
    chunks = 2 * part // LANES
    half = chunks * slots
    peers = replicas * experts
    group = min(8, experts)
    message_shape = jax.ShapeDtypeStruct((peers, half, LANES), BF)
    side = lax.axis_index("half")
    index = side.astype(jnp.int32)[None]
    cuts = (0, part // 4, 7 * part // 8, part)
    first_other = tuple(swapped(first[a:b], "half") for a, b in zip(cuts, cuts[1:]))
    step_width = hidden_width // HIDDEN_STEPS
    cut = hidden_width - step_width
    second_early = swapped(second[:cut], "half")
    second_other = (second_early, swapped(after(second[cut:], second_early), "half"))

    at = np.arange(experts * half, dtype=np.int32)
    owner, chunk_of, slot_of = (at // half)[None], at % half // slots, (at % slots)[None]
    sizes = (experts, replicas, chunks, slots)
    token_scratch = [pltpu.VMEM((chunks * tokens, replicas * LANES), BF)]
    message, normed, place = kernel_call(
        functools.partial(send_kernel, *sizes),
        (
            message_shape,
            jax.ShapeDtypeStruct((tokens, width), BF),
            jax.ShapeDtypeStruct((tokens, router_width), F32),
        ),
        (x, route_ids, gain, owner, chunk_of[:, None], slot_of),
        token_scratch,
    )
    arrived = exchange(after(message, first_other[0]), SHARE)

    message, gates = kernel_call(
        functools.partial(send_grad_kernel, *sizes),
        (message_shape, jax.ShapeDtypeStruct((tokens, router_width), F32)),
        (normed, route_ids, grad_top, table, place, owner, chunk_of[:, None], slot_of),
        token_scratch,
    )
    message, arrived = lax.optimization_barrier((message, arrived, first_other[1]))[:2]
    arrived_grad = exchange(message, SHARE)

    at = np.arange(group * half, dtype=np.int32)
    into_messages = (at % half // slots * group + at // half) * slots + at % slots
    into_rows = np.zeros_like(at)
    into_rows[into_messages] = at
    all_rows = peers * slots
    whole = lambda shape: pl.BlockSpec(shape, lambda i: (0,) * len(shape))
    scalar = pl.BlockSpec(memory_space=pltpu.SMEM)

    sizes_other = tuple(piece.shape[0] for piece in first_other)

    def products(arrived, weights, side, steps, weight_specs):
        return kernel_call(
            functools.partial(products_kernel, group, chunks, slots, side),
            (
                jax.ShapeDtypeStruct((all_rows, steps * step_width), BF),
                jax.ShapeDtypeStruct((all_rows, 2 * part), BF),
            ),
            (index, arrived, into_rows[:, None]) + weights,
            grid=(steps,),
            in_specs=[scalar, whole(arrived.shape), whole((at.size, 1))] + weight_specs,
            out_specs=[pl.BlockSpec((all_rows, step_width), lambda i: (0, i)), whole((all_rows, 2 * part))],
        )

    partial, expert_rows = products(
        arrived,
        (first,) + first_other,
        0,
        2 * HIDDEN_STEPS,
        [pl.BlockSpec((size, step_width), lambda i: (0, i)) for size in (part,) + sizes_other],
    )
    partial = partial.reshape(replicas, rows, 2 * hidden_width)
    place_in_dp = lax.axis_index("dp")
    terms = [lax.dynamic_index_in_dim(partial, place_in_dp, 0, False)]
    for step in range(1, replicas):
        shift = [(j, (j + step) % replicas) for j in range(replicas)]
        block = lax.dynamic_index_in_dim(partial, (place_in_dp + step) % replicas, 0, False)
        terms.append(lax.ppermute(block, "dp", shift))
    partial, grad_rows = products(
        arrived_grad,
        (second,) + second_other,
        1,
        HIDDEN_STEPS,
        [
            pl.BlockSpec((step_width, part), lambda i: (i, 0)),
            pl.BlockSpec((step_width, part), lambda i: (jnp.minimum(i, HIDDEN_STEPS - 2), 0)),
            whole((step_width, part)),
        ],
    )
    terms = [after(term, partial) for term in terms]
    summands = exchange(partial.reshape(replicas, rows, hidden_width), "dp")
    pre_act = sum(term.astype(F32) for term in terms)
    gate_pre, up = pre_act[:, :hidden_width], pre_act[:, hidden_width:]
    hidden = (gate_pre / (1.0 + jnp.exp(-gate_pre)) * up).astype(BF)
    hidden_blocks = [hidden]
    for step in range(1, replicas):
        shift = [(j, (j + step) % replicas) for j in range(replicas)]
        hidden_blocks.append(lax.ppermute(hidden, "dp", shift))
    at = np.arange(rows, dtype=np.int32)
    pre_grad, worth = kernel_call(
        functools.partial(act_kernel, slots),
        (
            jax.ShapeDtypeStruct((rows, 2 * hidden_width), BF),
            jax.ShapeDtypeStruct((experts, LANES), F32),
        ),
        (summands, pre_act, hidden, at[None] // slots, at[:, None] % slots),
    )
    pre_grad_all = lax.all_gather(pre_grad, "dp", axis=0, tiled=True)
    hidden_blocks = [after(block, worth) for block in hidden_blocks]
    hidden_all = jnp.zeros((all_rows, hidden_width), BF)
    for step, block in enumerate(hidden_blocks):
        at_row = (place_in_dp + replicas - step) % replicas * rows
        hidden_all = lax.dynamic_update_slice(hidden_all, block, (at_row, 0))

    worth = exchange(worth[:, None], "expert")[:, 0, :slots]
    slot_ids = jnp.arange(slots, dtype=F32)
    gate_worth = jnp.sum(
        jnp.where(place[:, :experts, None] == slot_ids, worth[None], 0.0), axis=2
    )
    inner = jnp.sum(gate_worth, axis=1, keepdims=True)
    logit_grad = jnp.pad(gate_worth, ((0, 0), (0, router_width - experts))) - gates * inner
    logit_high, logit_low = two_terms(logit_grad)
    local_router = mm(normed, logit_high, ((0,), (0,))) + mm(normed, logit_low, ((0,), (0,)))
    local_router = local_router.astype(BF).reshape(experts, -1, router_width)
    second_other_grad = mm(hidden_all, grad_rows[:, part:], ((0,), (0,))).astype(BF)
    second_sent = swapped(second_other_grad, "half")
    local_router = after(local_router, second_other_grad)
    steps = 2 if all_rows // 2 % (2 * group * slots) == 0 else 1

    def by_rows(width):
        return pl.BlockSpec((all_rows // steps, width), lambda i: (i, 0))

    messages = pl.BlockSpec((peers // steps, half, LANES), lambda i: (i, 0, 0))
    order = into_messages[:, None]
    out_message = kernel_call(
        functools.partial(out_kernel, group, chunks, slots),
        message_shape,
        (index, hidden_all, order, second) + second_other,
        grid=(steps,),
        in_specs=[scalar, by_rows(hidden_width), whole(order.shape), whole(second.shape)]
        + [whole(piece.shape) for piece in second_other],
        out_specs=messages,
    )
    summed = exchange(local_router, "expert")
    router_part = jnp.sum(after(summed, out_message).astype(F32), axis=0)
    piece = router_part.shape[0] // (2 * replicas)
    router_part = exchange(router_part.reshape(2 * replicas, piece, router_width), ("half", "dp"))

    message, gain_part = kernel_call(
        functools.partial(back_kernel, group, chunks, slots),
        (jax.ShapeDtypeStruct((peers, 2 * half, LANES), BF), jax.ShapeDtypeStruct((1, 2 * part), F32)),
        (index, pre_grad_all, order, first, expert_rows, after(out_message, second_sent)) + first_other,
        grid=(steps,),
        in_specs=[
            scalar,
            by_rows(2 * hidden_width),
            whole(order.shape),
            whole(first.shape),
            by_rows(2 * part),
            messages,
            *(whole(piece.shape) for piece in first_other),
        ],
        out_specs=[
            pl.BlockSpec((peers // steps, 2 * half, LANES), lambda i: (i, 0, 0)),
            whole((1, 2 * part)),
        ],
    )
    router_own = jnp.sum(after(router_part, gain_part), axis=0)
    at = lax.axis_index("expert") * 2 * replicas + side * replicas + place_in_dp
    table_own = lax.dynamic_slice_in_dim(table, at * piece, piece, axis=0).astype(F32)
    gain_own = jnp.sum(router_own * table_own, axis=1)
    gain_part = gain_part.reshape(2, part)
    gain_part = jnp.where(side == 0, gain_part, gain_part[::-1])

    lines = 2 * part // LANES
    terms = three_terms(gain_part.reshape(lines, LANES))
    lone = [jnp.pad(term[None], ((0, 0), (0, LANES - piece))) for term in three_terms(gain_own)]
    block = jnp.concatenate([router_own.astype(BF), *terms, *lone], axis=0)
    block = jnp.pad(block, ((0, -block.shape[0] % 16), (0, 0)))
    owners = 2 * experts
    joined = exchange(jnp.broadcast_to(block[None], (owners,) + block.shape), OWNERS)
    first_other_grad = mm(expert_rows[:, part:], pre_grad_all, ((0,), (0,))).astype(BF)
    first_sent = swapped(first_other_grad, "half")
    message, joined = lax.optimization_barrier((message, joined, first_other_grad))[:2]
    returned = exchange(message, SHARE)
    end = piece + 3 * lines
    gain_rows = jnp.sum(joined[:, piece:end].astype(F32).reshape(owners, 3, lines, LANES), axis=(0, 1))
    lone = jnp.sum(joined[:, end : end + 3, :piece].astype(F32), axis=1).reshape(-1, LANES)
    sums = jnp.concatenate([*three_terms(gain_rows), *three_terms(lone)], axis=0)
    sums = jnp.pad(sums, ((0, -sums.shape[0] % 16), (0, 0)))
    packed = jnp.concatenate([joined[:, :piece].reshape(-1, LANES), sums], axis=0)
    packed = lax.all_gather(packed, "dp", axis=0)

    second_own_grad = mm(hidden_all, grad_rows[:, :part], ((0,), (0,)))
    second_grad = (second_own_grad + second_sent.astype(F32)).astype(BF)
    first_own_grad = lax.optimization_barrier(mm(expert_rows[:, :part], pre_grad_all, ((0,), (0,))))

    token_shape = jax.ShapeDtypeStruct((tokens, width), BF)
    joined_scratch = pltpu.VMEM((experts * half, replicas * LANES), BF)
    layer_out = kernel_call(
        functools.partial(layer_kernel, experts, replicas, chunks),
        token_shape,
        (returned, after(x, second_grad, first_own_grad), gates, place, owner, chunk_of[None], slot_of),
        [joined_scratch],
    )
    in_grad = kernel_call(
        functools.partial(in_grad_kernel, experts, replicas, chunks),
        token_shape,
        (returned, after(x, first_sent), grad_top, gain, table, place, logit_grad, owner, chunk_of[None], slot_of),
        [joined_scratch, pltpu.VMEM((tokens, width), F32)],
    )
    handoff = swapped(layer_out, "section")
    handback = swapped(in_grad, "section")
    packed = after(packed, in_grad)
    router_rows = owners * piece
    router_total = packed[:, :router_rows].reshape(replicas, 2, experts, piece, router_width)
    router_total = router_total.transpose(2, 1, 0, 3, 4).reshape(width, router_width)
    gain_rows = packed[:, router_rows : router_rows + 3 * lines].astype(F32)
    gain_rows = jnp.sum(gain_rows.reshape(replicas, 3, 2, part), axis=1)
    lone = packed[:, router_rows + 3 * lines : router_rows + 6 * lines].astype(F32)
    lone = jnp.sum(lone.reshape(replicas, 3, 2, experts, piece), axis=1)
    gain_total = gain_rows.transpose(1, 0, 2).reshape(width) + lone.transpose(2, 1, 0, 3).reshape(width)
    gain_total = gain_total / gain[0]
    first_grad = (first_own_grad + after(first_sent, in_grad).astype(F32)).astype(BF)
    return (
        handoff[None],
        handback[None],
        first_grad[None, None],
        second_grad[None, None],
        router_total[None],
        gain_total[None],
    )


def solution(mesh):
    sizes = mesh.shape
    halves = (sizes["section"], sizes["expert"], 2, sizes["dp"] // 2)
    split = Mesh(mesh.devices.reshape(halves), ("section", "expert", "half", "dp"))
    blocks = ("half", "dp")
    tokens = ("expert",) + blocks
    return jax.shard_map(
        shards,
        mesh=split,
        in_specs=(
            P("section", tokens, None),
            P("section", tokens, None),
            P("section", tokens, None),
            P("section", None),
            P("section", None, None),
            P("section", "expert", blocks, None),
            P("section", "expert", None, blocks),
        ),
        out_specs=(
            P("section", tokens, None),
            P("section", tokens, None),
            P("section", "expert", blocks, None),
            P("section", "expert", None, blocks),
            P("section", None, None),
            P("section", None),
        ),
        check_vma=False,
    )
```
